128 devices in a mesh: clip: 2 (over y_lo), frame: 16 (over z, y_hi, core), head: 4 (over x).
Axes of the slice: x: 4, y: 4 (y_hi: 2, y_lo: 2; y = y_hi * 2 + y_lo), z: 4, core: 2. Of those that a mesh axis runs over, the one named last changes fastest.
Arguments:
- frames_wide: bfloat16 [2, 16, 256, 1024], P('clip', 'frame'), may hold values from -6 to 6
- frames_small: bfloat16 [8, 16, 64, 1024], P('clip', 'frame'), may hold values from -6 to 6
- actions_wide: int32 [2, 16], P('clip', 'frame'), may hold values from 0 to 7
- actions_small: int32 [8, 16], P('clip', 'frame'), may hold values from 0 to 7
- cotangent_wide: bfloat16 [2, 16, 256, 1024], P('clip', 'frame'), may hold values from -6 to 6
- cotangent_small: bfloat16 [8, 16, 64, 1024], P('clip', 'frame'), may hold values from -6 to 6
- action_table: bfloat16 [8, 1024], P(None, ('clip', 'frame')), may hold values from -3 to 3
- norm_gains: bfloat16 [3, 1024], P(None, ('clip', 'frame')), may hold values from 0.099609375 to 1.8984375
- norm_shifts: bfloat16 [3, 1024], P(None, ('clip', 'frame')), may hold values from -2 to 2
- space_project: bfloat16 [1024, 3, 1024], P(('clip', 'frame'), None, 'head'), may hold values from -0.1875 to 0.1875
- space_output: bfloat16 [1024, 1024], P(('clip', 'frame'), 'head'), may hold values from -0.5 to 0.5
- time_project: bfloat16 [1024, 3, 1024], P(('clip', 'frame'), None, 'head'), may hold values from -0.1875 to 0.1875
- time_output: bfloat16 [1024, 1024], P(('clip', 'frame'), 'head'), may hold values from -0.5 to 0.5
- expand_weight: bfloat16 [1024, 4096], P(('clip', 'frame'), 'head'), may hold values from -0.1875 to 0.1875
- shrink_weight: bfloat16 [1024, 4096], P(('clip', 'frame'), 'head'), may hold values from -0.09375 to 0.09375
Outputs:
- output_wide: bfloat16 [2, 16, 256, 1024], P('clip', 'frame')
- output_small: bfloat16 [8, 16, 64, 1024], P('clip', 'frame')
- gradient_wide: float32 [2, 16, 256, 1024], P('clip', 'frame')
- gradient_small: float32 [8, 16, 64, 1024], P('clip', 'frame')
- table_gradient: float32 [8, 1024], P(None, ('clip', 'frame'))
- gains_gradient: float32 [3, 1024], P(None, ('clip', 'frame'))
- shifts_gradient: float32 [3, 1024], P(None, ('clip', 'frame'))
- space_project_gradient: float32 [1024, 3, 1024], P(('clip', 'frame'), None, 'head')
- space_output_gradient: float32 [1024, 1024], P(('clip', 'frame'), 'head')
- time_project_gradient: float32 [1024, 3, 1024], P(('clip', 'frame'), None, 'head')
- time_output_gradient: float32 [1024, 1024], P(('clip', 'frame'), 'head')
- expand_gradient: float32 [1024, 4096], P(('clip', 'frame'), 'head')
- shrink_gradient: float32 [1024, 4096], P(('clip', 'frame'), 'head')
The draws below stay inside these ranges and needn't reach their ends.
All inputs are finite; a program needn't handle non-finite values.
Results may differ from the reference program's by a relative error of at most 0.03.
Values may be sent and summed in bfloat16 or wider, within the bound.
No kernel may reach another device: no remote copies, remote signals or barrier semaphores. Data moves between devices by JAX's collectives and lax.ppermute only.
A program may use at most 128 MiB of HBM per device.

```python
import jax
import jax.numpy as jnp
from jax import lax

D = 1024
HEADS = 16
HEAD_DIM = 64
FF = 4096
ACTIONS = 8
FRAMES = 16
POS_WIDE = 256
POS_SMALL = 64
CLIPS_WIDE = 2
CLIPS_SMALL = 8


def with_ends(result, own_key, low, high):
    shape = result.shape
    index_at = [jax.random.randint(jax.random.fold_in(own_key, axis), (), 0, shape[axis]) for axis in range(len(shape))]
    result = result.at[tuple(index_at)].set(low)
    longest = shape.index(max(shape))
    index_at[longest] = (index_at[longest] + 1) % shape[longest]
    return result.at[tuple(index_at)].set(high)


def level_of(key, extent, cuts, least, largest):
    def one(position, blocks):
        draws = jax.random.uniform(jax.random.fold_in(jax.random.fold_in(key, 6), position), (blocks,), jnp.float32, least / len(cuts), largest / len(cuts))
        return jnp.repeat(jnp.exp(draws), extent[position] // blocks).reshape((-1,) + (1,) * (len(extent) - position - 1))

    factor_of = one(*cuts[0])
    for cut in cuts[1:]:
        factor_of = factor_of * one(*cut)
    return factor_of


def noise(stream_key, extent, scale, bound, cuts=(), kind=jnp.bfloat16):
    array = jax.random.normal(stream_key, extent, jnp.float32) * scale
    if len(cuts) > 0:
        array = level_of(stream_key, extent, cuts, -0.22, 0.18) * array
    return jnp.clip(array, min=-bound, max=bound).astype(kind)


def setup_inputs(seed: int = 0) -> dict:
    seeds = jax.random.split(jax.random.key(seed), 16)
    frames_wide = noise(seeds[0], (CLIPS_WIDE, FRAMES, POS_WIDE, D), 1.0, 6.0, ((0, 2), (1, 16)))
    frames_small = noise(seeds[1], (CLIPS_SMALL, FRAMES, POS_SMALL, D), 1.0, 6.0, ((0, 2), (1, 16)))
    actions_wide = with_ends(jax.random.randint(seeds[2], (CLIPS_WIDE, FRAMES), 0, ACTIONS), jax.random.fold_in(seeds[2], 1), 0, ACTIONS - 1).astype(jnp.int32)
    actions_small = with_ends(jax.random.randint(seeds[3], (CLIPS_SMALL, FRAMES), 0, ACTIONS), jax.random.fold_in(seeds[3], 1), 0, ACTIONS - 1).astype(jnp.int32)
    cotangent_wide = noise(seeds[4], (CLIPS_WIDE, FRAMES, POS_WIDE, D), 1.0, 6.0, ((0, 2), (1, 16)))
    cotangent_small = noise(seeds[5], (CLIPS_SMALL, FRAMES, POS_SMALL, D), 1.0, 6.0, ((0, 2), (1, 16)))
    action_table = noise(seeds[6], (ACTIONS, D), 0.5, 3.0, ((1, 32),))
    norm_gains = jnp.clip(1.0 + 0.18 * jax.random.normal(seeds[7], (3, D), jnp.float32), 0.099609375, 1.8984375).astype(jnp.bfloat16)
    norm_shifts = noise(seeds[8], (3, D), 0.3, 2.0, ((1, 32),))
    space_project = noise(seeds[9], (D, 3, D), D ** -0.5, 0.1875, ((0, 32), (2, 4)))
    space_output = noise(seeds[10], (D, D), (D // 8) ** -0.5, 0.5, ((0, 32), (1, 4)))
    time_project = noise(seeds[11], (D, 3, D), D ** -0.5, 0.1875, ((0, 32), (2, 4)))
    time_output = noise(seeds[12], (D, D), (D // 8) ** -0.5, 0.5, ((0, 32), (1, 4)))
    expand_weight = noise(seeds[13], (D, FF), D ** -0.5, 0.1875, ((0, 32), (1, 4)))
    shrink_weight = noise(seeds[14], (D, FF), FF ** -0.5, 0.09375, ((0, 32), (1, 4)))
    return {"frames_wide": frames_wide, "frames_small": frames_small, "actions_wide": actions_wide, "actions_small": actions_small, "cotangent_wide": cotangent_wide, "cotangent_small": cotangent_small, "action_table": action_table, "norm_gains": norm_gains, "norm_shifts": norm_shifts, "space_project": space_project, "space_output": space_output, "time_project": time_project, "time_output": time_output, "expand_weight": expand_weight, "shrink_weight": shrink_weight}


@jax.custom_vjp
def low(v):
    return lax.optimization_barrier(v.astype(jnp.bfloat16)).astype(jnp.float32)

@jax.custom_vjp
def low_back(v):
    return v

def low_keep(v):
    return (low(v), None)

def low_pass(kept, grad):
    return (grad,)

def back_keep(v):
    return (v, None)

def back_low(kept, grad):
    return (low(grad),)
low.defvjp(low_keep, low_pass)
low_back.defvjp(back_keep, back_low)
epsilon = 1e-05
HIGHEST = lax.Precision.HIGHEST

def causal_mask(length):
    row_index = lax.broadcasted_iota(jnp.int32, (length, length), 0)
    col_index = lax.broadcasted_iota(jnp.int32, (length, length), 1)
    return col_index <= row_index

def layer_norm(stream, gain, shift):
    average = lax.optimization_barrier(jnp.mean(stream, axis=-1, keepdims=True))
    centered = stream - average
    inverse = lax.rsqrt(lax.optimization_barrier(jnp.mean(centered * centered, axis=-1, keepdims=True)) + epsilon)
    return centered * inverse * gain + shift

def attend(normed, project, output, causal):
    leading = normed.shape[:-1]
    packed = low(low_back(jnp.einsum('...d,dje->...je', low(normed), project, precision=HIGHEST)))
    pieces = packed.reshape(leading + (3, HEADS, HEAD_DIM))
    queries = pieces[..., 0, :, :]
    key_rows = pieces[..., 1, :, :]
    values = pieces[..., 2, :, :]
    scores = low_back(jnp.einsum('...qhe,...khe->...hqk', queries, key_rows, precision=HIGHEST) * HEAD_DIM ** (-0.5))
    if causal:
        scores = jnp.where(causal_mask(scores.shape[-1]), scores, -1e+30)
    chances = low(jax.nn.softmax(scores, axis=-1))
    mixture = low(low_back(jnp.einsum('...hqk,...khe->...qhe', chances, values, precision=HIGHEST)))
    mixture = mixture.reshape(leading + (D,))
    return low_back(jnp.einsum('...e,de->...d', mixture, output, precision=HIGHEST))

def block(stream, chosen, action_table, norm_gains, norm_shifts, weights):
    space_project, space_output, time_project, time_output, expand_weight, shrink_weight = weights
    entered = stream + action_table[chosen][:, :, None, :]
    after_space = entered + attend(layer_norm(entered, norm_gains[0], norm_shifts[0]), space_project, space_output, False)
    turned = jnp.swapaxes(layer_norm(after_space, norm_gains[1], norm_shifts[1]), 1, 2)
    after_time = after_space + jnp.swapaxes(attend(turned, time_project, time_output, True), 1, 2)
    normed = low(layer_norm(after_time, norm_gains[2], norm_shifts[2]))
    raised = low_back(jnp.einsum('...d,dg->...g', normed, expand_weight, precision=HIGHEST))
    hidden = low(jax.nn.gelu(raised, approximate=False))
    return after_time + low_back(jnp.einsum('...g,dg->...d', hidden, shrink_weight, precision=HIGHEST))

def reference(frames_wide, frames_small, actions_wide, actions_small, cotangent_wide, cotangent_small, action_table, norm_gains, norm_shifts, space_project, space_output, time_project, time_output, expand_weight, shrink_weight):
    params = tuple((argument.astype(jnp.float32) for argument in (action_table, norm_gains, norm_shifts, space_project, space_output, time_project, time_output, expand_weight, shrink_weight)))
    streams = (frames_wide.astype(jnp.float32), frames_small.astype(jnp.float32))

    def forward(stream_pair, param_list):
        return tuple((block(stream, chosen, param_list[0], param_list[1], param_list[2], param_list[3:]) for stream, chosen in zip(stream_pair, (actions_wide, actions_small))))
    outputs, pullback = jax.vjp(forward, streams, params)
    grad_streams, grad_params = pullback((cotangent_wide.astype(jnp.float32), cotangent_small.astype(jnp.float32)))
    return (outputs[0].astype(jnp.bfloat16), outputs[1].astype(jnp.bfloat16), grad_streams[0], grad_streams[1], grad_params[0], grad_params[1], grad_params[2], grad_params[3], grad_params[4], grad_params[5], grad_params[6], grad_params[7], grad_params[8])
```

```python
import functools
import math

import jax
import jax.numpy as jnp
from jax import lax
from jax.experimental import pallas as pl
from jax.experimental.pallas import tpu as pltpu
from jax.sharding import Mesh
from jax.sharding import PartitionSpec as P

BF = jnp.bfloat16
F32 = jnp.float32
EPS = 1e-05
CF = ("clip", "z", "yh", "core")
FRAME = ("z", "yh", "core")
CHIPS = ("clip", "z", "yh")
HF = ("head", "z", "yh", "core")
ALL = ("clip", "z", "yh", "core", "head")
D = 1024
VM = pl.BlockSpec(memory_space=pltpu.VMEM)
SM = pl.BlockSpec(memory_space=pltpu.SMEM)
HB = pl.BlockSpec(memory_space=pl.ANY)
SCALE = 0.125


def mm(a, b):
    return lax.dot_general(a, b, (((1,), (0,)), ((), ())), preferred_element_type=F32)


def mt(a, b):
    return lax.dot_general(a, b, (((1,), (1,)), ((), ())), preferred_element_type=F32)


def tm(a, b):
    return lax.dot_general(a, b, (((0,), (0,)), ((), ())), preferred_element_type=F32)


def call(body, outs, specs, args, scratch=(), flops=0, size=0):
    return pl.pallas_call(
        body,
        out_shape=[jax.ShapeDtypeStruct(s, t) for s, t in outs],
        in_specs=specs,
        out_specs=[VM] * len(outs),
        scratch_shapes=list(scratch),
        compiler_params=pltpu.CompilerParams(vmem_limit_bytes=56 * 2**20),
        cost_estimate=pl.CostEstimate(flops=flops, bytes_accessed=size, transcendentals=0),
    )(*args)


def scaled_of(stream):
    average = jnp.mean(stream, axis=-1, keepdims=True)
    centered = stream - average
    inverse = lax.rsqrt(jnp.mean(centered * centered, axis=-1, keepdims=True) + EPS)
    return centered * inverse, inverse


def norm_back(grad, scaled, inverse, gain):
    grad_scaled = grad * gain
    inner = jnp.mean(grad_scaled, axis=-1, keepdims=True)
    along = jnp.mean(grad_scaled * scaled, axis=-1, keepdims=True)
    return inverse * (grad_scaled - inner - scaled * along)


def lane_half(side):
    lane = lax.broadcasted_iota(jnp.int32, (1, 128), 1)
    return (lane < 64) if side == 0 else (lane >= 64)


def pick(side, block):
    return jnp.where(lane_half(side), block, jnp.zeros_like(block))


def chances_of(queries, keys, mask):
    scores = mt(queries, keys) * SCALE
    if mask is not None:
        scores = jnp.where(mask, scores, -1e30)
    raised = jnp.exp(scores - jnp.max(scores, axis=-1, keepdims=True))
    return raised * (1.0 / jnp.sum(raised, axis=-1, keepdims=True))


def attend(q2, k2, v2, mask):
    total = 0.0
    for side in range(2):
        chances = chances_of(pick(side, q2), k2, mask).astype(BF)
        total = total + mm(chances, pick(side, v2))
    return total.astype(BF)


def attend_back(q2, k2, v2, g2, mask):
    grad_q, grad_k, grad_v = 0.0, 0.0, 0.0
    for side in range(2):
        qs = pick(side, q2)
        gs = pick(side, g2)
        chances = chances_of(qs, k2, mask)
        grad_v = grad_v + tm(chances.astype(BF), gs)
        grad_chances = mt(gs, v2)
        weighted = jnp.sum(grad_chances * chances, axis=-1, keepdims=True)
        grad_scores = (chances * (grad_chances - weighted)).astype(BF)
        grad_q = grad_q + mm(grad_scores, pick(side, k2))
        grad_k = grad_k + tm(grad_scores, qs)
    return (grad_q * SCALE).astype(BF), (grad_k * SCALE).astype(BF), grad_v.astype(BF)


def small_mask():
    row = lax.broadcasted_iota(jnp.int32, (256, 256), 0)
    col = lax.broadcasted_iota(jnp.int32, (256, 256), 1)
    return (row // 64) == (col // 64)


def time_mask():
    row = lax.broadcasted_iota(jnp.int32, (128, 128), 0)
    col = lax.broadcasted_iota(jnp.int32, (128, 128), 1)
    return (col <= row) & ((row % 8) == (col % 8))


def space_norm(acts, wide, small, par, normed):
    for sub, ref in enumerate((wide, small)):
        for b in range(4):
            action = acts[0] if sub == 0 else acts[1 + b]
            entered = ref[64 * b : 64 * b + 64, :].astype(F32) + par[pl.ds(action, 1), :]
            scaled, _ = scaled_of(entered)
            start = sub * 256 + b * 64
            normed[start : start + 64, :] = (scaled * par[8:9, :] + par[11:12, :]).astype(BF)


def space_kernel(acts, wide, small, par, weight, mix, packed, normed):
    space_norm(acts, wide, small, par, normed)
    for sub in range(2):
        rows = normed[sub * 256 : sub * 256 + 256, :]
        for j in range(3):
            packed[sub, :, j * 256 : j * 256 + 256] = mm(rows, weight[:, j * 256 : j * 256 + 256]).astype(BF)
        mask = None if sub == 0 else small_mask()
        for p in range(2):
            q2, k2, v2 = (packed[sub, :, j * 256 + p * 128 : j * 256 + p * 128 + 128] for j in range(3))
            out = attend(q2, k2, v2, mask)
            for b in range(4):
                mix[b, sub, :, p * 128 : p * 128 + 128] = out[64 * b : 64 * b + 64, :]


def time_kernel(stream, mix, par, big, after_space, after_time, packed, mixture, normed_ffn, wso, wtp, wto, sems):
    copies = [
        pltpu.make_async_copy(big.at[:, 0:1024], wso, sems.at[0]),
        pltpu.make_async_copy(big.at[:, 1024:4096], wtp, sems.at[1]),
        pltpu.make_async_copy(big.at[:, 4096:5120], wto, sems.at[2]),
    ]
    for copy in copies:
        copy.start()
    action = stream[:, 2048:2049].astype(F32)
    entered = stream[:, 0:1024].astype(F32)
    for a in range(8):
        entered = entered + jnp.where(action == float(a), par[a : a + 1, :], 0.0)
    mixed = jnp.concatenate([mix[h] for h in range(4)], axis=1)
    copies[0].wait()
    stepped = entered + mt(mixed, wso[...])
    after_space[...] = stepped
    scaled, _ = scaled_of(stepped)
    normed = (scaled * par[9:10, :] + par[12:13, :]).astype(BF)
    copies[1].wait()
    for j in range(3):
        packed[:, j * D : j * D + D] = mm(normed, wtp[:, j * D : j * D + D]).astype(BF)
    mask = time_mask()
    for p in range(8):
        q2, k2, v2 = (packed[:, j * D + p * 128 : j * D + p * 128 + 128] for j in range(3))
        mixture[:, p * 128 : p * 128 + 128] = attend(q2, k2, v2, mask)
    copies[2].wait()
    done = stepped + mt(mixture[...], wto[...])
    after_time[...] = done
    scaled, _ = scaled_of(done)
    normed_ffn[...] = (scaled * par[10:11, :] + par[13:14, :]).astype(BF)


def ffn_kernel(normed, cot, big, hidden, grad_raised, grad_normed, we, ws, sems):
    n = normed.shape[0]
    copies = [
        pltpu.make_async_copy(big.at[:, 5120:6144], we, sems.at[0]),
        pltpu.make_async_copy(big.at[:, 6144:7168], ws, sems.at[1]),
    ]
    for copy in copies:
        copy.start()
    for copy in copies:
        copy.wait()
    for c in range(4):
        cols = slice(c * 256, c * 256 + 256)
        raised = mm(normed[...], we[:, cols])
        grad_hidden = mm(cot[...], ws[:, cols])
        spread = 0.5 * (1.0 + lax.erf(raised * math.sqrt(0.5)))
        bell = jnp.exp(-0.5 * raised * raised) * (1.0 / math.sqrt(2.0 * math.pi))
        hidden[:, cols] = (raised * spread).astype(BF)
        grad_raised[:, cols] = (grad_hidden * (spread + raised * bell)).astype(BF)
    grad_normed[...] = mt(grad_raised[...], we[...]).astype(BF)


def ffn_out_kernel(hidden, big, out, ws, sems):
    copy = pltpu.make_async_copy(big.at[:, 6144:7168], ws, sems.at[0])
    copy.start()
    copy.wait()
    out[...] = mt(hidden[...], ws[...]).astype(BF)


def ffn_grad_kernel(normed, cot, hidden, grad_raised, out):
    for c in range(4):
        cols = slice(c * 256, c * 256 + 256)
        first = tm(normed[...], grad_raised[:, cols]).astype(BF).reshape(16, 2, 32, 256)
        second = tm(cot[...], hidden[:, cols]).astype(BF).reshape(16, 2, 32, 256)
        for s in range(2):
            out[s, :, :, c * 256 : c * 256 + 256] = first[:, s]
            out[s, :, :, D + c * 256 : D + c * 256 + 256] = second[:, s]


def time_back_kernel(
    stream, parts, after_space, after_time, packed, mixture, par, big,
    grad_mix, grad_after_space, branches, grad_packed, sums, wso, wtp, wto, sems,
):
    copies = [
        pltpu.make_async_copy(big.at[:, 4096:5120], wto, sems.at[0]),
        pltpu.make_async_copy(big.at[:, 1024:4096], wtp, sems.at[1]),
        pltpu.make_async_copy(big.at[:, 0:1024], wso, sems.at[2]),
    ]
    for copy in copies:
        copy.start()
    grad = parts[0].astype(F32)
    for d in range(1, 4):
        grad = grad + parts[d].astype(F32)
    scaled, inverse = scaled_of(after_time[...])
    sums[...] = jnp.zeros_like(sums)
    sums[10:11, :] = jnp.sum(grad * scaled, axis=0, keepdims=True)
    sums[13:14, :] = jnp.sum(grad, axis=0, keepdims=True)
    grad_after_time = stream[:, 1024:2048].astype(F32) + norm_back(grad, scaled, inverse, par[10:11, :])
    branch = grad_after_time.astype(BF)
    branches[0] = branch
    copies[0].wait()
    grad_mixture = mm(branch, wto[...]).astype(BF)
    mask = time_mask()
    for p in range(8):
        q2, k2, v2 = (packed[:, j * D + p * 128 : j * D + p * 128 + 128] for j in range(3))
        back = attend_back(q2, k2, v2, grad_mixture[:, p * 128 : p * 128 + 128], mask)
        for j in range(3):
            grad_packed[:, j * D + p * 128 : j * D + p * 128 + 128] = back[j]
    copies[1].wait()
    grad = mt(grad_packed[...], wtp[...])
    scaled, inverse = scaled_of(after_space[...])
    branches[1] = (scaled * par[9:10, :] + par[12:13, :]).astype(BF)
    sums[9:10, :] = jnp.sum(grad * scaled, axis=0, keepdims=True)
    sums[12:13, :] = jnp.sum(grad, axis=0, keepdims=True)
    grad_after = grad_after_time + norm_back(grad, scaled, inverse, par[9:10, :])
    branch = grad_after.astype(BF)
    grad_after_space[...] = branch
    copies[2].wait()
    back = mm(branch, wso[...]).astype(BF)
    for h in range(4):
        grad_mix[h] = back[:, h * 256 : h * 256 + 256]


def time_grad_kernel(branches, grad_branch_space, mix, mixture, grad_packed, out):
    for h in range(4):
        pieces = (
            tm(grad_branch_space[...], mix[h]),
            tm(branches[1], grad_packed[:, h * 256 : h * 256 + 256]),
            tm(branches[1], grad_packed[:, D + h * 256 : D + h * 256 + 256]),
            tm(branches[1], grad_packed[:, 2 * D + h * 256 : 2 * D + h * 256 + 256]),
            tm(branches[0], mixture[:, h * 256 : h * 256 + 256]),
        )
        for i, piece in enumerate(pieces):
            block = piece.astype(BF).reshape(16, 2, 32, 256)
            for s in range(2):
                out[s, h, :, :, i * 256 : i * 256 + 256] = block[:, s]


def space_back_kernel(grad_mix, packed, weight, grad_packed, grad_normed):
    for sub in range(2):
        mask = None if sub == 0 else small_mask()
        for p in range(2):
            q2, k2, v2 = (packed[sub, :, j * 256 + p * 128 : j * 256 + p * 128 + 128] for j in range(3))
            g2 = jnp.concatenate([grad_mix[b, sub, :, p * 128 : p * 128 + 128] for b in range(4)], axis=0)
            back = attend_back(q2, k2, v2, g2, mask)
            for j in range(3):
                grad_packed[sub, :, j * 256 + p * 128 : j * 256 + p * 128 + 128] = back[j]
        grad = mt(grad_packed[sub], weight[:, 0:768]).astype(BF)
        for b in range(4):
            grad_normed[b, sub] = grad[64 * b : 64 * b + 64, :]


def space_grad_kernel(acts, wide, small, par, grad_packed, out, normed):
    space_norm(acts, wide, small, par, normed)
    for j in range(3):
        total = tm(normed[0:256, :], grad_packed[0, :, j * 256 : j * 256 + 256])
        total = total + tm(normed[256:512, :], grad_packed[1, :, j * 256 : j * 256 + 256])
        out[:, j * 256 : j * 256 + 256] = total.astype(BF)


def final_kernel(acts, own, parts, grad_after, par, sums_in, grad_out, sums):
    sums[...] = sums_in[...]
    for sub in range(2):
        entered = own[sub].astype(F32) + par[pl.ds(acts[sub], 1), :]
        scaled, inverse = scaled_of(entered)
        grad = parts[0, sub].astype(F32)
        for d in range(1, 4):
            grad = grad + parts[d, sub].astype(F32)
        sums[8:9, :] += jnp.sum(grad * scaled, axis=0, keepdims=True)
        sums[11:12, :] += jnp.sum(grad, axis=0, keepdims=True)
        total = grad_after[sub].astype(F32) + norm_back(grad, scaled, inverse, par[8:9, :])
        grad_out[sub] = total.astype(BF)
        sums[pl.ds(acts[sub], 1), :] += jnp.sum(total, axis=0, keepdims=True)


def swap(x, axes):
    return lax.all_to_all(x, axes, split_axis=0, concat_axis=0, tiled=True)


def spread(x, axes, n):
    return swap(jnp.broadcast_to(x[None], (n,) + x.shape), axes)


def shift(x, d):
    return lax.ppermute(x, "head", [(i, (i + d) % 4) for i in range(4)])


def core_swap(x):
    return lax.ppermute(x, "core", [(0, 1), (1, 0)])


def body(
    frames_wide, frames_small, actions_wide, actions_small, cotangent_wide, cotangent_small,
    action_table, norm_gains, norm_shifts, space_project, space_output, time_project, time_output,
    expand_weight, shrink_weight,
):
    me = lax.axis_index("head")
    core = lax.axis_index("core")
    wide, small = frames_wide.reshape(256, D), frames_small.reshape(256, D)
    acts = jnp.concatenate([actions_wide.reshape(1), actions_small.reshape(4), jnp.zeros((3,), jnp.int32)])
    own_acts = jnp.stack([acts[0], lax.dynamic_index_in_dim(acts, me + 1, 0, keepdims=False)])

    def own_rows(a, b):
        return jnp.stack([lax.dynamic_slice(v.reshape(256, D), (64 * me, 0), (64, D)) for v in (a, b)])

    own = own_rows(wide, small)
    own_cot = own_rows(cotangent_wide, cotangent_small)

    small_par = jnp.concatenate([action_table, norm_gains, norm_shifts, jnp.zeros((2, 32), BF)], axis=0).T
    first = jnp.concatenate([space_project.reshape(32, 768), jnp.pad(small_par, ((0, 0), (0, 112)))], axis=1)
    first = spread(first, CF, 32).reshape(D, 896)
    par = first[:, 768:784].T.astype(F32)

    mine = jnp.concatenate([space_output, time_project.reshape(32, 768), time_output], axis=1)
    heads = spread(mine, "head", 4)
    big = jnp.concatenate(
        [
            heads[:, :, 0:256].transpose(1, 0, 2).reshape(32, D),
            heads[:, :, 256:1024].reshape(4, 32, 3, 256).transpose(1, 2, 0, 3).reshape(32, 3 * D),
            heads[:, :, 1024:1280].transpose(1, 0, 2).reshape(32, D),
            expand_weight,
            shrink_weight,
        ],
        axis=1,
    )
    big = lax.all_gather(big, CF, axis=0, tiled=True)

    marks = jnp.broadcast_to(own_acts[:, None, None].astype(BF), (2, 64, 128))
    stream = jnp.concatenate([own, own_cot, marks], axis=2).reshape(16, 8, 2176)
    stream = swap(stream, FRAME).reshape(128, 2176)
    cots = [stream[:, D : 2 * D]]
    cots += [shift(cots[0], d) for d in (1, 3, 2)]

    mix_f, packed_f = call(
        space_kernel, [((4, 2, 64, 256), BF), ((2, 256, 768), BF)], [SM, VM, VM, VM, VM],
        (acts, wide, small, par, first), [pltpu.VMEM((512, D), BF)], flops=2 * 10**9, size=5 * 10**6,
    )
    mix = swap(mix_f.reshape(64, 8, 256), HF).reshape(4, 128, 256)

    weights = [pltpu.VMEM((D, D), BF), pltpu.VMEM((D, 3 * D), BF), pltpu.VMEM((D, D), BF), pltpu.SemaphoreType.DMA((3,))]
    after_space, after_time, packed_t, mixture_t, normed_ffn = call(
        time_kernel,
        [((128, D), F32), ((128, D), F32), ((128, 3 * D), BF), ((128, D), BF), ((128, D), BF)],
        [VM, VM, VM, HB], (stream, mix, par, big), weights, flops=2 * 10**9, size=14 * 10**6,
    )

    normeds = [normed_ffn] + [shift(normed_ffn, d) for d in (1, 3, 2)]
    normed_all, cot_all = jnp.concatenate(normeds), jnp.concatenate(cots)
    ffn_w = [pltpu.VMEM((D, D), BF), pltpu.VMEM((D, D), BF), pltpu.SemaphoreType.DMA((2,))]
    hidden, grad_raised, grad_normed = call(
        ffn_kernel, [((512, D), BF)] * 3, [VM, VM, HB], (normed_all, cot_all, big), ffn_w,
        flops=4 * 10**9, size=9 * 10**6,
    )
    rows = lambda x, i: x[128 * i : 128 * i + 128]
    parts = [rows(grad_normed, 0)] + [shift(rows(grad_normed, i), d) for i, d in ((1, 3), (2, 1), (3, 2))]

    grad_mix_p, grad_after, branches, grad_packed_t, sums = call(
        time_back_kernel,
        [((4, 128, 256), BF), ((128, D), BF), ((2, 128, D), BF), ((128, 3 * D), BF), ((16, D), F32)],
        [VM] * 7 + [HB],
        (stream, jnp.stack(parts), after_space, after_time, packed_t, mixture_t, par, big), weights,
        flops=3 * 10**9, size=14 * 10**6,
    )
    grad_mix = swap(grad_mix_p.reshape(64, 8, 256), HF).reshape(4, 2, 64, 256)
    grad_after_f = swap(grad_after.reshape(16, 8, D), FRAME).reshape(2, 64, D)

    grad_packed_f, grad_normed_f = call(
        space_back_kernel, [((2, 256, 768), BF), ((4, 2, 64, D), BF)], [VM] * 3,
        (grad_mix, packed_f, first), flops=2 * 10**9, size=4 * 10**6,
    )
    parts = [lax.dynamic_index_in_dim(grad_normed_f, me, 0, keepdims=False)]
    parts += [shift(lax.dynamic_index_in_dim(grad_normed_f, (me + d) % 4, 0, keepdims=False), d) for d in (1, 3, 2)]
    grad_own, sums = call(
        final_kernel, [((2, 64, D), BF), ((16, D), F32)], [SM] + [VM] * 5,
        (own_acts, own, jnp.stack(parts), grad_after_f, par, sums), flops=10**8, size=2 * 10**6,
    )
    grad_in = spread(grad_own, "head", 4).astype(F32)

    (ffn_grad,) = call(
        ffn_grad_kernel, [((2, 16, 32, 2 * D), BF)], [VM] * 4, (normed_all, cot_all, hidden, grad_raised),
        flops=2 * 10**9, size=8 * 10**6,
    )
    (time_grad,) = call(
        time_grad_kernel, [((2, 4, 16, 32, 1280), BF)], [VM] * 5,
        (branches, grad_after, mix, mixture_t, grad_packed_t), flops=2 * 10**9, size=12 * 10**6,
    )
    (space_grad,) = call(
        space_grad_kernel, [((D, 768), BF)], [SM] + [VM] * 4, (acts, wide, small, par, grad_packed_f),
        [pltpu.VMEM((512, D), BF)], flops=10**9, size=4 * 10**6,
    )

    def pair_sum(x):
        kept = lax.dynamic_index_in_dim(x, core, 0, keepdims=False)
        sent = lax.dynamic_index_in_dim(x, 1 - core, 0, keepdims=False)
        return (kept.astype(F32) + core_swap(sent).astype(F32)).astype(BF)

    def total(x):
        return jnp.sum(x.astype(F32), axis=0)

    ffn_total = total(swap(pair_sum(ffn_grad), CHIPS))
    time_total = total(swap(pair_sum(time_grad).reshape(64, 32, 1280), ("head",) + CHIPS))
    space_total = total(swap(space_grad.reshape(32, 32, 768), CF))
    shares = sums.astype(BF).reshape(16, 32, 32).transpose(1, 0, 2)
    shares = jnp.broadcast_to(shares[:, None], (32, 4, 16, 32)).reshape(128, 16, 32)
    par_total = total(swap(shares, ALL))

    (out_all,) = call(
        ffn_out_kernel, [((512, D), BF)], [VM, HB], (hidden, big),
        [pltpu.VMEM((D, D), BF), pltpu.SemaphoreType.DMA((1,))], flops=10**9, size=4 * 10**6,
    )
    result = after_time + rows(out_all, 0).astype(F32)
    for i, d in ((1, 3), (2, 1), (3, 2)):
        result = result + shift(rows(out_all, i), d).astype(F32)
    result = swap(result.astype(BF).reshape(16, 8, D), FRAME).reshape(2, 64, D)
    result = spread(result, "head", 4)
    return (
        result[:, 0].reshape(1, 1, 256, D),
        result[:, 1].reshape(4, 1, 64, D),
        grad_in[:, 0].reshape(1, 1, 256, D),
        grad_in[:, 1].reshape(4, 1, 64, D),
        par_total[0:8],
        par_total[8:11],
        par_total[11:14],
        space_total.reshape(32, 3, 256),
        time_total[:, 0:256],
        time_total[:, 256:1024].reshape(32, 3, 256),
        time_total[:, 1024:1280],
        ffn_total[:, 0:D],
        ffn_total[:, D : 2 * D],
    )


def solution(mesh):
    fine = Mesh(mesh.devices.reshape(2, 4, 2, 2, 4), ALL)
    tokens = P("clip", FRAME, None, None)
    columns = P(None, CF)
    square, cube = P(CF, "head"), P(CF, None, "head")
    frames = P("clip", FRAME)
    weights = (cube, square, cube, square, square, square)
    in_specs = (tokens, tokens, frames, frames, tokens, tokens) + (columns,) * 3 + weights
    out_specs = (tokens,) * 4 + (columns,) * 3 + weights
    return jax.shard_map(body, mesh=fine, in_specs=in_specs, out_specs=out_specs, check_vma=False)
```

```python
import functools
import math

import jax
import jax.numpy as jnp
from jax import lax
from jax.experimental import pallas as pl
from jax.experimental.pallas import tpu as pltpu
from jax.sharding import Mesh
from jax.sharding import PartitionSpec as P

BF = jnp.bfloat16
F32 = jnp.float32
EPS = 1e-05
CF = ("clip", "z", "yh", "core")
FRAME = ("z", "yh", "core")
CHIPS = ("clip", "z", "yh")
HF = ("head", "z", "yh", "core")
ALL = ("clip", "z", "yh", "core", "head")
D = 1024
VM = pl.BlockSpec(memory_space=pltpu.VMEM)
SM = pl.BlockSpec(memory_space=pltpu.SMEM)
HB = pl.BlockSpec(memory_space=pl.ANY)
SCALE = 0.125


def mm(a, b):
    return lax.dot_general(a, b, (((1,), (0,)), ((), ())), preferred_element_type=F32)


def mt(a, b):
    return lax.dot_general(a, b, (((1,), (1,)), ((), ())), preferred_element_type=F32)


def tm(a, b):
    return lax.dot_general(a, b, (((0,), (0,)), ((), ())), preferred_element_type=F32)


def call(body, outs, specs, args, scratch=(), flops=0, size=0):
    return pl.pallas_call(
        body,
        out_shape=[jax.ShapeDtypeStruct(s, t) for s, t in outs],
        in_specs=specs,
        out_specs=[VM] * len(outs),
        scratch_shapes=list(scratch),
        compiler_params=pltpu.CompilerParams(vmem_limit_bytes=56 * 2**20),
        cost_estimate=pl.CostEstimate(flops=flops, bytes_accessed=size, transcendentals=0),
    )(*args)


def scaled_of(stream):
    average = jnp.mean(stream, axis=-1, keepdims=True)
    centered = stream - average
    inverse = lax.rsqrt(jnp.mean(centered * centered, axis=-1, keepdims=True) + EPS)
    return centered * inverse, inverse


def norm_back(grad, scaled, inverse, gain):
    grad_scaled = grad * gain
    inner = jnp.mean(grad_scaled, axis=-1, keepdims=True)
    along = jnp.mean(grad_scaled * scaled, axis=-1, keepdims=True)
    return inverse * (grad_scaled - inner - scaled * along)


def lane_half(side):
    lane = lax.broadcasted_iota(jnp.int32, (1, 128), 1)
    return (lane < 64) if side == 0 else (lane >= 64)


def pick(side, block):
    return jnp.where(lane_half(side), block, jnp.zeros_like(block))


def chances_of(queries, keys, mask):
    scores = mt(queries, keys) * SCALE
    if mask is not None:
        scores = jnp.where(mask, scores, -1e30)
    raised = jnp.exp(scores - jnp.max(scores, axis=-1, keepdims=True))
    return raised * (1.0 / jnp.sum(raised, axis=-1, keepdims=True))


def attend(q2, k2, v2, mask):
    total = 0.0
    for side in range(2):
        chances = chances_of(pick(side, q2), k2, mask).astype(BF)
        total = total + mm(chances, pick(side, v2))
    return total.astype(BF)


def attend_back(q2, k2, v2, g2, mask):
    grad_q, grad_k, grad_v = 0.0, 0.0, 0.0
    for side in range(2):
        qs = pick(side, q2)
        gs = pick(side, g2)
        chances = chances_of(qs, k2, mask)
        grad_v = grad_v + tm(chances.astype(BF), gs)
        grad_chances = mt(gs, v2)
        weighted = jnp.sum(grad_chances * chances, axis=-1, keepdims=True)
        grad_scores = (chances * (grad_chances - weighted)).astype(BF)
        grad_q = grad_q + mm(grad_scores, pick(side, k2))
        grad_k = grad_k + tm(grad_scores, qs)
    return (grad_q * SCALE).astype(BF), (grad_k * SCALE).astype(BF), grad_v.astype(BF)


def small_mask():
    row = lax.broadcasted_iota(jnp.int32, (256, 256), 0)
    col = lax.broadcasted_iota(jnp.int32, (256, 256), 1)
    return (row // 64) == (col // 64)


def time_mask():
    row = lax.broadcasted_iota(jnp.int32, (128, 128), 0)
    col = lax.broadcasted_iota(jnp.int32, (128, 128), 1)
    return (col <= row) & ((row % 8) == (col % 8))


TURNS = (0, 1, 3, 2)


def load_chips(side, mine, other, dest, sems):
    core = side[0]
    copies = [
        pltpu.make_async_copy(mine, dest.at[:, core], sems.at[0]),
        pltpu.make_async_copy(other, dest.at[:, 1 - core], sems.at[1]),
    ]
    for copy in copies:
        copy.start()
    return copies


def load_turns(big, offset, dest, sems):
    copies = []
    for d in range(4):
        start = 2816 + 512 * d + offset
        copies.append(pltpu.make_async_copy(big.at[:, start : start + 256], dest.at[d], sems.at[d]))
        copies[d].start()
    return copies


def finish(copies):
    for copy in copies:
        copy.wait()


def turned(side, d, sign):
    return lax.rem(side[1] + 4 + sign * d, 4)


def regroup(block):
    width = block.shape[1]
    parts = block.reshape(16, 4, 8, width)
    return [parts[:, g].reshape(128, width) for g in range(4)]


def ungroup(blocks):
    width = blocks[0].shape[1]
    return jnp.stack([block.reshape(16, 8, width) for block in blocks], axis=1).reshape(512, width)


def space_norm(acts, wide, small, par, normed):
    for sub, ref in enumerate((wide, small)):
        for b in range(4):
            action = acts[0] if sub == 0 else acts[1 + b]
            entered = ref[64 * b : 64 * b + 64, :].astype(F32) + par[pl.ds(action, 1), :]
            scaled, _ = scaled_of(entered)
            start = sub * 256 + b * 64
            normed[start : start + 64, :] = (scaled * par[8:9, :] + par[11:12, :]).astype(BF)


def space_kernel(side, acts, wide, small, mine, other, mix, packed, par, normed, weight, sems):
    finish(load_chips(side, mine, other, weight, sems))
    par[...] = weight[:, :, :, 768:896].reshape(D, 128).astype(F32).T[0:16, :]
    space_norm(acts, wide, small, par, normed)
    for sub in range(2):
        rows = normed[sub * 256 : sub * 256 + 256, :]
        for j in range(3):
            columns = weight[:, :, :, j * 256 : j * 256 + 256].reshape(D, 256)
            packed[sub, :, j * 256 : j * 256 + 256] = mm(rows, columns).astype(BF)
        mask = None if sub == 0 else small_mask()
        for p in range(2):
            q2, k2, v2 = (packed[sub, :, j * 256 + p * 128 : j * 256 + p * 128 + 128] for j in range(3))
            mix[sub * 256 : sub * 256 + 256, p * 128 : p * 128 + 128] = attend(q2, k2, v2, mask)


def time_kernel(
    side, s0, s1, s2, s3, mix, par, big,
    after_space, own_after, normed, packed, mixture, own_mix, wso, wtp, sems,
):
    copies = load_turns(big, 0, wso, sems)
    copy = pltpu.make_async_copy(big.at[:, 0:768], wtp, sems.at[4])
    copy.start()
    lane = lax.broadcasted_iota(jnp.int32, (1, 16), 1).astype(F32)
    for d, s in zip(TURNS, (s0, s1, s2, s3)):
        chosen = (s[:, D : D + 1].astype(F32) == lane).astype(BF)
        after_space[turned(side, d, -1)] = s[:, 0:D].astype(F32) + mm(chosen, par[...].astype(BF))
    stepped = 0.0
    for i, d in enumerate(TURNS):
        copies[i].wait()
        stepped = stepped + mt(mix[turned(side, d, -1)], wso[i])
    for g, block in enumerate(regroup(stepped)):
        block = after_space[g] + block
        after_space[g] = block
        scaled, _ = scaled_of(block)
        normed[128 * g : 128 * g + 128, :] = (scaled * par[9:10, :] + par[12:13, :]).astype(BF)
    for g, block in enumerate(regroup(mix[side[1]].astype(F32))):
        own_mix[128 * g : 128 * g + 128, :] = block.astype(BF)
    own_after[...] = after_space[side[1]]
    copy.wait()
    for j in range(3):
        packed[:, j * 256 : j * 256 + 256] = mm(normed[...], wtp[:, j * 256 : j * 256 + 256]).astype(BF)
    mask = time_mask()
    for g in range(4):
        rows = slice(128 * g, 128 * g + 128)
        for p in range(2):
            q2, k2, v2 = (packed[rows, j * 256 + p * 128 : j * 256 + p * 128 + 128] for j in range(3))
            mixture[rows, p * 128 : p * 128 + 128] = attend(q2, k2, v2, mask)


UP = slice(768, 1792)
DOWN = slice(1792, 2816)


def ffn_kernel(
    side, m0, m1, m2, m3, c0, c1, c2, c3, after_space, par, big,
    own_after, normed, cot, hidden, grad_raised, g0, g1, g2, g3, done, grad, wto, we, ws, sems,
):
    copies = load_turns(big, 256, wto, sems)
    more = [
        pltpu.make_async_copy(big.at[:, UP], we, sems.at[4]),
        pltpu.make_async_copy(big.at[:, DOWN], ws, sems.at[5]),
    ]
    for copy in more:
        copy.start()
    for d, c in zip(TURNS, (c0, c1, c2, c3)):
        cot[turned(side, d, -1)] = c[...]
    total = after_space[...].reshape(512, D)
    for i, m in enumerate((m0, m1, m2, m3)):
        copies[i].wait()
        total = total + mt(m[...], wto[i])
    scaled, _ = scaled_of(total)
    done[...] = total.reshape(4, 128, D)
    normed[...] = (scaled * par[10:11, :] + par[13:14, :]).astype(BF)
    own_after[...] = done[side[1]]
    for copy in more:
        copy.wait()
    for c in range(4):
        cols = slice(c * 256, c * 256 + 256)
        raised = mm(normed[...], we[:, cols])
        grad_hidden = mm(cot[...].reshape(512, D), ws[:, cols])
        spread = 0.5 * (1.0 + lax.erf(raised * math.sqrt(0.5)))
        bell = jnp.exp(-0.5 * raised * raised) * (1.0 / math.sqrt(2.0 * math.pi))
        hidden[:, cols] = (raised * spread).astype(BF)
        grad_raised[:, cols] = (grad_hidden * (spread + raised * bell)).astype(BF)
    grad[...] = mt(grad_raised[...], we[...]).astype(BF).reshape(4, 128, D)
    for d, g in zip(TURNS, (g0, g1, g2, g3)):
        g[...] = grad[turned(side, d, 1)]


def ffn_out_kernel(side, hidden, branch, big, o0, o1, o2, o3, out, ws, sems):
    copy = pltpu.make_async_copy(big.at[:, DOWN], ws, sems.at[0])
    copy.start()
    copy.wait()
    out[...] = mt(hidden[...], ws[...]).astype(BF).reshape(4, 128, D)
    for d, o in zip(TURNS, (o0, o1, o2, o3)):
        o[:, 0:D] = out[turned(side, d, 1)]
        o[:, D : 2 * D] = branch[...]


def halves(side, block):
    first, second = block[:, 0], block[:, 1]
    low = side[0] == 0
    return jnp.where(low, first, second), jnp.where(low, second, first)


def ffn_grad_kernel(normed, cot, hidden, grad_raised, out):
    for c in range(4):
        cols = slice(c * 256, c * 256 + 256)
        first = tm(normed[...], grad_raised[:, cols]).astype(BF).reshape(16, 2, 32, 256)
        second = tm(cot[...].reshape(512, D), hidden[:, cols]).astype(BF).reshape(16, 2, 32, 256)
        for start, block in ((c * 256, first), (D + c * 256, second)):
            for chip in range(16):
                clip, z, yh = chip // 8, (chip // 2) % 4, chip % 2
                for s in range(2):
                    out[z * 4 + yh * 2 + s, clip, :, start : start + 256] = block[chip, s]


def total_of(parts):
    return (parts[0][...].astype(F32) + parts[1][...].astype(F32)) + (parts[2][...].astype(F32) + parts[3][...].astype(F32))


def after_time_kernel(p0, p1, p2, p3, own_after, cot, par, grad_after, branch, sums):
    grad = total_of((p0, p1, p2, p3))
    scaled, inverse = scaled_of(own_after[...])
    sums[...] = jnp.zeros_like(sums)
    sums[10:11, :] = jnp.sum(grad * scaled, axis=0, keepdims=True)
    sums[13:14, :] = jnp.sum(grad, axis=0, keepdims=True)
    total = cot[...].astype(F32) + norm_back(grad, scaled, inverse, par[10:11, :])
    grad_after[...] = total
    branch[...] = total.astype(BF)


def time_back_kernel(
    side, b0, b1, b2, b3, packed, big,
    branches, grad_packed, p0, p1, p2, p3, grad, wto, wtp, sems,
):
    copy_out = pltpu.make_async_copy(big.at[:, 2816 + 256 : 2816 + 512], wto, sems.at[0])
    copy_out.start()
    copy = pltpu.make_async_copy(big.at[:, 0:768], wtp, sems.at[1])
    copy.start()
    copy_out.wait()
    mask = time_mask()
    for d, b in zip(TURNS, (b0, b1, b2, b3)):
        at = turned(side, d, -1)
        branches[at] = b[...]
        grad_mixture = mm(b[...], wto[...]).astype(BF)
        for p in range(2):
            q2, k2, v2 = (packed[at, :, j * 256 + p * 128 : j * 256 + p * 128 + 128] for j in range(3))
            back = attend_back(q2, k2, v2, grad_mixture[:, p * 128 : p * 128 + 128], mask)
            for j in range(3):
                grad_packed[at, :, j * 256 + p * 128 : j * 256 + p * 128 + 128] = back[j]
    copy.wait()
    grad[...] = mt(grad_packed[...].reshape(512, 768), wtp[...]).astype(BF).reshape(4, 128, D)
    for d, p in zip(TURNS, (p0, p1, p2, p3)):
        p[...] = grad[turned(side, d, 1)]


def after_space_kernel(
    side, p0, p1, p2, p3, own_after, grad_time, par, sums_in, big, grad_mix, grad_after, sums, wso, sems,
):
    copies = load_turns(big, 0, wso, sems)
    grad = total_of((p0, p1, p2, p3))
    scaled, inverse = scaled_of(own_after[...])
    sums[...] = sums_in[...]
    sums[9:10, :] = jnp.sum(grad * scaled, axis=0, keepdims=True)
    sums[12:13, :] = jnp.sum(grad, axis=0, keepdims=True)
    branch = (grad_time[...] + norm_back(grad, scaled, inverse, par[9:10, :])).astype(BF)
    grad_after[...] = branch
    for i, d in enumerate(TURNS):
        copies[i].wait()
        grad_mix[turned(side, d, -1)] = mm(branch, wso[i]).astype(BF)


def put_halves(side, pieces, kept, sent):
    for i, piece in enumerate(pieces):
        here, there = halves(side, piece.astype(BF).reshape(16, 2, 32, 256))
        kept[:, :, i * 256 : i * 256 + 256] = here
        sent[:, :, i * 256 : i * 256 + 256] = there


def time_grad_kernel(side, normed, grad_packed, branches, mixture, kept, sent):
    pieces = [tm(normed[...], grad_packed[:, j * 256 : j * 256 + 256]) for j in range(3)]
    put_halves(side, pieces + [tm(branches[...], mixture[...])], kept, sent)


def space_back_kernel(side, grad_mix, packed, mine, other, grad_packed, g0, g1, g2, g3, natural, grad, weight, sems):
    copies = load_chips(side, mine, other, weight, sems)
    natural[...] = ungroup([grad_mix[g].astype(F32) for g in range(4)]).astype(BF)
    for sub in range(2):
        mask = None if sub == 0 else small_mask()
        for p in range(2):
            q2, k2, v2 = (packed[sub, :, j * 256 + p * 128 : j * 256 + p * 128 + 128] for j in range(3))
            back = attend_back(q2, k2, v2, natural[sub * 256 : sub * 256 + 256, p * 128 : p * 128 + 128], mask)
            for j in range(3):
                grad_packed[sub, :, j * 256 + p * 128 : j * 256 + p * 128 + 128] = back[j]
    finish(copies)
    total = mt(grad_packed[...].reshape(512, 768), weight[:, :, :, 0:768].reshape(D, 768))
    for g, block in enumerate(regroup(total)):
        grad[g] = block.astype(BF)
    for d, ref in zip(TURNS, (g0, g1, g2, g3)):
        ref[...] = grad[turned(side, d, 1)]


def space_grad_kernel(side, acts, wide, small, par, grad_packed, own_mix, s0, s1, s2, s3, kept, sent, normed, spaces):
    space_norm(acts, wide, small, par, normed)
    for d, s in zip(TURNS, (s0, s1, s2, s3)):
        spaces[turned(side, d, -1)] = s[:, D : 2 * D]
    pieces = [tm(normed[...], grad_packed[...].reshape(512, 768)[:, j * 256 : j * 256 + 256]) for j in range(3)]
    put_halves(side, pieces + [tm(spaces[...].reshape(512, D), own_mix[...])], kept, sent)


def final_kernel(side, acts, own, p0, p1, p2, p3, grad_after, par, sums_in, grad_out, kept, sent, sums):
    sums[...] = sums_in[...]
    spans = [(0, 64, acts[0])] + [(64 + 16 * c, 80 + 16 * c, acts[1 + c]) for c in range(4)]
    for low, high, action in spans:
        rows = slice(low, high)
        entered = own[rows, 0:D].astype(F32) + par[pl.ds(action, 1), :]
        scaled, inverse = scaled_of(entered)
        grad = total_of([p.at[rows, :] for p in (p0, p1, p2, p3)])
        sums[8:9, :] += jnp.sum(grad * scaled, axis=0, keepdims=True)
        sums[11:12, :] += jnp.sum(grad, axis=0, keepdims=True)
        total = grad_after[rows, :].astype(F32) + norm_back(grad, scaled, inverse, par[8:9, :])
        grad_out[rows, :] = total.astype(BF)
        sums[pl.ds(action, 1), :] += jnp.sum(total, axis=0, keepdims=True)
    turned_sums = jnp.concatenate([sums[...], jnp.zeros((112, D), F32)], axis=0).T.reshape(16, 2, 32, 128)
    here, there = halves(side, turned_sums.astype(BF))
    kept[...] = here
    sent[...] = there


def place_kernel(side, b0, b1, b2, b3, wide, small, natural):
    for d, b in zip(TURNS, (b0, b1, b2, b3)):
        at = turned(side, d, -1)
        block = b[...].astype(F32)
        for f in range(16):
            natural[f, at] = block[8 * f : 8 * f + 8]
    wide[...] = natural[0:8].reshape(256, D).astype(wide.dtype)
    small[...] = natural[8:16].reshape(256, D).astype(small.dtype)


def swap(x, axes):
    return lax.all_to_all(x, axes, split_axis=0, concat_axis=0, tiled=True)


def spread(x, axes, n):
    return swap(jnp.broadcast_to(x[None], (n,) + x.shape), axes)


def shift(x, d):
    return lax.ppermute(x, "head", [(i, (i + d) % 4) for i in range(4)])


def core_swap(x):
    return lax.ppermute(x, "core", [(0, 1), (1, 0)])


def after(x, *others):
    return lax.optimization_barrier((x,) + others)[0]


def around(x):
    return [x] + [shift(x, d) for d in TURNS[1:]]


def body(
    frames_wide, frames_small, actions_wide, actions_small, cotangent_wide, cotangent_small,
    action_table, norm_gains, norm_shifts, space_project, space_output, time_project, time_output,
    expand_weight, shrink_weight,
):
    me = lax.axis_index("head")
    core = lax.axis_index("core")
    side = jnp.stack([core, me]).astype(jnp.int32)
    wide, small = frames_wide.reshape(256, D), frames_small.reshape(256, D)
    acts = jnp.concatenate([actions_wide.reshape(1), actions_small.reshape(4), jnp.zeros((3,), jnp.int32)])

    big = [time_project.reshape(32, 768), expand_weight, shrink_weight]
    big += around(jnp.concatenate([space_output, time_output], axis=1))
    big = lax.all_gather(jnp.concatenate(big, axis=1), CF, axis=0, tiled=True)

    def own_rows(x):
        return lax.dynamic_index_in_dim(x.reshape(8, 4, 8, D), me, 1, keepdims=False)

    marks = jnp.concatenate([jnp.broadcast_to(acts[0:1], (8,)), jnp.repeat(acts[1:5], 2)]).astype(BF)
    marks = jnp.broadcast_to(marks[:, None, None], (16, 8, 128))
    own = jnp.concatenate([own_rows(wide), own_rows(small)])
    own_cot = jnp.concatenate([own_rows(cotangent_wide), own_rows(cotangent_small)])
    own = lax.optimization_barrier(jnp.concatenate([own, marks, own_cot], axis=2))

    small_par = jnp.concatenate([action_table, norm_gains, norm_shifts, jnp.zeros((2, 32), BF)], axis=0).T
    first = jnp.concatenate([space_project.reshape(32, 768), jnp.pad(small_par, ((0, 0), (0, 112)))], axis=1)
    mine = spread(first, CHIPS, 16)
    other = core_swap(mine)
    stream = swap(after(own, mine), FRAME).reshape(128, 2176)
    streams, cots = around(stream[:, 0:1152]), around(stream[:, 1152:2176])

    def chips(size):
        return pltpu.VMEM((16, 2, 32, size), BF)

    def sems(count):
        return pltpu.SemaphoreType.DMA((count,))

    one, four, all_rows = ((128, D), BF), ((4, 128, D), BF), ((512, D), BF)
    mix_f, packed_f, par = call(
        space_kernel, [((512, 256), BF), ((2, 256, 768), BF), ((16, D), F32)], [SM] * 2 + [VM] * 2 + [HB] * 2,
        (side, acts, wide, small, mine, other), [pltpu.VMEM((512, D), BF), chips(896), sems(2)],
        flops=2 * 10**9, size=5 * 10**6,
    )
    mix = jnp.broadcast_to(mix_f.reshape(1, 16, 32, 256), (4, 16, 32, 256)).reshape(64, 32, 256)
    mix = swap(after(mix, stream), HF).reshape(4, 512, 256)

    turns = pltpu.VMEM((4, D, 256), BF)
    after_space, own_space, normed_t, packed_t, mixture, own_mix = call(
        time_kernel,
        [((4, 128, D), F32), ((128, D), F32), all_rows, ((512, 768), BF), ((512, 256), BF), ((512, 256), BF)],
        [SM] + [VM] * 6 + [HB], (side, *streams, mix, par, big),
        [turns, pltpu.VMEM((D, 768), BF), sems(5)], flops=3 * 10**9, size=9 * 10**6,
    )
    square = pltpu.VMEM((D, D), BF)
    own_time, normed_ffn, cot, hidden, grad_raised, *parts = call(
        ffn_kernel, [((128, D), F32), all_rows, four, all_rows, all_rows] + [one] * 4, [SM] + [VM] * 10 + [HB],
        (side, *around(mixture), *cots, after_space, par, big),
        [pltpu.VMEM((4, 128, D), F32), pltpu.VMEM((4, 128, D), BF), turns, square, square, sems(6)],
        flops=5 * 10**9, size=14 * 10**6,
    )

    def send(blocks):
        return [blocks[0]] + [shift(block, d) for block, d in zip(blocks[1:], TURNS[1:])]

    parts = send(parts)
    (ffn_grad,) = call(
        ffn_grad_kernel, [((16, 2, 32, 2 * D), BF)], [VM] * 4, (normed_ffn, cot, hidden, grad_raised),
        flops=2 * 10**9, size=8 * 10**6,
    )
    grad_time, branch, sums = call(
        after_time_kernel, [((128, D), F32), one, ((16, D), F32)], [VM] * 7,
        (*parts, own_time, cots[0], after(par, ffn_grad)), flops=10**8, size=4 * 10**6,
    )
    branches = around(branch)
    branches, grad_packed_t, *parts = call(
        time_back_kernel, [four, ((4, 128, 768), BF)] + [one] * 4, [SM] + [VM] * 5 + [HB],
        (side, *branches, packed_t.reshape(4, 128, 768), big),
        [pltpu.VMEM((4, 128, D), BF), pltpu.VMEM((D, 256), BF), pltpu.VMEM((D, 768), BF), sems(2)], flops=2 * 10**9, size=8 * 10**6,
    )
    parts = send(parts)
    grad_mix, grad_space, sums = call(
        after_space_kernel, [((4, 128, 256), BF), one, ((16, D), F32)], [SM] + [VM] * 8 + [HB],
        (side, *parts, own_space, grad_time, par, sums, big), [turns, sems(4)],
        flops=3 * 10**8, size=5 * 10**6,
    )
    grad_mix = swap(grad_mix.reshape(64, 8, 256), HF).reshape(4, 128, 256)
    outs = call(
        ffn_out_kernel, [((128, 2 * D), BF)] * 4, [SM, VM, VM, HB], (side, hidden, grad_space, big),
        [pltpu.VMEM((4, 128, D), BF), square, sems(1)], flops=10**9, size=4 * 10**6,
    )
    outs = send(outs)
    grad_space = swap(after(grad_space, grad_mix).reshape(16, 8, D), FRAME).reshape(128, D)

    grad_packed_f, *parts = call(
        space_back_kernel, [((2, 256, 768), BF)] + [one] * 4, [SM] + [VM] * 2 + [HB] * 2,
        (side, grad_mix, packed_f, mine, other),
        [pltpu.VMEM((512, 256), BF), pltpu.VMEM((4, 128, D), BF), chips(896), sems(2)], flops=2 * 10**9, size=4 * 10**6,
    )
    parts = send(parts)
    chunk = ((16, 32, 128), BF)
    grad_own, par_kept, par_sent = call(
        final_kernel, [one, chunk, chunk], [SM] * 2 + [VM] * 8,
        (side, acts, own.reshape(128, 2176), *parts, grad_space, par, sums), [pltpu.VMEM((16, D), F32)],
        flops=10**8, size=2 * 10**6,
    )
    grad_in = around(grad_own)
    result = total_of([block[:, 0:D] for block in outs]) + own_time
    result = swap(after(result.astype(BF), grad_space).reshape(16, 8, D), FRAME).reshape(128, D)
    result = around(after(result, grad_in[1]))
    ffn_total = lax.psum_scatter(ffn_grad, FRAME, scatter_dimension=0, tiled=True).reshape(2, 32, 2 * D)
    clip = lax.axis_index("clip")
    ffn_kept, ffn_sent = (lax.dynamic_index_in_dim(ffn_total, i, 0, keepdims=False) for i in (clip, 1 - clip))
    ffn_total = ffn_kept.astype(F32) + lax.ppermute(ffn_sent, "clip", [(0, 1), (1, 0)]).astype(F32)

    natural = [pltpu.VMEM((16, 4, 8, D), F32)]
    grad_out = call(
        place_kernel, [((256, D), F32)] * 2, [SM] + [VM] * 4, (side, *grad_in), natural, flops=10**6, size=3 * 10**6,
    )
    result = call(
        place_kernel, [((256, D), BF)] * 2, [SM] + [VM] * 4, (side, *after(result, ffn_total)), natural, flops=10**6, size=3 * 10**6,
    )

    time_kept, time_sent = call(
        time_grad_kernel, [((16, 32, D), BF)] * 2, [SM] + [VM] * 4,
        (side, normed_t, grad_packed_t.reshape(512, 768), branches.reshape(512, D), mixture),
        flops=2 * 10**9, size=8 * 10**6,
    )
    space_kept, space_sent = call(
        space_grad_kernel, [((16, 32, D), BF)] * 2, [SM] * 2 + [VM] * 9,
        (side, acts, wide, small, par, grad_packed_f, after(own_mix, parts[1]), *outs),
        [pltpu.VMEM((512, D), BF), pltpu.VMEM((4, 128, D), BF)], flops=10**9, size=4 * 10**6,
    )

    def pair_sum(kept, sent):
        return (kept.astype(F32) + core_swap(sent).astype(F32)).astype(BF)

    def chip_sum(x):
        return jnp.sum(swap(x, CHIPS).astype(F32), axis=0)

    total = [pair_sum(time_kept, time_sent), pair_sum(space_kept, space_sent), pair_sum(par_kept, par_sent)]
    total = chip_sum(jnp.concatenate(total, axis=2))
    par_total = total_of(around(total[:, 2048:2176].astype(BF)))[:, 0:16].T

    return (
        result[0].reshape(1, 1, 256, D),
        result[1].reshape(4, 1, 64, D),
        grad_out[0].reshape(1, 1, 256, D),
        grad_out[1].reshape(4, 1, 64, D),
        par_total[0:8],
        par_total[8:11],
        par_total[11:14],
        total[:, 1024:1792].reshape(32, 3, 256),
        total[:, 1792:2048],
        total[:, 0:768].reshape(32, 3, 256),
        total[:, 768:1024],
        ffn_total[:, 0:D],
        ffn_total[:, D : 2 * D],
    )


def solution(mesh):
    fine = Mesh(mesh.devices.reshape(2, 4, 2, 2, 4), ALL)
    tokens = P("clip", FRAME, None, None)
    columns = P(None, CF)
    square, cube = P(CF, "head"), P(CF, None, "head")
    frames = P("clip", FRAME)
    weights = (cube, square, cube, square, square, square)
    in_specs = (tokens, tokens, frames, frames, tokens, tokens) + (columns,) * 3 + weights
    out_specs = (tokens,) * 4 + (columns,) * 3 + weights
    return jax.shard_map(body, mesh=fine, in_specs=in_specs, out_specs=out_specs, check_vma=False)
```

```python
import functools
import math

import jax
import jax.numpy as jnp
from jax import lax
from jax.experimental import pallas as pl
from jax.experimental.pallas import tpu as pltpu
from jax.sharding import Mesh
from jax.sharding import PartitionSpec as P

BF = jnp.bfloat16
F32 = jnp.float32
EPS = 1e-05
CF = ("clip", "z", "yh", "core")
FRAME = ("z", "yh", "core")
CHIPS = ("clip", "z", "yh")
HF = ("head", "z", "yh", "core")
ALL = ("clip", "z", "yh", "core", "head")
D = 1024
VM = pl.BlockSpec(memory_space=pltpu.VMEM)
SM = pl.BlockSpec(memory_space=pltpu.SMEM)
HB = pl.BlockSpec(memory_space=pl.ANY)
SCALE = 0.125


def mm(a, b):
    return lax.dot_general(a, b, (((1,), (0,)), ((), ())), preferred_element_type=F32)


def mt(a, b):
    return lax.dot_general(a, b, (((1,), (1,)), ((), ())), preferred_element_type=F32)


def tm(a, b):
    return lax.dot_general(a, b, (((0,), (0,)), ((), ())), preferred_element_type=F32)


def call(body, outs, specs, args, scratch=(), flops=0, size=0):
    return pl.pallas_call(
        body,
        out_shape=[jax.ShapeDtypeStruct(s, t) for s, t in outs],
        in_specs=specs,
        out_specs=[VM] * len(outs),
        scratch_shapes=list(scratch),
        compiler_params=pltpu.CompilerParams(vmem_limit_bytes=56 * 2**20),
        cost_estimate=pl.CostEstimate(flops=flops, bytes_accessed=size, transcendentals=0),
    )(*args)


def scaled_of(stream):
    average = jnp.mean(stream, axis=-1, keepdims=True)
    centered = stream - average
    inverse = lax.rsqrt(jnp.mean(centered * centered, axis=-1, keepdims=True) + EPS)
    return centered * inverse, inverse


def norm_back(grad, scaled, inverse, gain):
    grad_scaled = grad * gain
    inner = jnp.mean(grad_scaled, axis=-1, keepdims=True)
    along = jnp.mean(grad_scaled * scaled, axis=-1, keepdims=True)
    return inverse * (grad_scaled - inner - scaled * along)


def lane_half(side):
    lane = lax.broadcasted_iota(jnp.int32, (1, 128), 1)
    return (lane < 64) if side == 0 else (lane >= 64)


def pick(side, block):
    return jnp.where(lane_half(side), block, jnp.zeros_like(block))


def chances_of(queries, keys, mask):
    scores = mt(queries, keys) * SCALE
    if mask is not None:
        scores = jnp.where(mask, scores, -1e30)
    raised = jnp.exp(scores - jnp.max(scores, axis=-1, keepdims=True))
    return raised * (1.0 / jnp.sum(raised, axis=-1, keepdims=True))


def attend(q2, k2, v2, mask):
    total = 0.0
    for side in range(2):
        chances = chances_of(pick(side, q2), k2, mask).astype(BF)
        total = total + mm(chances, pick(side, v2))
    return total.astype(BF)


def attend_back(q2, k2, v2, g2, mask):
    grad_q, grad_k, grad_v = 0.0, 0.0, 0.0
    for side in range(2):
        qs = pick(side, q2)
        gs = pick(side, g2)
        chances = chances_of(qs, k2, mask)
        grad_v = grad_v + tm(chances.astype(BF), gs)
        grad_chances = mt(gs, v2)
        weighted = jnp.sum(grad_chances * chances, axis=-1, keepdims=True)
        grad_scores = (chances * (grad_chances - weighted)).astype(BF)
        grad_q = grad_q + mm(grad_scores, pick(side, k2))
        grad_k = grad_k + tm(grad_scores, qs)
    return (grad_q * SCALE).astype(BF), (grad_k * SCALE).astype(BF), grad_v.astype(BF)


def small_mask():
    row = lax.broadcasted_iota(jnp.int32, (256, 256), 0)
    col = lax.broadcasted_iota(jnp.int32, (256, 256), 1)
    return (row // 64) == (col // 64)


def time_mask():
    row = lax.broadcasted_iota(jnp.int32, (128, 128), 0)
    col = lax.broadcasted_iota(jnp.int32, (128, 128), 1)
    return (col <= row) & ((row % 8) == (col % 8))


TURNS = (0, 1, 3, 2)


def load_chips(side, mine, other, dest, sems):
    core = side[0]
    copies = [
        pltpu.make_async_copy(mine, dest.at[:, core], sems.at[0]),
        pltpu.make_async_copy(other, dest.at[:, 1 - core], sems.at[1]),
    ]
    for copy in copies:
        copy.start()
    return copies


def load_turns(big, offset, dest, sems):
    copies = []
    for d in range(4):
        start = 2816 + 512 * d + offset
        copies.append(pltpu.make_async_copy(big.at[:, start : start + 256], dest.at[d], sems.at[d]))
        copies[d].start()
    return copies


def finish(copies):
    for copy in copies:
        copy.wait()


def turned(side, d, sign):
    return lax.rem(side[1] + 4 + sign * d, 4)


def regroup(block):
    width = block.shape[1]
    parts = block.reshape(16, 4, 8, width)
    return [parts[:, g].reshape(128, width) for g in range(4)]


def ungroup(blocks):
    width = blocks[0].shape[1]
    return jnp.stack([block.reshape(16, 8, width) for block in blocks], axis=1).reshape(512, width)


def space_norm(acts, wide, small, par, normed):
    for sub, ref in enumerate((wide, small)):
        for b in range(4):
            action = acts[0] if sub == 0 else acts[1 + b]
            entered = ref[64 * b : 64 * b + 64, :].astype(F32) + par[pl.ds(action, 1), :]
            scaled, _ = scaled_of(entered)
            start = sub * 256 + b * 64
            normed[start : start + 64, :] = (scaled * par[8:9, :] + par[11:12, :]).astype(BF)


def space_kernel(side, acts, wide, small, mine, other, mix, packed, par, normed, weight, sems):
    finish(load_chips(side, mine, other, weight, sems))
    par[...] = weight[:, :, :, 768:896].reshape(D, 128).astype(F32).T[0:16, :]
    space_norm(acts, wide, small, par, normed)
    for sub in range(2):
        rows = normed[sub * 256 : sub * 256 + 256, :]
        for j in range(3):
            columns = weight[:, :, :, j * 256 : j * 256 + 256].reshape(D, 256)
            packed[sub, :, j * 256 : j * 256 + 256] = mm(rows, columns).astype(BF)
        mask = None if sub == 0 else small_mask()
        for p in range(2):
            q2, k2, v2 = (packed[sub, :, j * 256 + p * 128 : j * 256 + p * 128 + 128] for j in range(3))
            mix[sub * 256 : sub * 256 + 256, p * 128 : p * 128 + 128] = attend(q2, k2, v2, mask)


def time_kernel(
    side, s0, s1, s2, s3, mix, par, big,
    after_space, own_after, normed, packed, mixture, own_mix, wso, wtp, sems,
):
    copies = load_turns(big, 0, wso, sems)
    copy = pltpu.make_async_copy(big.at[:, 0:768], wtp, sems.at[4])
    copy.start()
    lane = lax.broadcasted_iota(jnp.int32, (1, 16), 1).astype(F32)
    for d, s in zip(TURNS, (s0, s1, s2, s3)):
        chosen = (s[:, D : D + 1].astype(F32) == lane).astype(BF)
        after_space[turned(side, d, -1)] = s[:, 0:D].astype(F32) + mm(chosen, par[...].astype(BF))
    stepped = 0.0
    for i, d in enumerate(TURNS):
        copies[i].wait()
        stepped = stepped + mt(mix[turned(side, d, -1)], wso[i])
    for g, block in enumerate(regroup(stepped)):
        block = after_space[g] + block
        after_space[g] = block
        scaled, _ = scaled_of(block)
        normed[128 * g : 128 * g + 128, :] = (scaled * par[9:10, :] + par[12:13, :]).astype(BF)
    for g, block in enumerate(regroup(mix[side[1]].astype(F32))):
        own_mix[128 * g : 128 * g + 128, :] = block.astype(BF)
    own_after[...] = after_space[side[1]]
    copy.wait()
    for j in range(3):
        packed[:, j * 256 : j * 256 + 256] = mm(normed[...], wtp[:, j * 256 : j * 256 + 256]).astype(BF)
    mask = time_mask()
    for g in range(4):
        rows = slice(128 * g, 128 * g + 128)
        for p in range(2):
            q2, k2, v2 = (packed[rows, j * 256 + p * 128 : j * 256 + p * 128 + 128] for j in range(3))
            mixture[rows, p * 128 : p * 128 + 128] = attend(q2, k2, v2, mask)


UP = slice(768, 1792)
DOWN = slice(1792, 2816)


def ffn_kernel(
    side, m0, m1, m2, m3, c0, c1, c2, c3, after_space, par, big,
    own_after, normed, cot, hidden, grad_raised, g0, g1, g2, g3, done, grad, wto, we, ws, sems,
):
    copies = load_turns(big, 256, wto, sems)
    more = [
        pltpu.make_async_copy(big.at[:, UP], we, sems.at[4]),
        pltpu.make_async_copy(big.at[:, DOWN], ws, sems.at[5]),
    ]
    for copy in more:
        copy.start()
    for d, c in zip(TURNS, (c0, c1, c2, c3)):
        cot[turned(side, d, -1)] = c[...]
    total = after_space[...].reshape(512, D)
    for i, m in enumerate((m0, m1, m2, m3)):
        copies[i].wait()
        total = total + mt(m[...], wto[i])
    scaled, _ = scaled_of(total)
    done[...] = total.reshape(4, 128, D)
    normed[...] = (scaled * par[10:11, :] + par[13:14, :]).astype(BF)
    own_after[...] = done[side[1]]
    for copy in more:
        copy.wait()
    for c in range(4):
        cols = slice(c * 256, c * 256 + 256)
        raised = mm(normed[...], we[:, cols])
        grad_hidden = mm(cot[...].reshape(512, D), ws[:, cols])
        spread = 0.5 * (1.0 + lax.erf(raised * math.sqrt(0.5)))
        bell = jnp.exp(-0.5 * raised * raised) * (1.0 / math.sqrt(2.0 * math.pi))
        hidden[:, cols] = (raised * spread).astype(BF)
        grad_raised[:, cols] = (grad_hidden * (spread + raised * bell)).astype(BF)
    grad[...] = mt(grad_raised[...], we[...]).astype(BF).reshape(4, 128, D)
    for d, g in zip(TURNS, (g0, g1, g2, g3)):
        g[...] = grad[turned(side, d, 1)]


def ffn_out_kernel(side, hidden, big, o0, o1, o2, o3, out, ws, sems):
    copy = pltpu.make_async_copy(big.at[:, DOWN], ws, sems.at[0])
    copy.start()
    copy.wait()
    out[...] = mt(hidden[...], ws[...]).astype(BF).reshape(4, 128, D)
    for d, o in zip(TURNS, (o0, o1, o2, o3)):
        o[...] = out[turned(side, d, 1)]


def halves(side, block):
    first, second = block[:, 0], block[:, 1]
    low = side[0] == 0
    return jnp.where(low, first, second), jnp.where(low, second, first)


def put_frames(piece, out, start):
    block = piece.astype(BF).reshape(16, 2, 32, piece.shape[1])
    for chip in range(16):
        clip, z, yh = chip // 8, (chip // 2) % 4, chip % 2
        for s in range(2):
            out[z * 4 + yh * 2 + s, clip, :, start : start + piece.shape[1]] = block[chip, s]


def ffn_grad_kernel(normed, cot, hidden, grad_raised, out):
    for c in range(4):
        cols = slice(c * 256, c * 256 + 256)
        put_frames(tm(normed[...], grad_raised[:, cols]), out, c * 256)
        put_frames(tm(cot[...].reshape(512, D), hidden[:, cols]), out, D + c * 256)


def total_of(parts):
    return (parts[0][...].astype(F32) + parts[1][...].astype(F32)) + (parts[2][...].astype(F32) + parts[3][...].astype(F32))


def after_time_kernel(p0, p1, p2, p3, own_after, cot, par, grad_after, branch, sums):
    grad = total_of((p0, p1, p2, p3))
    scaled, inverse = scaled_of(own_after[...])
    sums[...] = jnp.zeros_like(sums)
    sums[10:11, :] = jnp.sum(grad * scaled, axis=0, keepdims=True)
    sums[13:14, :] = jnp.sum(grad, axis=0, keepdims=True)
    total = cot[...].astype(F32) + norm_back(grad, scaled, inverse, par[10:11, :])
    grad_after[...] = total
    branch[...] = total.astype(BF)


def time_back_kernel(
    side, b0, b1, b2, b3, packed, big,
    branches, grad_packed, p0, p1, p2, p3, grad, wto, wtp, sems,
):
    copy_out = pltpu.make_async_copy(big.at[:, 2816 + 256 : 2816 + 512], wto, sems.at[0])
    copy_out.start()
    copy = pltpu.make_async_copy(big.at[:, 0:768], wtp, sems.at[1])
    copy.start()
    copy_out.wait()
    mask = time_mask()
    for d, b in zip(TURNS, (b0, b1, b2, b3)):
        at = turned(side, d, -1)
        branches[at] = b[...]
        grad_mixture = mm(b[...], wto[...]).astype(BF)
        for p in range(2):
            q2, k2, v2 = (packed[at, :, j * 256 + p * 128 : j * 256 + p * 128 + 128] for j in range(3))
            back = attend_back(q2, k2, v2, grad_mixture[:, p * 128 : p * 128 + 128], mask)
            for j in range(3):
                grad_packed[at, :, j * 256 + p * 128 : j * 256 + p * 128 + 128] = back[j]
    copy.wait()
    grad[...] = mt(grad_packed[...].reshape(512, 768), wtp[...]).astype(BF).reshape(4, 128, D)
    for d, p in zip(TURNS, (p0, p1, p2, p3)):
        p[...] = grad[turned(side, d, 1)]


def after_space_kernel(
    side, p0, p1, p2, p3, o0, o1, o2, o3, own_after, own_time, grad_time, par, sums_in, big,
    grad_mix, grad_after, sums, wso, sems,
):
    copies = load_turns(big, 0, wso, sems)
    grad = total_of((p0, p1, p2, p3))
    scaled, inverse = scaled_of(own_after[...])
    sums[...] = sums_in[...]
    sums[9:10, :] = jnp.sum(grad * scaled, axis=0, keepdims=True)
    sums[12:13, :] = jnp.sum(grad, axis=0, keepdims=True)
    branch = (grad_time[...] + norm_back(grad, scaled, inverse, par[9:10, :])).astype(BF)
    grad_after[...] = branch
    result = (total_of((o0, o1, o2, o3)) + own_time[...]).astype(BF)
    for h in range(4):
        grad_mix[h, :, 256:512] = branch[:, h * 256 : h * 256 + 256]
        grad_mix[h, :, 512:768] = result[:, h * 256 : h * 256 + 256]
    for i, d in enumerate(TURNS):
        copies[i].wait()
        grad_mix[turned(side, d, -1), :, 0:256] = mm(branch, wso[i]).astype(BF)


def put_halves(side, pieces, kept, sent):
    for i, piece in enumerate(pieces):
        here, there = halves(side, piece.astype(BF).reshape(16, 2, 32, 256))
        kept[:, :, i * 256 : i * 256 + 256] = here
        sent[:, :, i * 256 : i * 256 + 256] = there


def time_grad_kernel(normed, grad_packed, branches, mixture, grads_in, grads, part, sems):
    for j in range(3):
        put_frames(tm(normed[...], grad_packed[:, j * 256 : j * 256 + 256]), part, j * 256)
    put_frames(tm(branches[...], mixture[...]), part, 768)
    copy = pltpu.make_async_copy(part, grads.at[:, :, :, 2 * D : 3 * D], sems.at[0])
    copy.start()
    copy.wait()


def space_back_kernel(side, grad_mix, packed, mine, other, grad_packed, result, g0, g1, g2, g3, natural, grad, weight, sems):
    copies = load_chips(side, mine, other, weight, sems)
    natural[...] = ungroup([grad_mix[g, :, 0:256].astype(F32) for g in range(4)]).astype(BF)
    for sub in range(2):
        mask = None if sub == 0 else small_mask()
        for p in range(2):
            q2, k2, v2 = (packed[sub, :, j * 256 + p * 128 : j * 256 + p * 128 + 128] for j in range(3))
            back = attend_back(q2, k2, v2, natural[sub * 256 : sub * 256 + 256, p * 128 : p * 128 + 128], mask)
            for j in range(3):
                grad_packed[sub, :, j * 256 + p * 128 : j * 256 + p * 128 + 128] = back[j]
    finish(copies)
    total = mt(grad_packed[...].reshape(512, 768), weight[:, :, :, 0:768].reshape(D, 768))
    for g, block in enumerate(regroup(total)):
        grad[g] = block.astype(BF)
    for d, ref in zip(TURNS, (g0, g1, g2, g3)):
        at = turned(side, d, 1)
        ref[:, 0:D] = grad[at]
        ref[:, D : D + 256] = grad_mix[at, :, 256:512]
    for g in range(4):
        result[128 * g : 128 * g + 128, :] = grad_mix[g, :, 512:768]


def space_grad_kernel(side, normed, grad_packed, own_mix, s0, s1, s2, s3, kept, sent, spaces):
    for d, s in zip(TURNS, (s0, s1, s2, s3)):
        spaces[turned(side, d, -1)] = s[...]
    pieces = [tm(normed[...], grad_packed[...].reshape(512, 768)[:, j * 256 : j * 256 + 256]) for j in range(3)]
    put_halves(side, pieces + [tm(spaces[...].reshape(512, D), own_mix[...])], kept, sent)


def final_kernel(side, acts, own, p0, p1, p2, p3, result, par, sums_in, grad_out, par_out, sums, after):
    sums[...] = sums_in[...]
    for d, p in zip(TURNS, (p0, p1, p2, p3)):
        after[:, pl.ds(pl.multiple_of(turned(side, d, -1) * 256, 256), 256)] = p[:, D : D + 256]
    spans = [(0, 64, acts[0])] + [(64 + 16 * c, 80 + 16 * c, acts[1 + c]) for c in range(4)]
    for low, high, action in spans:
        rows = slice(low, high)
        entered = own[rows, 0:D].astype(F32) + par[pl.ds(action, 1), :]
        scaled, inverse = scaled_of(entered)
        grad = total_of([p.at[rows, 0:D] for p in (p0, p1, p2, p3)])
        sums[8:9, :] += jnp.sum(grad * scaled, axis=0, keepdims=True)
        sums[11:12, :] += jnp.sum(grad, axis=0, keepdims=True)
        total = after[rows, :].astype(F32) + norm_back(grad, scaled, inverse, par[8:9, :])
        grad_out[rows, 0:D] = total.astype(BF)
        sums[pl.ds(action, 1), :] += jnp.sum(total, axis=0, keepdims=True)
    for g in range(4):
        grad_out[:, D + g * 256 : D + g * 256 + 256] = result[128 * g : 128 * g + 128, :]
    turned_sums = jnp.concatenate([sums[...], jnp.zeros((112, D), F32)], axis=0).T.reshape(16, 2, 32, 128)
    both = jnp.concatenate([turned_sums[:, 0, :, 0:16], turned_sums[:, 1, :, 0:16], turned_sums[:, 0, :, 32:128]], axis=2)
    par_out[...] = both.astype(BF)


def place_kernel(side, b0, b1, b2, b3, grad_wide, grad_small, wide, small, grad, result):
    for d, b in zip(TURNS, (b0, b1, b2, b3)):
        at = turned(side, d, -1)
        cols = pl.ds(pl.multiple_of(at * 256, 256), 256)
        block = b[:, 0:D].astype(F32)
        for f in range(16):
            grad[f, at] = block[8 * f : 8 * f + 8]
        for g in range(4):
            block = b[:, D + g * 256 : D + g * 256 + 256].astype(F32)
            for f in range(16):
                result[f, g, :, cols] = block[8 * f : 8 * f + 8]
    grad_wide[...] = grad[0:8].reshape(256, D)
    grad_small[...] = grad[8:16].reshape(256, D)
    wide[...] = result[0:8].reshape(256, D).astype(BF)
    small[...] = result[8:16].reshape(256, D).astype(BF)


def swap(x, axes):
    return lax.all_to_all(x, axes, split_axis=0, concat_axis=0, tiled=True)


def spread(x, axes, n):
    return swap(jnp.broadcast_to(x[None], (n,) + x.shape), axes)


def shift(x, d):
    return lax.ppermute(x, "head", [(i, (i + d) % 4) for i in range(4)])


def core_swap(x):
    return lax.ppermute(x, "core", [(0, 1), (1, 0)])


def after(x, *others):
    return lax.optimization_barrier((x,) + others)[0]


def around(x):
    return [x] + [shift(x, d) for d in TURNS[1:]]


def body(
    frames_wide, frames_small, actions_wide, actions_small, cotangent_wide, cotangent_small,
    action_table, norm_gains, norm_shifts, space_project, space_output, time_project, time_output,
    expand_weight, shrink_weight,
):
    me = lax.axis_index("head")
    core = lax.axis_index("core")
    side = jnp.stack([core, me]).astype(jnp.int32)
    wide, small = frames_wide.reshape(256, D), frames_small.reshape(256, D)
    acts = jnp.concatenate([actions_wide.reshape(1), actions_small.reshape(4), jnp.zeros((3,), jnp.int32)])

    big = [time_project.reshape(32, 768), expand_weight, shrink_weight]
    big += around(jnp.concatenate([space_output, time_output], axis=1))
    big = lax.all_gather(jnp.concatenate(big, axis=1), CF, axis=0, tiled=True)

    def own_rows(x):
        return lax.dynamic_index_in_dim(x.reshape(8, 4, 8, D), me, 1, keepdims=False)

    marks = jnp.concatenate([jnp.broadcast_to(acts[0:1], (8,)), jnp.repeat(acts[1:5], 2)]).astype(BF)
    marks = jnp.broadcast_to(marks[:, None, None], (16, 8, 128))
    own = jnp.concatenate([own_rows(wide), own_rows(small)])
    own_cot = jnp.concatenate([own_rows(cotangent_wide), own_rows(cotangent_small)])
    own = lax.optimization_barrier(jnp.concatenate([own, marks, own_cot], axis=2))

    small_par = jnp.concatenate([action_table, norm_gains, norm_shifts, jnp.zeros((2, 32), BF)], axis=0).T
    first = jnp.concatenate([space_project.reshape(32, 768), jnp.pad(small_par, ((0, 0), (0, 112)))], axis=1)
    mine = spread(first, CHIPS, 16)
    other = core_swap(mine)
    stream = swap(after(own, mine), FRAME).reshape(128, 2176)
    streams = around(stream[:, 0:1152])
    cots = around(after(stream[:, 1152:2176], *streams))

    def chips(size):
        return pltpu.VMEM((16, 2, 32, size), BF)

    def sems(count):
        return pltpu.SemaphoreType.DMA((count,))

    one, four, all_rows = ((128, D), BF), ((4, 128, D), BF), ((512, D), BF)
    mix_f, packed_f, par, normed_s = call(
        space_kernel, [((512, 256), BF), ((2, 256, 768), BF), ((16, D), F32), all_rows], [SM] * 2 + [VM] * 2 + [HB] * 2,
        (side, acts, wide, small, mine, other), [chips(896), sems(2)],
        flops=2 * 10**9, size=5 * 10**6,
    )
    mix = jnp.broadcast_to(mix_f.reshape(1, 16, 32, 256), (4, 16, 32, 256)).reshape(64, 32, 256)
    mix = swap(after(mix, stream), HF).reshape(4, 512, 256)

    turns = pltpu.VMEM((4, D, 256), BF)
    after_space, own_space, normed_t, packed_t, mixture, own_mix = call(
        time_kernel,
        [((4, 128, D), F32), ((128, D), F32), all_rows, ((512, 768), BF), ((512, 256), BF), ((512, 256), BF)],
        [SM] + [VM] * 6 + [HB], (side, *streams, mix, par, big),
        [turns, pltpu.VMEM((D, 768), BF), sems(5)], flops=3 * 10**9, size=9 * 10**6,
    )
    square = pltpu.VMEM((D, D), BF)
    own_time, normed_ffn, cot, hidden, grad_raised, *parts = call(
        ffn_kernel, [((128, D), F32), all_rows, four, all_rows, all_rows] + [one] * 4, [SM] + [VM] * 10 + [HB],
        (side, *around(after(mixture, *cots)), *cots, after_space, par, big),
        [pltpu.VMEM((4, 128, D), F32), pltpu.VMEM((4, 128, D), BF), turns, square, square, sems(6)],
        flops=5 * 10**9, size=14 * 10**6,
    )

    def send(blocks):
        return [blocks[0]] + [shift(block, d) for block, d in zip(blocks[1:], TURNS[1:])]

    parts = send(parts)
    (ffn_grad,) = call(
        ffn_grad_kernel, [((16, 2, 32, 3 * D), BF)], [VM] * 4, (normed_ffn, cot, hidden, grad_raised),
        flops=2 * 10**9, size=8 * 10**6,
    )
    grad_time, branch, sums = call(
        after_time_kernel, [((128, D), F32), one, ((16, D), F32)], [VM] * 7,
        (*parts, own_time, cots[0], after(par, ffn_grad)), flops=10**8, size=4 * 10**6,
    )
    branch_list = around(branch)
    outs = call(
        ffn_out_kernel, [one] * 4, [SM, VM, HB], (side, after(hidden, grad_time), big),
        [pltpu.VMEM((4, 128, D), BF), square, sems(1)], flops=10**9, size=4 * 10**6,
    )
    branches, grad_packed_t, *parts = call(
        time_back_kernel, [four, ((4, 128, 768), BF)] + [one] * 4, [SM] + [VM] * 5 + [HB],
        (side, *branch_list, after(packed_t, outs[0]).reshape(4, 128, 768), big),
        [pltpu.VMEM((4, 128, D), BF), pltpu.VMEM((D, 256), BF), pltpu.VMEM((D, 768), BF), sems(2)], flops=2 * 10**9, size=8 * 10**6,
    )
    outs = send([outs[0]] + [after(block, *branch_list) for block in outs[1:]])
    grads = pl.pallas_call(
        time_grad_kernel,
        out_shape=jax.ShapeDtypeStruct((16, 2, 32, 3 * D), BF),
        in_specs=[VM] * 4 + [HB],
        out_specs=HB,
        scratch_shapes=[pltpu.VMEM((16, 2, 32, D), BF), sems(1)],
        input_output_aliases={4: 0},
        compiler_params=pltpu.CompilerParams(vmem_limit_bytes=56 * 2**20),
        cost_estimate=pl.CostEstimate(flops=2 * 10**9, bytes_accessed=8 * 10**6, transcendentals=0),
    )(normed_t, grad_packed_t.reshape(512, 768), branches.reshape(512, D), after(mixture, *outs), ffn_grad)
    parts = send([parts[0]] + [after(block, *outs) for block in parts[1:]])
    grad_mix, grad_space, sums = call(
        after_space_kernel, [((4, 128, 768), BF), one, ((16, D), F32)], [SM] + [VM] * 13 + [HB],
        (side, *parts, *outs, own_space, own_time, grad_time, after(par, grads), sums, big), [turns, sems(4)],
        flops=3 * 10**8, size=5 * 10**6,
    )
    grad_mix = swap(grad_mix.reshape(64, 8, 768), HF).reshape(4, 128, 768)
    spaces = around(grad_space)
    def pair_sum(kept, sent):
        return (kept.astype(F32) + core_swap(sent).astype(F32)).astype(BF)

    def chip_sum(x):
        return jnp.sum(swap(x, CHIPS).astype(F32), axis=0)

    grad_packed_f, result, *parts = call(
        space_back_kernel, [((2, 256, 768), BF), ((512, 256), BF)] + [((128, 1280), BF)] * 4, [SM] + [VM] * 2 + [HB] * 2,
        (side, grad_mix, packed_f, mine, other),
        [pltpu.VMEM((512, 256), BF), pltpu.VMEM((4, 128, D), BF), chips(896), sems(2)], flops=2 * 10**9, size=4 * 10**6,
    )
    parts = send(parts)
    space_kept, space_sent = call(
        space_grad_kernel, [((16, 32, D), BF)] * 2, [SM] + [VM] * 7, (side, normed_s, grad_packed_f, own_mix, *spaces),
        [pltpu.VMEM((4, 128, D), BF)], flops=10**9, size=4 * 10**6,
    )
    chunk = ((16, 32, 128), BF)
    grad_own, par_part = call(
        final_kernel, [((128, 2 * D), BF), chunk], [SM] * 2 + [VM] * 8,
        (side, acts, own.reshape(128, 2176), *parts, result, after(par, space_kept), sums),
        [pltpu.VMEM((16, D), F32), pltpu.VMEM((128, D), BF)],
        flops=10**8, size=2 * 10**6,
    )
    shape = (256, D)
    placed = call(
        place_kernel, [(shape, F32), (shape, F32), (shape, BF), (shape, BF)], [SM] + [VM] * 4,
        (side, *around(grad_own)), [pltpu.VMEM((16, 4, 8, D), F32)] * 2, flops=10**6, size=6 * 10**6,
    )

    total = jnp.concatenate([pair_sum(space_kept, after(space_sent, *parts)), par_part], axis=2)
    total = chip_sum(total)
    grads = lax.psum_scatter(after(grads, grad_space), FRAME, scatter_dimension=0, tiled=True).reshape(2, 32, 3 * D)
    clip = lax.axis_index("clip")
    kept, sent = (lax.dynamic_index_in_dim(grads, i, 0, keepdims=False) for i in (clip, 1 - clip))
    grads = kept.astype(F32) + lax.ppermute(sent, "clip", [(0, 1), (1, 0)]).astype(F32)
    par_total = total[:, D : D + 128]
    par_total = (par_total + core_swap(par_total.astype(BF)).astype(F32)).astype(BF)
    par_total = total_of(around(par_total))
    par_total = jnp.where(core == 0, par_total[:, 0:16], par_total[:, 16:32]).T

    return (
        placed[2].reshape(1, 1, 256, D),
        placed[3].reshape(4, 1, 64, D),
        placed[0].reshape(1, 1, 256, D),
        placed[1].reshape(4, 1, 64, D),
        par_total[0:8],
        par_total[8:11],
        par_total[11:14],
        total[:, 0:768].reshape(32, 3, 256),
        total[:, 768:1024],
        grads[:, 2 * D : 2 * D + 768].reshape(32, 3, 256),
        grads[:, 2 * D + 768 : 3 * D],
        grads[:, 0:D],
        grads[:, D : 2 * D],
    )


def solution(mesh):
    fine = Mesh(mesh.devices.reshape(2, 4, 2, 2, 4), ALL)
    tokens = P("clip", FRAME, None, None)
    columns = P(None, CF)
    square, cube = P(CF, "head"), P(CF, None, "head")
    frames = P("clip", FRAME)
    weights = (cube, square, cube, square, square, square)
    in_specs = (tokens, tokens, frames, frames, tokens, tokens) + (columns,) * 3 + weights
    out_specs = (tokens,) * 4 + (columns,) * 3 + weights
    return jax.shard_map(body, mesh=fine, in_specs=in_specs, out_specs=out_specs, check_vma=False)
```

```python
import functools
import math

import jax
import jax.numpy as jnp
from jax import lax
from jax.experimental import pallas as pl
from jax.experimental.pallas import tpu as pltpu
from jax.sharding import Mesh
from jax.sharding import PartitionSpec as P

BF = jnp.bfloat16
F32 = jnp.float32
EPS = 1e-05
CF = ("clip", "z", "yh", "core")
FRAME = ("z", "yh", "core")
CHIPS = ("clip", "z", "yh")
HF = ("head", "z", "yh", "core")
ALL = ("clip", "z", "yh", "core", "head")
D = 1024
VM = pl.BlockSpec(memory_space=pltpu.VMEM)
SM = pl.BlockSpec(memory_space=pltpu.SMEM)
HB = pl.BlockSpec(memory_space=pltpu.MemorySpace.HBM)
SCALE = 0.125


def mm(a, b):
    return lax.dot_general(a, b, (((1,), (0,)), ((), ())), preferred_element_type=F32)


def mt(a, b):
    return lax.dot_general(a, b, (((1,), (1,)), ((), ())), preferred_element_type=F32)


def tm(a, b):
    return lax.dot_general(a, b, (((0,), (0,)), ((), ())), preferred_element_type=F32)


def call(body, outs, specs, args, scratch=(), flops=0, size=0):
    return pl.pallas_call(
        body,
        out_shape=[jax.ShapeDtypeStruct(s, t) for s, t in outs],
        in_specs=specs,
        out_specs=[VM] * len(outs),
        scratch_shapes=list(scratch),
        compiler_params=pltpu.CompilerParams(vmem_limit_bytes=50 * 2**20),
        cost_estimate=pl.CostEstimate(flops=flops, bytes_accessed=size, transcendentals=0),
    )(*args)


def scaled_of(stream):
    average = jnp.mean(stream, axis=-1, keepdims=True)
    centered = stream - average
    inverse = lax.rsqrt(jnp.mean(centered * centered, axis=-1, keepdims=True) + EPS)
    return centered * inverse, inverse


def norm_back(grad, scaled, inverse, gain):
    grad_scaled = grad * gain
    inner = jnp.mean(grad_scaled, axis=-1, keepdims=True)
    along = jnp.mean(grad_scaled * scaled, axis=-1, keepdims=True)
    return inverse * (grad_scaled - inner - scaled * along)


def lane_half(side):
    lane = lax.broadcasted_iota(jnp.int32, (1, 128), 1)
    return (lane < 64) if side == 0 else (lane >= 64)


def both_heads(block):
    zero = jnp.zeros_like(block)
    return jnp.concatenate([jnp.where(lane_half(0), block, zero), jnp.where(lane_half(1), block, zero)], axis=0)


def own_lanes(double):
    rows = double.shape[0] // 2
    return jnp.where(lane_half(0), double[:rows], double[rows:])


def chances_of(q_both, keys, mask):
    scores = mt(keys, q_both) * SCALE
    if mask is not None:
        scores = jnp.where(mask, scores, -1e30)
    raised = jnp.exp(scores - jnp.max(scores, axis=0, keepdims=True))
    return raised * (1.0 / jnp.sum(raised, axis=0, keepdims=True))


def attend(q2, k2, v2, mask):
    chances = chances_of(both_heads(q2), k2, mask).astype(BF)
    return own_lanes(tm(chances, v2)).astype(BF)


def attend_back(q2, k2, v2, g2, mask):
    q_both, g_both = both_heads(q2), both_heads(g2)
    chances = chances_of(q_both, k2, mask)
    grad_v = mm(chances.astype(BF), g_both)
    grad_chances = mt(v2, g_both)
    weighted = jnp.sum(grad_chances * chances, axis=0, keepdims=True)
    grad_scores = (chances * (grad_chances - weighted)).astype(BF)
    grad_q = own_lanes(tm(grad_scores, k2))
    grad_k = mm(grad_scores, q_both)
    return (grad_q * SCALE).astype(BF), (grad_k * SCALE).astype(BF), grad_v.astype(BF)


def small_mask():
    key = lax.broadcasted_iota(jnp.int32, (256, 512), 0)
    query = lax.broadcasted_iota(jnp.int32, (256, 512), 1) % 256
    return (key // 64) == (query // 64)


def time_mask():
    key = lax.broadcasted_iota(jnp.int32, (128, 256), 0)
    query = lax.broadcasted_iota(jnp.int32, (128, 256), 1) % 128
    return (key <= query) & ((key % 8) == (query % 8))


TURNS = (0, 1, 3, 2)


def load_chips(side, mine, other, dest, sems):
    core = side[0]
    copies = [
        pltpu.make_async_copy(mine, dest.at[:, core], sems.at[0]),
        pltpu.make_async_copy(other, dest.at[:, 1 - core], sems.at[1]),
    ]
    for copy in copies:
        copy.start()
    return copies


def load_turns(big, offset, dest, sems):
    copies = []
    for d in range(4):
        start = 2816 + 512 * d + offset
        copies.append(pltpu.make_async_copy(big.at[:, start : start + 256], dest.at[d], sems.at[d]))
        copies[d].start()
    return copies


def finish(copies):
    for copy in copies:
        copy.wait()


def turned(side, d, sign):
    return lax.rem(side[1] + 4 + sign * d, 4)


def regroup(block):
    width = block.shape[1]
    parts = block.reshape(16, 4, 8, width)
    return [parts[:, g].reshape(128, width) for g in range(4)]


def ungroup(blocks):
    width = blocks[0].shape[1]
    return jnp.stack([block.reshape(16, 8, width) for block in blocks], axis=1).reshape(512, width)


def space_norm(acts, wide, small, par, normed):
    for sub, ref in enumerate((wide, small)):
        for b in range(4):
            action = acts[0] if sub == 0 else acts[1 + b]
            entered = ref[64 * b : 64 * b + 64, :].astype(F32) + par[pl.ds(action, 1), :]
            scaled, _ = scaled_of(entered)
            start = sub * 256 + b * 64
            normed[start : start + 64, :] = (scaled * par[8:9, :] + par[11:12, :]).astype(BF)


def space_kernel(side, acts, wide, small, mine, other, mix, packed, par, normed, weight, sems):
    finish(load_chips(side, mine, other, weight, sems))
    par[...] = weight[:, :, :, 768:896].reshape(D, 128).astype(F32).T[0:16, :]
    space_norm(acts, wide, small, par, normed)
    for sub in range(2):
        rows = normed[sub * 256 : sub * 256 + 256, :]
        for j in range(3):
            columns = weight[:, :, :, j * 256 : j * 256 + 256].reshape(D, 256)
            packed[sub, :, j * 256 : j * 256 + 256] = mm(rows, columns).astype(BF)
        mask = None if sub == 0 else small_mask()
        for p in range(2):
            q2, k2, v2 = (packed[sub, :, j * 256 + p * 128 : j * 256 + p * 128 + 128] for j in range(3))
            mix[sub * 256 : sub * 256 + 256, p * 128 : p * 128 + 128] = attend(q2, k2, v2, mask)


def time_kernel(
    side, s0, s1, s2, s3, mix, par, big,
    after_space, own_after, normed, packed, mixture, own_mix, wso, wtp, sems,
):
    copies = load_turns(big, 0, wso, sems)
    copy = pltpu.make_async_copy(big.at[:, 0:768], wtp, sems.at[4])
    copy.start()
    lane = lax.broadcasted_iota(jnp.int32, (1, 16), 1).astype(F32)
    for d, s in zip(TURNS, (s0, s1, s2, s3)):
        chosen = (s[:, D : D + 1].astype(F32) == lane).astype(BF)
        after_space[turned(side, d, -1)] = s[:, 0:D].astype(F32) + mm(chosen, par[...].astype(BF))
    stepped = 0.0
    for i, d in enumerate(TURNS):
        copies[i].wait()
        stepped = stepped + mt(mix[turned(side, d, -1)], wso[i])
    for g, block in enumerate(regroup(stepped)):
        block = after_space[g] + block
        after_space[g] = block
        scaled, _ = scaled_of(block)
        normed[128 * g : 128 * g + 128, :] = (scaled * par[9:10, :] + par[12:13, :]).astype(BF)
    for g, block in enumerate(regroup(mix[side[1]].astype(F32))):
        own_mix[128 * g : 128 * g + 128, :] = block.astype(BF)
    own_after[...] = after_space[side[1]]
    copy.wait()
    for j in range(3):
        packed[:, j * 256 : j * 256 + 256] = mm(normed[...], wtp[:, j * 256 : j * 256 + 256]).astype(BF)
    mask = time_mask()
    for g in range(4):
        rows = slice(128 * g, 128 * g + 128)
        for p in range(2):
            q2, k2, v2 = (packed[rows, j * 256 + p * 128 : j * 256 + p * 128 + 128] for j in range(3))
            mixture[rows, p * 128 : p * 128 + 128] = attend(q2, k2, v2, mask)


UP = slice(768, 1792)
DOWN = slice(1792, 2816)


def ffn_kernel(
    side, m0, m1, m2, m3, c0, c1, c2, c3, after_space, par, big,
    own_after, normed, cot, hidden, grad_raised, g0, g1, g2, g3, done, grad, wto, we, ws, sems,
):
    copies = load_turns(big, 256, wto, sems)
    more = [
        pltpu.make_async_copy(big.at[:, UP], we, sems.at[4]),
        pltpu.make_async_copy(big.at[:, DOWN], ws, sems.at[5]),
    ]
    for copy in more:
        copy.start()
    for d, c in zip(TURNS, (c0, c1, c2, c3)):
        cot[turned(side, d, -1)] = c[...]
    total = after_space[...].reshape(512, D)
    for i, m in enumerate((m0, m1, m2, m3)):
        copies[i].wait()
        total = total + mt(m[...], wto[i])
    scaled, _ = scaled_of(total)
    done[...] = total.reshape(4, 128, D)
    normed[...] = (scaled * par[10:11, :] + par[13:14, :]).astype(BF)
    own_after[...] = done[side[1]]
    for copy in more:
        copy.wait()
    for c in range(4):
        cols = slice(c * 256, c * 256 + 256)
        raised = mm(normed[...], we[:, cols])
        grad_hidden = mm(cot[...].reshape(512, D), ws[:, cols])
        spread = 0.5 * (1.0 + lax.erf(raised * math.sqrt(0.5)))
        bell = jnp.exp(-0.5 * raised * raised) * (1.0 / math.sqrt(2.0 * math.pi))
        hidden[:, cols] = (raised * spread).astype(BF)
        grad_raised[:, cols] = (grad_hidden * (spread + raised * bell)).astype(BF)
    grad[...] = mt(grad_raised[...], we[...]).astype(BF).reshape(4, 128, D)
    for d, g in zip(TURNS, (g0, g1, g2, g3)):
        g[...] = grad[turned(side, d, 1)]


def ffn_out_kernel(side, hidden, big, o0, o1, o2, o3, out, ws, sems):
    copy = pltpu.make_async_copy(big.at[:, DOWN], ws, sems.at[0])
    copy.start()
    copy.wait()
    out[...] = mt(hidden[...], ws[...]).astype(BF).reshape(4, 128, D)
    for d, o in zip(TURNS, (o0, o1, o2, o3)):
        o[...] = out[turned(side, d, 1)]


def halves(side, block):
    first, second = block[:, 0], block[:, 1]
    low = side[0] == 0
    return jnp.where(low, first, second), jnp.where(low, second, first)


def put_frames(piece, out, start):
    block = piece.astype(BF).reshape(16, 2, 32, piece.shape[1])
    for chip in range(16):
        clip, z, yh = chip // 8, (chip // 2) % 4, chip % 2
        for s in range(2):
            out[z * 4 + yh * 2 + s, clip, :, start : start + piece.shape[1]] = block[chip, s]


def ffn_grad_kernel(normed, cot, hidden, grad_raised, out):
    for c in range(4):
        cols = slice(c * 256, c * 256 + 256)
        put_frames(tm(normed[...], grad_raised[:, cols]), out, c * 256)
        put_frames(tm(cot[...].reshape(512, D), hidden[:, cols]), out, D + c * 256)


def total_of(parts):
    return (parts[0][...].astype(F32) + parts[1][...].astype(F32)) + (parts[2][...].astype(F32) + parts[3][...].astype(F32))


def after_time_kernel(p0, p1, p2, p3, own_after, cot, par, grad_after, branch, sums):
    grad = total_of((p0, p1, p2, p3))
    scaled, inverse = scaled_of(own_after[...])
    sums[...] = jnp.zeros_like(sums)
    sums[10:11, :] = jnp.sum(grad * scaled, axis=0, keepdims=True)
    sums[13:14, :] = jnp.sum(grad, axis=0, keepdims=True)
    total = cot[...].astype(F32) + norm_back(grad, scaled, inverse, par[10:11, :])
    grad_after[...] = total
    branch[...] = total.astype(BF)


def time_back_kernel(
    side, b0, b1, b2, b3, packed, big,
    branches, grad_packed, p0, p1, p2, p3, grad, wto, wtp, sems,
):
    copy_out = pltpu.make_async_copy(big.at[:, 2816 + 256 : 2816 + 512], wto, sems.at[0])
    copy_out.start()
    copy = pltpu.make_async_copy(big.at[:, 0:768], wtp, sems.at[1])
    copy.start()
    copy_out.wait()
    mask = time_mask()
    for d, b in zip(TURNS, (b0, b1, b2, b3)):
        at = turned(side, d, -1)
        branches[at] = b[...]
        grad_mixture = mm(b[...], wto[...]).astype(BF)
        for p in range(2):
            q2, k2, v2 = (packed[at, :, j * 256 + p * 128 : j * 256 + p * 128 + 128] for j in range(3))
            back = attend_back(q2, k2, v2, grad_mixture[:, p * 128 : p * 128 + 128], mask)
            for j in range(3):
                grad_packed[at, :, j * 256 + p * 128 : j * 256 + p * 128 + 128] = back[j]
    copy.wait()
    grad[...] = mt(grad_packed[...].reshape(512, 768), wtp[...]).astype(BF).reshape(4, 128, D)
    for d, p in zip(TURNS, (p0, p1, p2, p3)):
        p[...] = grad[turned(side, d, 1)]


def after_space_kernel(
    side, p0, p1, p2, p3, o0, o1, o2, o3, own_after, own_time, grad_time, par, sums_in, big,
    grad_mix, grad_after, sums, wso, outs, done, sems,
):
    copies = load_turns(big, 0, wso, sems)
    more = [pltpu.make_async_copy(o, outs.at[i], sems.at[4 + i]) for i, o in enumerate((o0, o1, o2, o3))]
    more.append(pltpu.make_async_copy(own_time, done, sems.at[8]))
    for copy in more:
        copy.start()
    grad = total_of((p0, p1, p2, p3))
    scaled, inverse = scaled_of(own_after[...])
    sums[...] = sums_in[...]
    sums[9:10, :] = jnp.sum(grad * scaled, axis=0, keepdims=True)
    sums[12:13, :] = jnp.sum(grad, axis=0, keepdims=True)
    branch = (grad_time[...] + norm_back(grad, scaled, inverse, par[9:10, :])).astype(BF)
    grad_after[...] = branch
    for copy in more:
        copy.wait()
    result = (total_of([outs.at[i] for i in range(4)]) + done[...]).astype(BF)
    for h in range(4):
        grad_mix[h, :, 256:512] = branch[:, h * 256 : h * 256 + 256]
        grad_mix[h, :, 512:768] = result[:, h * 256 : h * 256 + 256]
    for i, d in enumerate(TURNS):
        copies[i].wait()
        grad_mix[turned(side, d, -1), :, 0:256] = mm(branch, wso[i]).astype(BF)


def put_halves(side, pieces, kept, sent):
    for i, piece in enumerate(pieces):
        here, there = halves(side, piece.astype(BF).reshape(16, 2, 32, 256))
        kept[:, :, i * 256 : i * 256 + 256] = here
        sent[:, :, i * 256 : i * 256 + 256] = there


def time_grad_kernel(normed, grad_packed, branches, mixture, grads_in, grads, part, sems):
    for j in range(3):
        put_frames(tm(normed[...], grad_packed[:, j * 256 : j * 256 + 256]), part, j * 256)
    put_frames(tm(branches[...], mixture[...]), part, 768)
    copy = pltpu.make_async_copy(part, grads.at[:, :, :, 2 * D : 3 * D], sems.at[0])
    copy.start()
    copy.wait()


def space_back_kernel(
    side, grad_mix, packed_in, mine, other, grad_packed, result, g0, g1, g2, g3, natural, grad, weight, packed, sems
):
    copy = pltpu.make_async_copy(packed_in, packed, sems.at[2])
    copy.start()
    copies = load_chips(side, mine, other, weight, sems)
    natural[...] = ungroup([grad_mix[g, :, 0:256].astype(F32) for g in range(4)]).astype(BF)
    copy.wait()
    for sub in range(2):
        mask = None if sub == 0 else small_mask()
        for p in range(2):
            q2, k2, v2 = (packed[sub, :, j * 256 + p * 128 : j * 256 + p * 128 + 128] for j in range(3))
            back = attend_back(q2, k2, v2, natural[sub * 256 : sub * 256 + 256, p * 128 : p * 128 + 128], mask)
            for j in range(3):
                grad_packed[sub, :, j * 256 + p * 128 : j * 256 + p * 128 + 128] = back[j]
    finish(copies)
    total = mt(grad_packed[...].reshape(512, 768), weight[:, :, :, 0:768].reshape(D, 768))
    for g, block in enumerate(regroup(total)):
        grad[g] = block.astype(BF)
    for d, ref in zip(TURNS, (g0, g1, g2, g3)):
        at = turned(side, d, 1)
        ref[:, 0:D] = grad[at]
        ref[:, D : D + 256] = grad_mix[at, :, 256:512]
    for g in range(4):
        result[128 * g : 128 * g + 128, :] = grad_mix[g, :, 512:768]


def space_grad_kernel(side, normed, grad_packed, own_mix, s0, s1, s2, s3, kept, sent, spaces):
    for d, s in zip(TURNS, (s0, s1, s2, s3)):
        spaces[turned(side, d, -1)] = s[...]
    pieces = [tm(normed[...], grad_packed[...].reshape(512, 768)[:, j * 256 : j * 256 + 256]) for j in range(3)]
    put_halves(side, pieces + [tm(spaces[...].reshape(512, D), own_mix[...])], kept, sent)


def final_kernel(side, acts, own, p0, p1, p2, p3, result, par, sums_in, grad_out, par_out, sums, after):
    sums[...] = sums_in[...]
    for d, p in zip(TURNS, (p0, p1, p2, p3)):
        after[:, pl.ds(pl.multiple_of(turned(side, d, -1) * 256, 256), 256)] = p[:, D : D + 256]
    spans = [(0, 64, acts[0])] + [(64 + 16 * c, 80 + 16 * c, acts[1 + c]) for c in range(4)]
    for low, high, action in spans:
        rows = slice(low, high)
        entered = own[rows, 0:D].astype(F32) + par[pl.ds(action, 1), :]
        scaled, inverse = scaled_of(entered)
        grad = total_of([p.at[rows, 0:D] for p in (p0, p1, p2, p3)])
        sums[8:9, :] += jnp.sum(grad * scaled, axis=0, keepdims=True)
        sums[11:12, :] += jnp.sum(grad, axis=0, keepdims=True)
        total = after[rows, :].astype(F32) + norm_back(grad, scaled, inverse, par[8:9, :])
        grad_out[rows, 0:D] = total.astype(BF)
        sums[pl.ds(action, 1), :] += jnp.sum(total, axis=0, keepdims=True)
    for g in range(4):
        grad_out[:, D + g * 256 : D + g * 256 + 256] = result[128 * g : 128 * g + 128, :]
    turned_sums = jnp.concatenate([sums[...], jnp.zeros((112, D), F32)], axis=0).T.reshape(16, 2, 32, 128)
    both = jnp.concatenate([turned_sums[:, 0, :, 0:16], turned_sums[:, 1, :, 0:16], turned_sums[:, 0, :, 32:128]], axis=2)
    par_out[...] = both.astype(BF)


def place_kernel(side, b0, b1, b2, b3, grad_wide, grad_small, wide, small, grad, result):
    for d, b in zip(TURNS, (b0, b1, b2, b3)):
        at = turned(side, d, -1)
        cols = pl.ds(pl.multiple_of(at * 256, 256), 256)
        block = b[:, 0:D].astype(F32)
        for f in range(16):
            grad[f, at] = block[8 * f : 8 * f + 8]
        for g in range(4):
            block = b[:, D + g * 256 : D + g * 256 + 256].astype(F32)
            for f in range(16):
                result[f, g, :, cols] = block[8 * f : 8 * f + 8]
    grad_wide[...] = grad[0:8].reshape(256, D)
    grad_small[...] = grad[8:16].reshape(256, D)
    wide[...] = result[0:8].reshape(256, D).astype(BF)
    small[...] = result[8:16].reshape(256, D).astype(BF)


def swap(x, axes):
    return lax.all_to_all(x, axes, split_axis=0, concat_axis=0, tiled=True)


def spread(x, axes, n):
    return swap(jnp.broadcast_to(x[None], (n,) + x.shape), axes)


def shift(x, d):
    return lax.ppermute(x, "head", [(i, (i + d) % 4) for i in range(4)])


def core_swap(x):
    return lax.ppermute(x, "core", [(0, 1), (1, 0)])


def after(x, *others):
    return lax.optimization_barrier((x,) + others)[0]


def around(x):
    return [x] + [shift(x, d) for d in TURNS[1:]]


def body(
    frames_wide, frames_small, actions_wide, actions_small, cotangent_wide, cotangent_small,
    action_table, norm_gains, norm_shifts, space_project, space_output, time_project, time_output,
    expand_weight, shrink_weight,
):
    me = lax.axis_index("head")
    core = lax.axis_index("core")
    side = jnp.stack([core, me]).astype(jnp.int32)
    wide, small = frames_wide.reshape(256, D), frames_small.reshape(256, D)
    acts = jnp.concatenate([actions_wide.reshape(1), actions_small.reshape(4), jnp.zeros((3,), jnp.int32)])

    big = [time_project.reshape(32, 768), expand_weight, shrink_weight]
    big += around(jnp.concatenate([space_output, time_output], axis=1))
    big = lax.all_gather(jnp.concatenate(big, axis=1), CF, axis=0, tiled=True)

    def own_rows(x):
        return lax.dynamic_index_in_dim(x.reshape(8, 4, 8, D), me, 1, keepdims=False)

    marks = jnp.concatenate([jnp.broadcast_to(acts[0:1], (8,)), jnp.repeat(acts[1:5], 2)]).astype(BF)
    marks = jnp.broadcast_to(marks[:, None, None], (16, 8, 128))
    own = jnp.concatenate([own_rows(wide), own_rows(small)])
    own_cot = jnp.concatenate([own_rows(cotangent_wide), own_rows(cotangent_small)])
    own = lax.optimization_barrier(jnp.concatenate([own, marks, own_cot], axis=2))

    small_par = jnp.concatenate([action_table, norm_gains, norm_shifts, jnp.zeros((2, 32), BF)], axis=0).T
    first = jnp.concatenate([space_project.reshape(32, 768), jnp.pad(small_par, ((0, 0), (0, 112)))], axis=1)
    mine = spread(first, CHIPS, 16)
    other = core_swap(mine)
    stream = swap(after(own, mine), FRAME).reshape(128, 2176)
    streams = around(stream[:, 0:1152])
    cots = around(after(stream[:, 1152:2176], *streams))

    def chips(size):
        return pltpu.VMEM((16, 2, 32, size), BF)

    def sems(count):
        return pltpu.SemaphoreType.DMA((count,))

    one, four, all_rows = ((128, D), BF), ((4, 128, D), BF), ((512, D), BF)
    mix_f, packed_f, par, normed_s = call(
        space_kernel, [((512, 256), BF), ((2, 256, 768), BF), ((16, D), F32), all_rows], [SM] * 2 + [VM] * 2 + [HB] * 2,
        (side, acts, wide, small, mine, other), [chips(896), sems(2)],
        flops=2 * 10**9, size=5 * 10**6,
    )
    mix = jnp.broadcast_to(mix_f.reshape(1, 16, 32, 256), (4, 16, 32, 256)).reshape(64, 32, 256)
    mix = swap(after(mix, stream), HF).reshape(4, 512, 256)

    turns = pltpu.VMEM((4, D, 256), BF)
    after_space, own_space, normed_t, packed_t, mixture, own_mix = call(
        time_kernel,
        [((4, 128, D), F32), ((128, D), F32), all_rows, ((512, 768), BF), ((512, 256), BF), ((512, 256), BF)],
        [SM] + [VM] * 6 + [HB], (side, *streams, mix, par, big),
        [turns, pltpu.VMEM((D, 768), BF), sems(5)], flops=3 * 10**9, size=9 * 10**6,
    )
    square = pltpu.VMEM((D, D), BF)
    own_time, normed_ffn, cot, hidden, grad_raised, *parts = call(
        ffn_kernel, [((128, D), F32), all_rows, four, all_rows, all_rows] + [one] * 4, [SM] + [VM] * 10 + [HB],
        (side, *around(after(mixture, *cots)), *cots, after_space, par, big),
        [pltpu.VMEM((4, 128, D), F32), pltpu.VMEM((4, 128, D), BF), turns, square, square, sems(6)],
        flops=5 * 10**9, size=14 * 10**6,
    )

    def send(blocks):
        return [blocks[0]] + [shift(block, d) for block, d in zip(blocks[1:], TURNS[1:])]

    parts = send(parts)
    (ffn_grad,) = call(
        ffn_grad_kernel, [((16, 2, 32, 3 * D), BF)], [VM] * 4, (normed_ffn, cot, hidden, grad_raised),
        flops=2 * 10**9, size=8 * 10**6,
    )
    grad_time, branch, sums = call(
        after_time_kernel, [((128, D), F32), one, ((16, D), F32)], [VM] * 7,
        (*parts, own_time, cots[0], after(par, ffn_grad)), flops=10**8, size=4 * 10**6,
    )
    branch_list = around(branch)
    outs = call(
        ffn_out_kernel, [one] * 4, [SM, VM, HB], (side, after(hidden, grad_time), big),
        [pltpu.VMEM((4, 128, D), BF), square, sems(1)], flops=10**9, size=4 * 10**6,
    )
    branches, grad_packed_t, *parts = call(
        time_back_kernel, [four, ((4, 128, 768), BF)] + [one] * 4, [SM] + [VM] * 5 + [HB],
        (side, *branch_list, after(packed_t, outs[0]).reshape(4, 128, 768), big),
        [pltpu.VMEM((4, 128, D), BF), pltpu.VMEM((D, 256), BF), pltpu.VMEM((D, 768), BF), sems(2)], flops=2 * 10**9, size=8 * 10**6,
    )
    outs = send([outs[0]] + [after(block, *branch_list) for block in outs[1:]])
    grads = pl.pallas_call(
        time_grad_kernel,
        out_shape=jax.ShapeDtypeStruct((16, 2, 32, 3 * D), BF),
        in_specs=[VM] * 4 + [HB],
        out_specs=HB,
        scratch_shapes=[pltpu.VMEM((16, 2, 32, D), BF), sems(1)],
        input_output_aliases={4: 0},
        compiler_params=pltpu.CompilerParams(vmem_limit_bytes=50 * 2**20),
        cost_estimate=pl.CostEstimate(flops=2 * 10**9, bytes_accessed=8 * 10**6, transcendentals=0),
    )(normed_t, grad_packed_t.reshape(512, 768), branches.reshape(512, D), after(mixture, *outs), ffn_grad)
    parts = send([parts[0]] + [after(block, *outs) for block in parts[1:]])
    early = parts[1:]
    grad_mix, grad_space, sums = call(
        after_space_kernel, [((4, 128, 768), BF), one, ((16, D), F32)], [SM] + [VM] * 4 + [HB] * 4 + [VM, HB] + [VM] * 3 + [HB],
        (side, *parts, *outs, own_space, own_time, grad_time, after(par, grads), sums, big),
        [turns, pltpu.VMEM((4, 128, D), BF), pltpu.VMEM((128, D), F32), sems(9)],
        flops=3 * 10**8, size=5 * 10**6,
    )
    grad_mix = swap(grad_mix.reshape(64, 8, 768), HF).reshape(4, 128, 768)
    spaces = around(grad_space)
    def pair_sum(kept, sent):
        return (kept.astype(F32) + core_swap(sent).astype(F32)).astype(BF)

    def chip_sum(x):
        return jnp.sum(swap(x, CHIPS).astype(F32), axis=0)

    grad_packed_f, result, *parts = call(
        space_back_kernel, [((2, 256, 768), BF), ((512, 256), BF)] + [((128, 1280), BF)] * 4, [SM, VM] + [HB] * 3,
        (side, grad_mix, packed_f, mine, other),
        [pltpu.VMEM((512, 256), BF), pltpu.VMEM((4, 128, D), BF), chips(896), pltpu.VMEM((2, 256, 768), BF), sems(3)], flops=2 * 10**9, size=4 * 10**6,
    )
    parts = send(parts)
    space_kept, space_sent = call(
        space_grad_kernel, [((16, 32, D), BF)] * 2, [SM] + [VM] * 7, (side, normed_s, grad_packed_f, own_mix, *spaces),
        [pltpu.VMEM((4, 128, D), BF)], flops=10**9, size=4 * 10**6,
    )
    chunk = ((16, 32, 128), BF)
    grad_own, par_part = call(
        final_kernel, [((128, 2 * D), BF), chunk], [SM] * 2 + [VM] * 8,
        (side, acts, own.reshape(128, 2176), *parts, result, after(par, space_kept), sums),
        [pltpu.VMEM((16, D), F32), pltpu.VMEM((128, D), BF)],
        flops=10**8, size=2 * 10**6,
    )
    shape = (256, D)
    placed = call(
        place_kernel, [(shape, F32), (shape, F32), (shape, BF), (shape, BF)], [SM] + [VM] * 4,
        (side, *around(grad_own)), [pltpu.VMEM((16, 4, 8, D), F32)] * 2, flops=10**6, size=6 * 10**6,
    )

    total = jnp.concatenate([pair_sum(space_kept, after(space_sent, *parts)), par_part], axis=2)
    total = chip_sum(total)
    grads = lax.psum_scatter(after(grads, *early), FRAME, scatter_dimension=0, tiled=True).reshape(2, 32, 3 * D)
    clip = lax.axis_index("clip")
    kept, sent = (lax.dynamic_index_in_dim(grads, i, 0, keepdims=False) for i in (clip, 1 - clip))
    grads = kept.astype(F32) + lax.ppermute(sent, "clip", [(0, 1), (1, 0)]).astype(F32)
    par_total = total[:, D : D + 128]
    par_total = (par_total + core_swap(par_total.astype(BF)).astype(F32)).astype(BF)
    par_total = total_of(around(par_total))
    par_total = jnp.where(core == 0, par_total[:, 0:16], par_total[:, 16:32]).T

    return (
        placed[2].reshape(1, 1, 256, D),
        placed[3].reshape(4, 1, 64, D),
        placed[0].reshape(1, 1, 256, D),
        placed[1].reshape(4, 1, 64, D),
        par_total[0:8],
        par_total[8:11],
        par_total[11:14],
        total[:, 0:768].reshape(32, 3, 256),
        total[:, 768:1024],
        grads[:, 2 * D : 2 * D + 768].reshape(32, 3, 256),
        grads[:, 2 * D + 768 : 3 * D],
        grads[:, 0:D],
        grads[:, D : 2 * D],
    )


def solution(mesh):
    fine = Mesh(mesh.devices.reshape(2, 4, 2, 2, 4), ALL)
    tokens = P("clip", FRAME, None, None)
    columns = P(None, CF)
    square, cube = P(CF, "head"), P(CF, None, "head")
    frames = P("clip", FRAME)
    weights = (cube, square, cube, square, square, square)
    in_specs = (tokens, tokens, frames, frames, tokens, tokens) + (columns,) * 3 + weights
    out_specs = (tokens,) * 4 + (columns,) * 3 + weights
    return jax.shard_map(body, mesh=fine, in_specs=in_specs, out_specs=out_specs, check_vma=False)
```

```python
import functools
import math

import jax
import jax.numpy as jnp
from jax import lax
from jax.experimental import pallas as pl
from jax.experimental.pallas import tpu as pltpu
from jax.sharding import Mesh
from jax.sharding import PartitionSpec as P

BF = jnp.bfloat16
F32 = jnp.float32
EPS = 1e-05
CF = ("clip", "z", "yh", "core")
FRAME = ("z", "yh", "core")
CHIPS = ("clip", "z", "yh")
HF = ("head", "z", "yh", "core")
ALL = ("clip", "z", "yh", "core", "head")
D = 1024
VM = pl.BlockSpec(memory_space=pltpu.VMEM)
SM = pl.BlockSpec(memory_space=pltpu.SMEM)
HB = pl.BlockSpec(memory_space=pltpu.MemorySpace.HBM)
SCALE = 0.125


def mm(a, b):
    return lax.dot_general(a, b, (((1,), (0,)), ((), ())), preferred_element_type=F32)


def mt(a, b):
    return lax.dot_general(a, b, (((1,), (1,)), ((), ())), preferred_element_type=F32)


def tm(a, b):
    return lax.dot_general(a, b, (((0,), (0,)), ((), ())), preferred_element_type=F32)


def call(body, outs, specs, args, scratch=(), flops=0, size=0):
    return pl.pallas_call(
        body,
        out_shape=[jax.ShapeDtypeStruct(s, t) for s, t in outs],
        in_specs=specs,
        out_specs=[VM] * len(outs),
        scratch_shapes=list(scratch),
        compiler_params=pltpu.CompilerParams(vmem_limit_bytes=50 * 2**20),
        cost_estimate=pl.CostEstimate(flops=flops, bytes_accessed=size, transcendentals=0),
    )(*args)


def scaled_of(stream):
    average = jnp.mean(stream, axis=-1, keepdims=True)
    centered = stream - average
    inverse = lax.rsqrt(jnp.mean(centered * centered, axis=-1, keepdims=True) + EPS)
    return centered * inverse, inverse


def norm_back(grad, scaled, inverse, gain):
    grad_scaled = grad * gain
    inner = jnp.mean(grad_scaled, axis=-1, keepdims=True)
    along = jnp.mean(grad_scaled * scaled, axis=-1, keepdims=True)
    return inverse * (grad_scaled - inner - scaled * along)


def lane_half(side):
    lane = lax.broadcasted_iota(jnp.int32, (1, 128), 1)
    return (lane < 64) if side == 0 else (lane >= 64)


def both_heads(block):
    zero = jnp.zeros_like(block)
    return jnp.concatenate([jnp.where(lane_half(0), block, zero), jnp.where(lane_half(1), block, zero)], axis=0)


def own_lanes(double):
    rows = double.shape[0] // 2
    return jnp.where(lane_half(0), double[:rows], double[rows:])


def chances_of(q_both, keys, mask):
    scores = mt(keys, q_both) * SCALE
    if mask is not None:
        scores = jnp.where(mask, scores, -1e30)
    raised = jnp.exp(scores - jnp.max(scores, axis=0, keepdims=True))
    return raised * (1.0 / jnp.sum(raised, axis=0, keepdims=True))


def attend(q2, k2, v2, mask):
    chances = chances_of(both_heads(q2), k2, mask).astype(BF)
    return own_lanes(tm(chances, v2)).astype(BF)


def attend_back(q2, k2, v2, g2, mask):
    q_both, g_both = both_heads(q2), both_heads(g2)
    chances = chances_of(q_both, k2, mask)
    grad_v = mm(chances.astype(BF), g_both)
    grad_chances = mt(v2, g_both)
    weighted = jnp.sum(grad_chances * chances, axis=0, keepdims=True)
    grad_scores = (chances * (grad_chances - weighted)).astype(BF)
    grad_q = own_lanes(tm(grad_scores, k2))
    grad_k = mm(grad_scores, q_both)
    return (grad_q * SCALE).astype(BF), (grad_k * SCALE).astype(BF), grad_v.astype(BF)


def small_mask():
    key = lax.broadcasted_iota(jnp.int32, (256, 512), 0)
    query = lax.broadcasted_iota(jnp.int32, (256, 512), 1) % 256
    return (key // 64) == (query // 64)


def time_mask():
    key = lax.broadcasted_iota(jnp.int32, (128, 256), 0)
    query = lax.broadcasted_iota(jnp.int32, (128, 256), 1) % 128
    return (key <= query) & ((key % 8) == (query % 8))


TURNS = (0, 2, 3, 1)


def load_chips(side, mine, other, dest, sems):
    core = side[0]
    copies = [
        pltpu.make_async_copy(mine, dest.at[:, core], sems.at[0]),
        pltpu.make_async_copy(other, dest.at[:, 1 - core], sems.at[1]),
    ]
    for copy in copies:
        copy.start()
    return copies


def load_turns(big, offset, dest, sems):
    copies = []
    for d in range(4):
        start = 2816 + 512 * d + offset
        copies.append(pltpu.make_async_copy(big.at[:, start : start + 256], dest.at[d], sems.at[d]))
        copies[d].start()
    return copies


def finish(copies):
    for copy in copies:
        copy.wait()


def turned(side, d, sign):
    return lax.rem(side[1] + 4 + sign * d, 4)


def regroup(block):
    width = block.shape[1]
    parts = block.reshape(16, 4, 8, width)
    return [parts[:, g].reshape(128, width) for g in range(4)]


def ungroup(blocks):
    width = blocks[0].shape[1]
    return jnp.stack([block.reshape(16, 8, width) for block in blocks], axis=1).reshape(512, width)


def space_norm(acts, wide, small, par, normed):
    for sub, ref in enumerate((wide, small)):
        for b in range(4):
            action = acts[0] if sub == 0 else acts[1 + b]
            entered = ref[64 * b : 64 * b + 64, :].astype(F32) + par[pl.ds(action, 1), :]
            scaled, _ = scaled_of(entered)
            start = sub * 256 + b * 64
            normed[start : start + 64, :] = (scaled * par[8:9, :] + par[11:12, :]).astype(BF)


def space_kernel(side, acts, wide, small, mine, other, mix, packed, par, normed, weight, sems):
    finish(load_chips(side, mine, other, weight, sems))
    par[...] = weight[:, :, :, 768:896].reshape(D, 128).astype(F32).T[0:16, :]
    space_norm(acts, wide, small, par, normed)
    for sub in range(2):
        rows = normed[sub * 256 : sub * 256 + 256, :]
        for j in range(3):
            columns = weight[:, :, :, j * 256 : j * 256 + 256].reshape(D, 256)
            packed[sub, :, j * 256 : j * 256 + 256] = mm(rows, columns).astype(BF)
        mask = None if sub == 0 else small_mask()
        for p in range(2):
            q2, k2, v2 = (packed[sub, :, j * 256 + p * 128 : j * 256 + p * 128 + 128] for j in range(3))
            mix[sub * 256 : sub * 256 + 256, p * 128 : p * 128 + 128] = attend(q2, k2, v2, mask)


def time_kernel(
    side, s0, s1, s2, s3, mix, par, big,
    after_space, own_after, normed, packed, mixture, own_mix, wso, wtp, sems,
):
    copies = load_turns(big, 0, wso, sems)
    copy = pltpu.make_async_copy(big.at[:, 0:768], wtp, sems.at[4])
    copy.start()
    lane = lax.broadcasted_iota(jnp.int32, (1, 16), 1).astype(F32)
    for d, s in zip(TURNS, (s0, s1, s2, s3)):
        chosen = (s[:, D : D + 1].astype(F32) == lane).astype(BF)
        after_space[turned(side, d, -1)] = s[:, 0:D].astype(F32) + mm(chosen, par[...].astype(BF))
    stepped = 0.0
    for i, d in enumerate(TURNS):
        copies[i].wait()
        stepped = stepped + mt(mix[turned(side, d, -1)], wso[i])
    for g, block in enumerate(regroup(stepped)):
        block = after_space[g] + block
        after_space[g] = block
        scaled, _ = scaled_of(block)
        normed[128 * g : 128 * g + 128, :] = (scaled * par[9:10, :] + par[12:13, :]).astype(BF)
    for g, block in enumerate(regroup(mix[side[1]].astype(F32))):
        own_mix[128 * g : 128 * g + 128, :] = block.astype(BF)
    own_after[...] = after_space[side[1]]
    copy.wait()
    for j in range(3):
        packed[:, j * 256 : j * 256 + 256] = mm(normed[...], wtp[:, j * 256 : j * 256 + 256]).astype(BF)
    mask = time_mask()
    for g in range(4):
        rows = slice(128 * g, 128 * g + 128)
        for p in range(2):
            q2, k2, v2 = (packed[rows, j * 256 + p * 128 : j * 256 + p * 128 + 128] for j in range(3))
            mixture[rows, p * 128 : p * 128 + 128] = attend(q2, k2, v2, mask)


UP = slice(768, 1792)
DOWN = slice(1792, 2816)


def ffn_kernel(
    side, m0, m1, m2, m3, c0, c1, c2, c3, after_space, par, big,
    own_after, normed, cot, hidden, grad_raised, g0, g1, g2, g3, done, grad, wto, we, ws, sems,
):
    copies = load_turns(big, 256, wto, sems)
    more = [
        pltpu.make_async_copy(big.at[:, UP], we, sems.at[4]),
        pltpu.make_async_copy(big.at[:, DOWN], ws, sems.at[5]),
    ]
    for copy in more:
        copy.start()
    for d, c in zip(TURNS, (c0, c1, c2, c3)):
        cot[turned(side, d, -1)] = c[...]
    total = after_space[...].reshape(512, D)
    for i, m in enumerate((m0, m1, m2, m3)):
        copies[i].wait()
        total = total + mt(m[...], wto[i])
    scaled, _ = scaled_of(total)
    done[...] = total.reshape(4, 128, D)
    normed[...] = (scaled * par[10:11, :] + par[13:14, :]).astype(BF)
    own_after[...] = done[side[1]]
    for copy in more:
        copy.wait()
    for c in range(4):
        cols = slice(c * 256, c * 256 + 256)
        raised = mm(normed[...], we[:, cols])
        grad_hidden = mm(cot[...].reshape(512, D), ws[:, cols])
        spread = 0.5 * (1.0 + lax.erf(raised * math.sqrt(0.5)))
        bell = jnp.exp(-0.5 * raised * raised) * (1.0 / math.sqrt(2.0 * math.pi))
        hidden[:, cols] = (raised * spread).astype(BF)
        grad_raised[:, cols] = (grad_hidden * (spread + raised * bell)).astype(BF)
    grad[...] = mt(grad_raised[...], we[...]).astype(BF).reshape(4, 128, D)
    for d, g in zip(TURNS, (g0, g1, g2, g3)):
        g[...] = grad[turned(side, d, 1)]


def ffn_out_kernel(side, hidden, big, o0, o1, o2, o3, out, ws, sems):
    copy = pltpu.make_async_copy(big.at[:, DOWN], ws, sems.at[0])
    copy.start()
    copy.wait()
    out[...] = mt(hidden[...], ws[...]).astype(BF).reshape(4, 128, D)
    for d, o in zip(TURNS, (o0, o1, o2, o3)):
        o[...] = out[turned(side, d, 1)]


def halves(side, block):
    first, second = block[:, 0], block[:, 1]
    low = side[0] == 0
    return jnp.where(low, first, second), jnp.where(low, second, first)


def put_frames(piece, out, start):
    block = piece.astype(BF).reshape(16, 2, 32, piece.shape[1])
    for chip in range(16):
        clip, z, yh = chip // 8, (chip // 2) % 4, chip % 2
        for s in range(2):
            out[z * 2 + s, clip * 2 + yh, :, start : start + piece.shape[1]] = block[chip, s]


def ffn_grad_kernel(normed, cot, hidden, grad_raised, out):
    for c in range(4):
        cols = slice(c * 256, c * 256 + 256)
        put_frames(tm(normed[...], grad_raised[:, cols]), out, c * 256)
        put_frames(tm(cot[...].reshape(512, D), hidden[:, cols]), out, D + c * 256)


def total_of(parts):
    return (parts[0][...].astype(F32) + parts[1][...].astype(F32)) + (parts[2][...].astype(F32) + parts[3][...].astype(F32))


def after_time_kernel(p0, p1, p2, p3, own_after, cot, par, grad_after, branch, sums):
    grad = total_of((p0, p1, p2, p3))
    scaled, inverse = scaled_of(own_after[...])
    sums[...] = jnp.zeros_like(sums)
    sums[10:11, :] = jnp.sum(grad * scaled, axis=0, keepdims=True)
    sums[13:14, :] = jnp.sum(grad, axis=0, keepdims=True)
    total = cot[...].astype(F32) + norm_back(grad, scaled, inverse, par[10:11, :])
    grad_after[...] = total
    branch[...] = total.astype(BF)


def time_back_kernel(
    side, b0, b1, b2, b3, packed, big,
    branches, grad_packed, p0, p1, p2, p3, grad, wto, wtp, sems,
):
    copy_out = pltpu.make_async_copy(big.at[:, 2816 + 256 : 2816 + 512], wto, sems.at[0])
    copy_out.start()
    copy = pltpu.make_async_copy(big.at[:, 0:768], wtp, sems.at[1])
    copy.start()
    copy_out.wait()
    mask = time_mask()
    for d, b in zip(TURNS, (b0, b1, b2, b3)):
        at = turned(side, d, -1)
        branches[at] = b[...]
        grad_mixture = mm(b[...], wto[...]).astype(BF)
        for p in range(2):
            q2, k2, v2 = (packed[at, :, j * 256 + p * 128 : j * 256 + p * 128 + 128] for j in range(3))
            back = attend_back(q2, k2, v2, grad_mixture[:, p * 128 : p * 128 + 128], mask)
            for j in range(3):
                grad_packed[at, :, j * 256 + p * 128 : j * 256 + p * 128 + 128] = back[j]
    copy.wait()
    grad[...] = mt(grad_packed[...].reshape(512, 768), wtp[...]).astype(BF).reshape(4, 128, D)
    for d, p in zip(TURNS, (p0, p1, p2, p3)):
        p[...] = grad[turned(side, d, 1)]


def after_space_kernel(
    side, p0, p1, p2, p3, own_after, grad_time, par, sums_in, big, grad_mix, grad_after, sums, wso, sems,
):
    copies = load_turns(big, 0, wso, sems)
    grad = total_of((p0, p1, p2, p3))
    scaled, inverse = scaled_of(own_after[...])
    sums[...] = sums_in[...]
    sums[9:10, :] = jnp.sum(grad * scaled, axis=0, keepdims=True)
    sums[12:13, :] = jnp.sum(grad, axis=0, keepdims=True)
    branch = (grad_time[...] + norm_back(grad, scaled, inverse, par[9:10, :])).astype(BF)
    grad_after[...] = branch
    for h in range(4):
        grad_mix[h, :, 256:512] = branch[:, h * 256 : h * 256 + 256]
    for i, d in enumerate(TURNS):
        copies[i].wait()
        grad_mix[turned(side, d, -1), :, 0:256] = mm(branch, wso[i]).astype(BF)


def put_halves(side, pieces, kept, sent):
    for i, piece in enumerate(pieces):
        here, there = halves(side, piece.astype(BF).reshape(16, 2, 32, 256))
        kept[:, :, i * 256 : i * 256 + 256] = here
        sent[:, :, i * 256 : i * 256 + 256] = there


def time_grad_kernel(normed, grad_packed, branches, mixture, grads_in, grads, part, sems):
    for j in range(3):
        put_frames(tm(normed[...], grad_packed[:, j * 256 : j * 256 + 256]), part, j * 256)
    put_frames(tm(branches[...], mixture[...]), part, 768)
    copy = pltpu.make_async_copy(part, grads.at[:, :, :, 2 * D : 3 * D], sems.at[0])
    copy.start()
    copy.wait()


def space_back_kernel(
    side, grad_mix, packed_in, mine, other, grad_packed, g0, g1, g2, g3, natural, grad, weight, packed, sems
):
    copy = pltpu.make_async_copy(packed_in, packed, sems.at[2])
    copy.start()
    copies = load_chips(side, mine, other, weight, sems)
    natural[...] = ungroup([grad_mix[g, :, 0:256].astype(F32) for g in range(4)]).astype(BF)
    copy.wait()
    for sub in range(2):
        mask = None if sub == 0 else small_mask()
        for p in range(2):
            q2, k2, v2 = (packed[sub, :, j * 256 + p * 128 : j * 256 + p * 128 + 128] for j in range(3))
            back = attend_back(q2, k2, v2, natural[sub * 256 : sub * 256 + 256, p * 128 : p * 128 + 128], mask)
            for j in range(3):
                grad_packed[sub, :, j * 256 + p * 128 : j * 256 + p * 128 + 128] = back[j]
    finish(copies)
    total = mt(grad_packed[...].reshape(512, 768), weight[:, :, :, 0:768].reshape(D, 768))
    for g, block in enumerate(regroup(total)):
        grad[g] = block.astype(BF)
    for d, ref in zip(TURNS, (g0, g1, g2, g3)):
        at = turned(side, d, 1)
        ref[:, 0:D] = grad[at]
        ref[:, D : D + 256] = grad_mix[at, :, 256:512]


def space_grad_kernel(side, normed, grad_packed, own_mix, s0, s1, s2, s3, kept, sent, spaces):
    for d, s in zip(TURNS, (s0, s1, s2, s3)):
        spaces[turned(side, d, -1)] = s[...]
    pieces = [tm(normed[...], grad_packed[...].reshape(512, 768)[:, j * 256 : j * 256 + 256]) for j in range(3)]
    put_halves(side, pieces + [tm(spaces[...].reshape(512, D), own_mix[...])], kept, sent)


def final_kernel(side, acts, own, p0, p1, p2, p3, result, par, sums_in, grad_out, par_out, sums, after):
    sums[...] = sums_in[...]
    for d, p in zip(TURNS, (p0, p1, p2, p3)):
        after[:, pl.ds(pl.multiple_of(turned(side, d, -1) * 256, 256), 256)] = p[:, D : D + 256]
    spans = [(0, 64, acts[0])] + [(64 + 16 * c, 80 + 16 * c, acts[1 + c]) for c in range(4)]
    for low, high, action in spans:
        rows = slice(low, high)
        entered = own[rows, 0:D].astype(F32) + par[pl.ds(action, 1), :]
        scaled, inverse = scaled_of(entered)
        grad = total_of([p.at[rows, 0:D] for p in (p0, p1, p2, p3)])
        sums[8:9, :] += jnp.sum(grad * scaled, axis=0, keepdims=True)
        sums[11:12, :] += jnp.sum(grad, axis=0, keepdims=True)
        total = after[rows, :].astype(F32) + norm_back(grad, scaled, inverse, par[8:9, :])
        grad_out[rows, 0:D] = total.astype(BF)
        sums[pl.ds(action, 1), :] += jnp.sum(total, axis=0, keepdims=True)
    grad_out[:, D : 2 * D] = result[...]
    turned_sums = jnp.concatenate([sums[...], jnp.zeros((112, D), F32)], axis=0).T.reshape(16, 2, 32, 128)
    both = jnp.concatenate([turned_sums[:, 0, :, 0:16], turned_sums[:, 1, :, 0:16], turned_sums[:, 0, :, 32:128]], axis=2)
    par_out[...] = both.astype(BF)


def place_kernel(side, b0, b1, b2, b3, grad_wide, grad_small, wide, small, grad, result):
    for d, b in zip(TURNS, (b0, b1, b2, b3)):
        at = turned(side, d, -1)
        for start, dest in ((0, grad), (D, result)):
            block = b[:, start : start + D].astype(F32)
            for f in range(16):
                dest[f, at] = block[8 * f : 8 * f + 8]
    grad_wide[...] = grad[0:8].reshape(256, D)
    grad_small[...] = grad[8:16].reshape(256, D)
    wide[...] = result[0:8].reshape(256, D).astype(BF)
    small[...] = result[8:16].reshape(256, D).astype(BF)


def swap(x, axes):
    return lax.all_to_all(x, axes, split_axis=0, concat_axis=0, tiled=True)


def spread(x, axes, n):
    return swap(jnp.broadcast_to(x[None], (n,) + x.shape), axes)


def shift(x, d):
    return lax.ppermute(x, "head", [(i, (i + d) % 4) for i in range(4)])


def core_swap(x):
    return lax.ppermute(x, "core", [(0, 1), (1, 0)])


def after(x, *others):
    return lax.optimization_barrier((x,) + others)[0]


def around(x):
    return [x] + [shift(x, d) for d in TURNS[1:]]


def body(
    frames_wide, frames_small, actions_wide, actions_small, cotangent_wide, cotangent_small,
    action_table, norm_gains, norm_shifts, space_project, space_output, time_project, time_output,
    expand_weight, shrink_weight,
):
    me = lax.axis_index("head")
    core = lax.axis_index("core")
    side = jnp.stack([core, me]).astype(jnp.int32)
    wide, small = frames_wide.reshape(256, D), frames_small.reshape(256, D)
    acts = jnp.concatenate([actions_wide.reshape(1), actions_small.reshape(4), jnp.zeros((3,), jnp.int32)])

    big = [time_project.reshape(32, 768), expand_weight, shrink_weight]
    big += around(jnp.concatenate([space_output, time_output], axis=1))
    big = lax.all_gather(jnp.concatenate(big, axis=1), CF, axis=0, tiled=True)

    def own_rows(x):
        return lax.dynamic_index_in_dim(x.reshape(8, 4, 8, D), me, 1, keepdims=False)

    marks = jnp.concatenate([jnp.broadcast_to(acts[0:1], (8,)), jnp.repeat(acts[1:5], 2)]).astype(BF)
    marks = jnp.broadcast_to(marks[:, None, None], (16, 8, 128))
    own = jnp.concatenate([own_rows(wide), own_rows(small)])
    own_cot = jnp.concatenate([own_rows(cotangent_wide), own_rows(cotangent_small)])
    own = lax.optimization_barrier(jnp.concatenate([own, marks, own_cot], axis=2))

    small_par = jnp.concatenate([action_table, norm_gains, norm_shifts, jnp.zeros((2, 32), BF)], axis=0).T
    first = jnp.concatenate([space_project.reshape(32, 768), jnp.pad(small_par, ((0, 0), (0, 112)))], axis=1)
    mine = spread(first, CHIPS, 16)
    other = core_swap(mine)
    stream = swap(after(own, mine), FRAME).reshape(128, 2176)
    streams = around(stream[:, 0:1152])
    cots = around(after(stream[:, 1152:2176], *streams))

    def chips(size):
        return pltpu.VMEM((16, 2, 32, size), BF)

    def sems(count):
        return pltpu.SemaphoreType.DMA((count,))

    one, four, all_rows = ((128, D), BF), ((4, 128, D), BF), ((512, D), BF)
    mix_f, packed_f, par, normed_s = call(
        space_kernel, [((512, 256), BF), ((2, 256, 768), BF), ((16, D), F32), all_rows], [SM] * 2 + [VM] * 2 + [HB] * 2,
        (side, acts, wide, small, mine, other), [chips(896), sems(2)],
        flops=2 * 10**9, size=5 * 10**6,
    )
    mix = jnp.broadcast_to(mix_f.reshape(1, 16, 32, 256), (4, 16, 32, 256)).reshape(64, 32, 256)
    mix = swap(after(mix, stream), HF).reshape(4, 512, 256)

    turns = pltpu.VMEM((4, D, 256), BF)
    after_space, own_space, normed_t, packed_t, mixture, own_mix = call(
        time_kernel,
        [((4, 128, D), F32), ((128, D), F32), all_rows, ((512, 768), BF), ((512, 256), BF), ((512, 256), BF)],
        [SM] + [VM] * 6 + [HB], (side, *streams, mix, par, big),
        [turns, pltpu.VMEM((D, 768), BF), sems(5)], flops=3 * 10**9, size=9 * 10**6,
    )
    square = pltpu.VMEM((D, D), BF)
    own_time, normed_ffn, cot, hidden, grad_raised, *parts = call(
        ffn_kernel, [((128, D), F32), all_rows, four, all_rows, all_rows] + [one] * 4, [SM] + [VM] * 10 + [HB],
        (side, *around(after(mixture, *cots)), *cots, after_space, par, big),
        [pltpu.VMEM((4, 128, D), F32), pltpu.VMEM((4, 128, D), BF), turns, square, square, sems(6)],
        flops=5 * 10**9, size=14 * 10**6,
    )

    def send(blocks):
        return [blocks[0]] + [shift(block, d) for block, d in zip(blocks[1:], TURNS[1:])]

    parts = send(parts)
    (ffn_grad,) = call(
        ffn_grad_kernel, [((8, 4, 32, 3 * D), BF)], [VM] * 4, (normed_ffn, cot, hidden, grad_raised),
        flops=2 * 10**9, size=8 * 10**6,
    )
    grad_time, branch, sums = call(
        after_time_kernel, [((128, D), F32), one, ((16, D), F32)], [VM] * 7,
        (*parts, own_time, cots[0], after(par, ffn_grad)), flops=10**8, size=4 * 10**6,
    )
    branch_list = around(branch)
    outs = call(
        ffn_out_kernel, [one] * 4, [SM, VM, HB], (side, after(hidden, grad_time), big),
        [pltpu.VMEM((4, 128, D), BF), square, sems(1)], flops=10**9, size=4 * 10**6,
    )
    branches, grad_packed_t, *parts = call(
        time_back_kernel, [four, ((4, 128, 768), BF)] + [one] * 4, [SM] + [VM] * 5 + [HB],
        (side, *branch_list, after(packed_t, outs[0]).reshape(4, 128, 768), big),
        [pltpu.VMEM((4, 128, D), BF), pltpu.VMEM((D, 256), BF), pltpu.VMEM((D, 768), BF), sems(2)], flops=2 * 10**9, size=8 * 10**6,
    )
    grads = pl.pallas_call(
        time_grad_kernel,
        out_shape=jax.ShapeDtypeStruct((8, 4, 32, 3 * D), BF),
        in_specs=[VM] * 4 + [HB],
        out_specs=HB,
        scratch_shapes=[pltpu.VMEM((8, 4, 32, D), BF), sems(1)],
        input_output_aliases={4: 0},
        compiler_params=pltpu.CompilerParams(vmem_limit_bytes=50 * 2**20),
        cost_estimate=pl.CostEstimate(flops=2 * 10**9, bytes_accessed=8 * 10**6, transcendentals=0),
    )(normed_t, grad_packed_t.reshape(512, 768), branches.reshape(512, D), mixture, ffn_grad)
    parts = send(parts)
    early = parts[1:]
    grad_mix, grad_space, sums = call(
        after_space_kernel, [((4, 128, 512), BF), one, ((16, D), F32)], [SM] + [VM] * 8 + [HB],
        (side, *parts, own_space, grad_time, after(par, grads), sums, big),
        [turns, sems(4)],
        flops=3 * 10**8, size=5 * 10**6,
    )
    grad_mix = swap(grad_mix.reshape(64, 8, 512), HF).reshape(4, 128, 512)
    spaces = around(grad_space)
    outs = send([outs[0]] + [after(block, grad_space) for block in outs[1:]])
    result = (total_of(outs) + own_time).astype(BF)
    packed_f = after(packed_f, result)
    result = swap(after(result, grad_mix).reshape(16, 8, D), FRAME).reshape(128, D)
    def pair_sum(kept, sent):
        return (kept.astype(F32) + core_swap(sent).astype(F32)).astype(BF)

    def chip_sum(x):
        return jnp.sum(swap(x, CHIPS).astype(F32), axis=0)

    grad_packed_f, *parts = call(
        space_back_kernel, [((2, 256, 768), BF)] + [((128, 1280), BF)] * 4, [SM, VM] + [HB] * 3,
        (side, grad_mix, packed_f, mine, other),
        [pltpu.VMEM((512, 256), BF), pltpu.VMEM((4, 128, D), BF), chips(896), pltpu.VMEM((2, 256, 768), BF), sems(3)], flops=2 * 10**9, size=4 * 10**6,
    )
    parts = send(parts)
    space_kept, space_sent = call(
        space_grad_kernel, [((16, 32, D), BF)] * 2, [SM] + [VM] * 7, (side, normed_s, grad_packed_f, after(own_mix, result), *spaces),
        [pltpu.VMEM((4, 128, D), BF)], flops=10**9, size=4 * 10**6,
    )
    chunk = ((16, 32, 128), BF)
    grad_own, par_part = call(
        final_kernel, [((128, 2 * D), BF), chunk], [SM] * 2 + [VM] * 8,
        (side, acts, own.reshape(128, 2176), *parts, result, after(par, space_kept), sums),
        [pltpu.VMEM((16, D), F32), pltpu.VMEM((128, D), BF)],
        flops=10**8, size=2 * 10**6,
    )
    shape = (256, D)
    placed = call(
        place_kernel, [(shape, F32), (shape, F32), (shape, BF), (shape, BF)], [SM] + [VM] * 4,
        (side, *around(grad_own)), [pltpu.VMEM((16, 4, 8, D), F32)] * 2, flops=10**6, size=6 * 10**6,
    )

    total = jnp.concatenate([pair_sum(space_kept, after(space_sent, *parts)), par_part], axis=2)
    total = chip_sum(total)
    grads = lax.psum_scatter(after(grads, *early), ("z", "core"), scatter_dimension=0, tiled=True).reshape(4, 32, 3 * D)
    grads = lax.psum_scatter(after(grads, space_kept), ("clip", "yh"), scatter_dimension=0, tiled=True)
    grads = grads.reshape(32, 3 * D).astype(F32)
    par_total = total[:, D : D + 128]
    par_total = (par_total + core_swap(par_total.astype(BF)).astype(F32)).astype(BF)
    par_total = total_of(around(par_total))
    par_total = jnp.where(core == 0, par_total[:, 0:16], par_total[:, 16:32]).T

    return (
        placed[2].reshape(1, 1, 256, D),
        placed[3].reshape(4, 1, 64, D),
        placed[0].reshape(1, 1, 256, D),
        placed[1].reshape(4, 1, 64, D),
        par_total[0:8],
        par_total[8:11],
        par_total[11:14],
        total[:, 0:768].reshape(32, 3, 256),
        total[:, 768:1024],
        grads[:, 2 * D : 2 * D + 768].reshape(32, 3, 256),
        grads[:, 2 * D + 768 : 3 * D],
        grads[:, 0:D],
        grads[:, D : 2 * D],
    )


def solution(mesh):
    fine = Mesh(mesh.devices.reshape(2, 4, 2, 2, 4), ALL)
    tokens = P("clip", FRAME, None, None)
    columns = P(None, CF)
    square, cube = P(CF, "head"), P(CF, None, "head")
    frames = P("clip", FRAME)
    weights = (cube, square, cube, square, square, square)
    in_specs = (tokens, tokens, frames, frames, tokens, tokens) + (columns,) * 3 + weights
    out_specs = (tokens,) * 4 + (columns,) * 3 + weights
    return jax.shard_map(body, mesh=fine, in_specs=in_specs, out_specs=out_specs, check_vma=False)
```

```python
import functools
import math

import jax
import jax.numpy as jnp
from jax import lax
from jax.experimental import pallas as pl
from jax.experimental.pallas import tpu as pltpu
from jax.sharding import Mesh
from jax.sharding import PartitionSpec as P

BF = jnp.bfloat16
F32 = jnp.float32
EPS = 1e-05
CF = ("clip", "z", "yh", "core")
FRAME = ("z", "yh", "core")
CHIPS = ("clip", "z", "yh")
HF = ("head", "z", "yh", "core")
ALL = ("clip", "z", "yh", "core", "head")
D = 1024
VM = pl.BlockSpec(memory_space=pltpu.VMEM)
SM = pl.BlockSpec(memory_space=pltpu.SMEM)
HB = pl.BlockSpec(memory_space=pltpu.MemorySpace.HBM)
SCALE = 0.125


def mm(a, b):
    return lax.dot_general(a, b, (((1,), (0,)), ((), ())), preferred_element_type=F32)


def mt(a, b):
    return lax.dot_general(a, b, (((1,), (1,)), ((), ())), preferred_element_type=F32)


def tm(a, b):
    return lax.dot_general(a, b, (((0,), (0,)), ((), ())), preferred_element_type=F32)


def call(body, outs, specs, args, scratch=(), flops=0, size=0):
    return pl.pallas_call(
        body,
        out_shape=[jax.ShapeDtypeStruct(s, t) for s, t in outs],
        in_specs=specs,
        out_specs=[VM] * len(outs),
        scratch_shapes=list(scratch),
        compiler_params=pltpu.CompilerParams(vmem_limit_bytes=50 * 2**20),
        cost_estimate=pl.CostEstimate(flops=flops, bytes_accessed=size, transcendentals=0),
    )(*args)


def scaled_of(stream):
    average = jnp.mean(stream, axis=-1, keepdims=True)
    centered = stream - average
    inverse = lax.rsqrt(jnp.mean(centered * centered, axis=-1, keepdims=True) + EPS)
    return centered * inverse, inverse


def norm_back(grad, scaled, inverse, gain):
    grad_scaled = grad * gain
    inner = jnp.mean(grad_scaled, axis=-1, keepdims=True)
    along = jnp.mean(grad_scaled * scaled, axis=-1, keepdims=True)
    return inverse * (grad_scaled - inner - scaled * along)


def lane_half(side):
    lane = lax.broadcasted_iota(jnp.int32, (1, 128), 1)
    return (lane < 64) if side == 0 else (lane >= 64)


def both_heads(block):
    zero = jnp.zeros_like(block)
    return jnp.concatenate([jnp.where(lane_half(0), block, zero), jnp.where(lane_half(1), block, zero)], axis=0)


def own_lanes(double):
    rows = double.shape[0] // 2
    return jnp.where(lane_half(0), double[:rows], double[rows:])


def chances_of(q_both, keys, mask):
    scores = mt(keys, q_both) * SCALE
    if mask is not None:
        scores = jnp.where(mask, scores, -1e30)
    raised = jnp.exp(scores - jnp.max(scores, axis=0, keepdims=True))
    return raised * (1.0 / jnp.sum(raised, axis=0, keepdims=True))


def attend(q2, k2, v2, mask):
    chances = chances_of(both_heads(q2), k2, mask).astype(BF)
    return own_lanes(tm(chances, v2)).astype(BF)


def attend_back(q2, k2, v2, g2, mask):
    q_both, g_both = both_heads(q2), both_heads(g2)
    chances = chances_of(q_both, k2, mask)
    grad_v = mm(chances.astype(BF), g_both)
    grad_chances = mt(v2, g_both)
    weighted = jnp.sum(grad_chances * chances, axis=0, keepdims=True)
    grad_scores = (chances * (grad_chances - weighted)).astype(BF)
    grad_q = own_lanes(tm(grad_scores, k2))
    grad_k = mm(grad_scores, q_both)
    return (grad_q * SCALE).astype(BF), (grad_k * SCALE).astype(BF), grad_v.astype(BF)


def small_mask():
    key = lax.broadcasted_iota(jnp.int32, (256, 512), 0)
    query = lax.broadcasted_iota(jnp.int32, (256, 512), 1) % 256
    return (key // 64) == (query // 64)


def time_mask():
    key = lax.broadcasted_iota(jnp.int32, (128, 256), 0)
    query = lax.broadcasted_iota(jnp.int32, (128, 256), 1) % 128
    return (key <= query) & ((key % 8) == (query % 8))


TURNS = (0, 2, 3, 1)


def load_chips(side, mine, other, dest, sems):
    core = side[0]
    copies = [
        pltpu.make_async_copy(mine, dest.at[:, core], sems.at[0]),
        pltpu.make_async_copy(other, dest.at[:, 1 - core], sems.at[1]),
    ]
    for copy in copies:
        copy.start()
    return copies


def load_turns(big, offset, dest, sems):
    copies = []
    for d in range(4):
        start = 2816 + 512 * d + offset
        copies.append(pltpu.make_async_copy(big.at[:, start : start + 256], dest.at[d], sems.at[d]))
        copies[d].start()
    return copies


def finish(copies):
    for copy in copies:
        copy.wait()


def turned(side, d, sign):
    return lax.rem(side[1] + 4 + sign * d, 4)


def regroup(block):
    width = block.shape[1]
    parts = block.reshape(16, 4, 8, width)
    return [parts[:, g].reshape(128, width) for g in range(4)]


def ungroup(blocks):
    width = blocks[0].shape[1]
    return jnp.stack([block.reshape(16, 8, width) for block in blocks], axis=1).reshape(512, width)


def space_norm(acts, wide, small, par, normed):
    for sub, ref in enumerate((wide, small)):
        for b in range(4):
            action = acts[0] if sub == 0 else acts[1 + b]
            entered = ref[64 * b : 64 * b + 64, :].astype(F32) + par[pl.ds(action, 1), :]
            scaled, _ = scaled_of(entered)
            start = sub * 256 + b * 64
            normed[start : start + 64, :] = (scaled * par[8:9, :] + par[11:12, :]).astype(BF)


def space_kernel(side, acts, wide, small, mine, other, mix, packed, par, normed, weight, sems):
    finish(load_chips(side, mine, other, weight, sems))
    par[...] = weight[:, :, :, 768:896].reshape(D, 128).astype(F32).T[0:16, :]
    space_norm(acts, wide, small, par, normed)
    for sub in range(2):
        rows = normed[sub * 256 : sub * 256 + 256, :]
        for j in range(3):
            columns = weight[:, :, :, j * 256 : j * 256 + 256].reshape(D, 256)
            packed[sub, :, j * 256 : j * 256 + 256] = mm(rows, columns).astype(BF)
        mask = None if sub == 0 else small_mask()
        for p in range(2):
            q2, k2, v2 = (packed[sub, :, j * 256 + p * 128 : j * 256 + p * 128 + 128] for j in range(3))
            mix[sub * 256 : sub * 256 + 256, p * 128 : p * 128 + 128] = attend(q2, k2, v2, mask)


def time_kernel(
    side, s0, s1, s2, s3, mix, par, big,
    after_space, own_after, normed, packed, mixture, own_mix, wso, wtp, sems,
):
    copies = load_turns(big, 0, wso, sems)
    copy = pltpu.make_async_copy(big.at[:, 0:768], wtp, sems.at[4])
    copy.start()
    lane = lax.broadcasted_iota(jnp.int32, (1, 16), 1).astype(F32)
    for d, s in zip(TURNS, (s0, s1, s2, s3)):
        chosen = (s[:, D : D + 1].astype(F32) == lane).astype(BF)
        after_space[turned(side, d, -1)] = s[:, 0:D].astype(F32) + mm(chosen, par[...].astype(BF))
    stepped = 0.0
    for i, d in enumerate(TURNS):
        copies[i].wait()
        stepped = stepped + mt(mix[turned(side, d, -1)], wso[i])
    for g, block in enumerate(regroup(stepped)):
        block = after_space[g] + block
        after_space[g] = block
        scaled, _ = scaled_of(block)
        normed[128 * g : 128 * g + 128, :] = (scaled * par[9:10, :] + par[12:13, :]).astype(BF)
    for g, block in enumerate(regroup(mix[side[1]].astype(F32))):
        own_mix[128 * g : 128 * g + 128, :] = block.astype(BF)
    own_after[...] = after_space[side[1]]
    copy.wait()
    for j in range(3):
        packed[:, j * 256 : j * 256 + 256] = mm(normed[...], wtp[:, j * 256 : j * 256 + 256]).astype(BF)
    mask = time_mask()
    for g in range(4):
        rows = slice(128 * g, 128 * g + 128)
        for p in range(2):
            q2, k2, v2 = (packed[rows, j * 256 + p * 128 : j * 256 + p * 128 + 128] for j in range(3))
            mixture[rows, p * 128 : p * 128 + 128] = attend(q2, k2, v2, mask)


UP = slice(768, 1792)
DOWN = slice(1792, 2816)


def ffn_kernel(
    side, m0, m1, m2, m3, c0, c1, c2, c3, after_space, par, big,
    own_after, normed, cot, hidden, grad_raised, g0, g1, g2, g3, done, grad, wto, we, ws, sems,
):
    copies = load_turns(big, 256, wto, sems)
    more = [
        pltpu.make_async_copy(big.at[:, UP], we, sems.at[4]),
        pltpu.make_async_copy(big.at[:, DOWN], ws, sems.at[5]),
    ]
    for copy in more:
        copy.start()
    for d, c in zip(TURNS, (c0, c1, c2, c3)):
        cot[turned(side, d, -1)] = c[...]
    total = after_space[...].reshape(512, D)
    for i, m in enumerate((m0, m1, m2, m3)):
        copies[i].wait()
        total = total + mt(m[...], wto[i])
    scaled, _ = scaled_of(total)
    done[...] = total.reshape(4, 128, D)
    normed[...] = (scaled * par[10:11, :] + par[13:14, :]).astype(BF)
    own_after[...] = done[side[1]]
    for copy in more:
        copy.wait()
    for c in range(4):
        cols = slice(c * 256, c * 256 + 256)
        raised = mm(normed[...], we[:, cols])
        grad_hidden = mm(cot[...].reshape(512, D), ws[:, cols])
        spread = 0.5 * (1.0 + lax.erf(raised * math.sqrt(0.5)))
        bell = jnp.exp(-0.5 * raised * raised) * (1.0 / math.sqrt(2.0 * math.pi))
        hidden[:, cols] = (raised * spread).astype(BF)
        grad_raised[:, cols] = (grad_hidden * (spread + raised * bell)).astype(BF)
    grad[...] = mt(grad_raised[...], we[...]).astype(BF).reshape(4, 128, D)
    for d, g in zip(TURNS, (g0, g1, g2, g3)):
        g[...] = grad[turned(side, d, 1)]


def ffn_out_kernel(side, hidden, big, o0, o1, o2, o3, out, ws, sems):
    copy = pltpu.make_async_copy(big.at[:, DOWN], ws, sems.at[0])
    copy.start()
    copy.wait()
    out[...] = mt(hidden[...], ws[...]).astype(BF).reshape(4, 128, D)
    for d, o in zip(TURNS, (o0, o1, o2, o3)):
        o[...] = out[turned(side, d, 1)]


def halves(side, block):
    first, second = block[:, 0], block[:, 1]
    low = side[0] == 0
    return jnp.where(low, first, second), jnp.where(low, second, first)


def put_frames(piece, out, start):
    block = piece.astype(BF).reshape(16, 2, 32, piece.shape[1])
    for chip in range(16):
        clip, z, yh = chip // 8, (chip // 2) % 4, chip % 2
        for s in range(2):
            out[z * 2 + s, clip * 2 + yh, :, start : start + piece.shape[1]] = block[chip, s]


def ffn_grad_kernel(normed, cot, hidden, grad_raised, out):
    for c in range(4):
        cols = slice(c * 256, c * 256 + 256)
        put_frames(tm(normed[...], grad_raised[:, cols]), out, c * 256)
        put_frames(tm(cot[...].reshape(512, D), hidden[:, cols]), out, D + c * 256)


def total_of(parts):
    return (parts[0][...].astype(F32) + parts[1][...].astype(F32)) + (parts[2][...].astype(F32) + parts[3][...].astype(F32))


def after_time_kernel(p0, p1, p2, p3, own_after, cot, par, grad_after, branch, sums):
    grad = total_of((p0, p1, p2, p3))
    scaled, inverse = scaled_of(own_after[...])
    sums[...] = jnp.zeros_like(sums)
    sums[10:11, :] = jnp.sum(grad * scaled, axis=0, keepdims=True)
    sums[13:14, :] = jnp.sum(grad, axis=0, keepdims=True)
    total = cot[...].astype(F32) + norm_back(grad, scaled, inverse, par[10:11, :])
    grad_after[...] = total
    branch[...] = total.astype(BF)


def time_back_kernel(
    side, b0, b1, b2, b3, packed, big,
    branches, grad_packed, p0, p1, p2, p3, grad, wto, wtp, sems,
):
    copy_out = pltpu.make_async_copy(big.at[:, 2816 + 256 : 2816 + 512], wto, sems.at[0])
    copy_out.start()
    copy = pltpu.make_async_copy(big.at[:, 0:768], wtp, sems.at[1])
    copy.start()
    copy_out.wait()
    mask = time_mask()
    for d, b in zip(TURNS, (b0, b1, b2, b3)):
        at = turned(side, d, -1)
        branches[at] = b[...]
        grad_mixture = mm(b[...], wto[...]).astype(BF)
        for p in range(2):
            q2, k2, v2 = (packed[at, :, j * 256 + p * 128 : j * 256 + p * 128 + 128] for j in range(3))
            back = attend_back(q2, k2, v2, grad_mixture[:, p * 128 : p * 128 + 128], mask)
            for j in range(3):
                grad_packed[at, :, j * 256 + p * 128 : j * 256 + p * 128 + 128] = back[j]
    copy.wait()
    grad[...] = mt(grad_packed[...].reshape(512, 768), wtp[...]).astype(BF).reshape(4, 128, D)
    for d, p in zip(TURNS, (p0, p1, p2, p3)):
        p[...] = grad[turned(side, d, 1)]


def after_space_kernel(
    side, p0, p1, p2, p3, own_after, grad_time, par, sums_in, big, grad_mix, grad_after, sums, wso, sems,
):
    copies = load_turns(big, 0, wso, sems)
    grad = total_of((p0, p1, p2, p3))
    scaled, inverse = scaled_of(own_after[...])
    sums[...] = sums_in[...]
    sums[9:10, :] = jnp.sum(grad * scaled, axis=0, keepdims=True)
    sums[12:13, :] = jnp.sum(grad, axis=0, keepdims=True)
    branch = (grad_time[...] + norm_back(grad, scaled, inverse, par[9:10, :])).astype(BF)
    grad_after[...] = branch
    for h in range(4):
        grad_mix[h, :, 256:512] = branch[:, h * 256 : h * 256 + 256]
    for i, d in enumerate(TURNS):
        copies[i].wait()
        grad_mix[turned(side, d, -1), :, 0:256] = mm(branch, wso[i]).astype(BF)


def put_halves(side, pieces, kept, sent):
    for i, piece in enumerate(pieces):
        here, there = halves(side, piece.astype(BF).reshape(16, 2, 32, 256))
        kept[:, :, i * 256 : i * 256 + 256] = here
        sent[:, :, i * 256 : i * 256 + 256] = there


def time_grad_kernel(normed, grad_packed, branches, mixture, grads_in, grads, part, sems):
    for j in range(3):
        put_frames(tm(normed[...], grad_packed[:, j * 256 : j * 256 + 256]), part, j * 256)
    put_frames(tm(branches[...], mixture[...]), part, 768)
    copy = pltpu.make_async_copy(part, grads.at[:, :, :, 2 * D : 3 * D], sems.at[0])
    copy.start()
    copy.wait()


def space_back_kernel(
    side, grad_mix, packed_in, mine, other, grad_packed, g0, g1, g2, g3, natural, grad, weight, packed, sems
):
    copy = pltpu.make_async_copy(packed_in, packed, sems.at[2])
    copy.start()
    copies = load_chips(side, mine, other, weight, sems)
    natural[...] = ungroup([grad_mix[g, :, 0:256].astype(F32) for g in range(4)]).astype(BF)
    copy.wait()
    for sub in range(2):
        mask = None if sub == 0 else small_mask()
        for p in range(2):
            q2, k2, v2 = (packed[sub, :, j * 256 + p * 128 : j * 256 + p * 128 + 128] for j in range(3))
            back = attend_back(q2, k2, v2, natural[sub * 256 : sub * 256 + 256, p * 128 : p * 128 + 128], mask)
            for j in range(3):
                grad_packed[sub, :, j * 256 + p * 128 : j * 256 + p * 128 + 128] = back[j]
    finish(copies)
    total = mt(grad_packed[...].reshape(512, 768), weight[:, :, :, 0:768].reshape(D, 768))
    for g, block in enumerate(regroup(total)):
        grad[g] = block.astype(BF)
    for d, ref in zip(TURNS, (g0, g1, g2, g3)):
        at = turned(side, d, 1)
        ref[:, 0:D] = grad[at]
        ref[:, D : D + 256] = grad_mix[at, :, 256:512]


def space_grad_kernel(side, normed, grad_packed, own_mix, s0, s1, s2, s3, kept, sent, spaces):
    for d, s in zip(TURNS, (s0, s1, s2, s3)):
        spaces[turned(side, d, -1)] = s[...]
    pieces = [tm(normed[...], grad_packed[...].reshape(512, 768)[:, j * 256 : j * 256 + 256]) for j in range(3)]
    put_halves(side, pieces + [tm(spaces[...].reshape(512, D), own_mix[...])], kept, sent)


def final_kernel(side, acts, own, p0, p1, p2, p3, result, par, sums_in, grad_out, par_out, sums, after):
    sums[...] = sums_in[...]
    for d, p in zip(TURNS, (p0, p1, p2, p3)):
        after[:, pl.ds(pl.multiple_of(turned(side, d, -1) * 256, 256), 256)] = p[:, D : D + 256]
    spans = [(0, 64, acts[0])] + [(64 + 16 * c, 80 + 16 * c, acts[1 + c]) for c in range(4)]
    for low, high, action in spans:
        rows = slice(low, high)
        entered = own[rows, 0:D].astype(F32) + par[pl.ds(action, 1), :]
        scaled, inverse = scaled_of(entered)
        grad = total_of([p.at[rows, 0:D] for p in (p0, p1, p2, p3)])
        sums[8:9, :] += jnp.sum(grad * scaled, axis=0, keepdims=True)
        sums[11:12, :] += jnp.sum(grad, axis=0, keepdims=True)
        total = after[rows, :].astype(F32) + norm_back(grad, scaled, inverse, par[8:9, :])
        grad_out[rows, 0:D] = total.astype(BF)
        sums[pl.ds(action, 1), :] += jnp.sum(total, axis=0, keepdims=True)
    grad_out[:, D : 2 * D] = result[...]
    turned_sums = jnp.concatenate([sums[...], jnp.zeros((112, D), F32)], axis=0).T.reshape(16, 2, 32, 128)
    both = jnp.concatenate([turned_sums[:, 0, :, 0:16], turned_sums[:, 1, :, 0:16], turned_sums[:, 0, :, 32:128]], axis=2)
    par_out[...] = both.astype(BF)


def place_kernel(side, b0, b1, b2, b3, grad_wide, grad_small, wide, small, grad, result):
    for d, b in zip(TURNS, (b0, b1, b2, b3)):
        at = turned(side, d, -1)
        for start, dest in ((0, grad), (D, result)):
            block = b[:, start : start + D].astype(F32)
            for f in range(16):
                dest[f, at] = block[8 * f : 8 * f + 8]
    grad_wide[...] = grad[0:8].reshape(256, D)
    grad_small[...] = grad[8:16].reshape(256, D)
    wide[...] = result[0:8].reshape(256, D).astype(BF)
    small[...] = result[8:16].reshape(256, D).astype(BF)


def swap(x, axes):
    return lax.all_to_all(x, axes, split_axis=0, concat_axis=0, tiled=True)


def spread(x, axes, n):
    return swap(jnp.broadcast_to(x[None], (n,) + x.shape), axes)


def shift(x, d):
    return lax.ppermute(x, "head", [(i, (i + d) % 4) for i in range(4)])


def core_swap(x):
    return lax.ppermute(x, "core", [(0, 1), (1, 0)])


def after(x, *others):
    return lax.optimization_barrier((x,) + others)[0]


def around(x):
    return [x] + [shift(x, d) for d in TURNS[1:]]


def body(
    frames_wide, frames_small, actions_wide, actions_small, cotangent_wide, cotangent_small,
    action_table, norm_gains, norm_shifts, space_project, space_output, time_project, time_output,
    expand_weight, shrink_weight,
):
    me = lax.axis_index("head")
    core = lax.axis_index("core")
    side = jnp.stack([core, me]).astype(jnp.int32)
    wide, small = frames_wide.reshape(256, D), frames_small.reshape(256, D)
    acts = jnp.concatenate([actions_wide.reshape(1), actions_small.reshape(4), jnp.zeros((3,), jnp.int32)])

    outputs = jnp.concatenate([space_output, time_output], axis=1)
    outputs, *big = lax.optimization_barrier((outputs, time_project, expand_weight, shrink_weight))
    big = [big[0].reshape(32, 768)] + big[1:] + around(outputs)
    big = lax.all_gather(jnp.concatenate(big, axis=1), CF, axis=0, tiled=True)

    def own_rows(x):
        return lax.dynamic_index_in_dim(x.reshape(8, 4, 8, D), me, 1, keepdims=False)

    marks = jnp.concatenate([jnp.broadcast_to(acts[0:1], (8,)), jnp.repeat(acts[1:5], 2)]).astype(BF)
    marks = jnp.broadcast_to(marks[:, None, None], (16, 8, 128))
    own = jnp.concatenate([own_rows(wide), own_rows(small)])
    own_cot = jnp.concatenate([own_rows(cotangent_wide), own_rows(cotangent_small)])
    own = lax.optimization_barrier(jnp.concatenate([own, marks, own_cot], axis=2))

    small_par = jnp.concatenate([action_table, norm_gains, norm_shifts, jnp.zeros((2, 32), BF)], axis=0).T
    first = jnp.concatenate([space_project.reshape(32, 768), jnp.pad(small_par, ((0, 0), (0, 112)))], axis=1)
    mine = spread(first, CHIPS, 16)
    other = core_swap(mine)
    stream = swap(after(own, mine), FRAME).reshape(128, 2176)
    streams = around(stream[:, 0:1152])
    cots = around(after(stream[:, 1152:2176], *streams))

    def chips(size):
        return pltpu.VMEM((16, 2, 32, size), BF)

    def sems(count):
        return pltpu.SemaphoreType.DMA((count,))

    one, four, all_rows = ((128, D), BF), ((4, 128, D), BF), ((512, D), BF)
    mix_f, packed_f, par, normed_s = call(
        space_kernel, [((512, 256), BF), ((2, 256, 768), BF), ((16, D), F32), all_rows], [SM] * 2 + [VM] * 2 + [HB] * 2,
        (side, acts, wide, small, mine, other), [chips(896), sems(2)],
        flops=2 * 10**9, size=5 * 10**6,
    )
    mix = jnp.broadcast_to(mix_f.reshape(1, 16, 32, 256), (4, 16, 32, 256)).reshape(64, 32, 256)
    mix = swap(after(mix, stream), HF).reshape(4, 512, 256)

    turns = pltpu.VMEM((4, D, 256), BF)
    after_space, own_space, normed_t, packed_t, mixture, own_mix = call(
        time_kernel,
        [((4, 128, D), F32), ((128, D), F32), all_rows, ((512, 768), BF), ((512, 256), BF), ((512, 256), BF)],
        [SM] + [VM] * 6 + [HB], (side, *streams, mix, par, big),
        [turns, pltpu.VMEM((D, 768), BF), sems(5)], flops=3 * 10**9, size=9 * 10**6,
    )
    square = pltpu.VMEM((D, D), BF)
    own_time, normed_ffn, cot, hidden, grad_raised, *parts = call(
        ffn_kernel, [((128, D), F32), all_rows, four, all_rows, all_rows] + [one] * 4, [SM] + [VM] * 10 + [HB],
        (side, *around(after(mixture, *cots)), *cots, after_space, par, big),
        [pltpu.VMEM((4, 128, D), F32), pltpu.VMEM((4, 128, D), BF), turns, square, square, sems(6)],
        flops=5 * 10**9, size=14 * 10**6,
    )

    def send(blocks):
        return [blocks[0]] + [shift(block, d) for block, d in zip(blocks[1:], TURNS[1:])]

    parts = send(parts)
    (ffn_grad,) = call(
        ffn_grad_kernel, [((8, 4, 32, 3 * D), BF)], [VM] * 4, (normed_ffn, cot, hidden, grad_raised),
        flops=2 * 10**9, size=8 * 10**6,
    )
    grad_time, branch, sums = call(
        after_time_kernel, [((128, D), F32), one, ((16, D), F32)], [VM] * 7,
        (*parts, own_time, cots[0], after(par, ffn_grad)), flops=10**8, size=4 * 10**6,
    )
    branch_list = around(branch)
    outs = call(
        ffn_out_kernel, [one] * 4, [SM, VM, HB], (side, after(hidden, grad_time), big),
        [pltpu.VMEM((4, 128, D), BF), square, sems(1)], flops=10**9, size=4 * 10**6,
    )
    branches, grad_packed_t, *parts = call(
        time_back_kernel, [four, ((4, 128, 768), BF)] + [one] * 4, [SM] + [VM] * 5 + [HB],
        (side, *branch_list, after(packed_t, outs[0]).reshape(4, 128, 768), big),
        [pltpu.VMEM((4, 128, D), BF), pltpu.VMEM((D, 256), BF), pltpu.VMEM((D, 768), BF), sems(2)], flops=2 * 10**9, size=8 * 10**6,
    )
    grads = pl.pallas_call(
        time_grad_kernel,
        out_shape=jax.ShapeDtypeStruct((8, 4, 32, 3 * D), BF),
        in_specs=[VM] * 4 + [HB],
        out_specs=HB,
        scratch_shapes=[pltpu.VMEM((8, 4, 32, D), BF), sems(1)],
        input_output_aliases={4: 0},
        compiler_params=pltpu.CompilerParams(vmem_limit_bytes=50 * 2**20),
        cost_estimate=pl.CostEstimate(flops=2 * 10**9, bytes_accessed=8 * 10**6, transcendentals=0),
    )(normed_t, grad_packed_t.reshape(512, 768), branches.reshape(512, D), mixture, ffn_grad)
    parts = send(parts)
    early = parts[1:]
    grad_mix, grad_space, sums = call(
        after_space_kernel, [((4, 128, 512), BF), one, ((16, D), F32)], [SM] + [VM] * 8 + [HB],
        (side, *parts, own_space, grad_time, after(par, grads), sums, big),
        [turns, sems(4)],
        flops=3 * 10**8, size=5 * 10**6,
    )
    grad_mix = swap(grad_mix.reshape(64, 8, 512), HF).reshape(4, 128, 512)
    spaces = around(grad_space)
    outs = send([outs[0]] + [after(block, grad_space) for block in outs[1:]])
    result = (total_of(outs) + own_time).astype(BF)
    packed_f = after(packed_f, result)
    result = swap(after(result, grad_mix).reshape(16, 8, D), FRAME).reshape(128, D)
    def pair_sum(kept, sent):
        return (kept.astype(F32) + core_swap(sent).astype(F32)).astype(BF)

    def chip_sum(x):
        return jnp.sum(swap(x, CHIPS).astype(F32), axis=0)

    grad_packed_f, *parts = call(
        space_back_kernel, [((2, 256, 768), BF)] + [((128, 1280), BF)] * 4, [SM, VM] + [HB] * 3,
        (side, grad_mix, packed_f, mine, other),
        [pltpu.VMEM((512, 256), BF), pltpu.VMEM((4, 128, D), BF), chips(896), pltpu.VMEM((2, 256, 768), BF), sems(3)], flops=2 * 10**9, size=4 * 10**6,
    )
    parts = send(parts)
    space_kept, space_sent = call(
        space_grad_kernel, [((16, 32, D), BF)] * 2, [SM] + [VM] * 7, (side, normed_s, grad_packed_f, after(own_mix, result), *spaces),
        [pltpu.VMEM((4, 128, D), BF)], flops=10**9, size=4 * 10**6,
    )
    chunk = ((16, 32, 128), BF)
    grad_own, par_part = call(
        final_kernel, [((128, 2 * D), BF), chunk], [SM] * 2 + [VM] * 8,
        (side, acts, own.reshape(128, 2176), *parts, result, after(par, space_kept), sums),
        [pltpu.VMEM((16, D), F32), pltpu.VMEM((128, D), BF)],
        flops=10**8, size=2 * 10**6,
    )
    shape = (256, D)
    placed = call(
        place_kernel, [(shape, F32), (shape, F32), (shape, BF), (shape, BF)], [SM] + [VM] * 4,
        (side, *around(grad_own)), [pltpu.VMEM((16, 4, 8, D), F32)] * 2, flops=10**6, size=6 * 10**6,
    )

    total = jnp.concatenate([pair_sum(space_kept, after(space_sent, *parts)), par_part], axis=2)
    total = chip_sum(total)
    grads = lax.psum_scatter(after(grads, *early), ("z", "core"), scatter_dimension=0, tiled=True).reshape(4, 32, 3 * D)
    grads = lax.psum_scatter(after(grads, space_kept), ("clip", "yh"), scatter_dimension=0, tiled=True)
    grads = grads.reshape(32, 3 * D).astype(F32)
    par_total = total[:, D : D + 128]
    par_total = (par_total + core_swap(par_total.astype(BF)).astype(F32)).astype(BF)
    par_total = total_of(around(par_total))
    par_total = jnp.where(core == 0, par_total[:, 0:16], par_total[:, 16:32]).T

    return (
        placed[2].reshape(1, 1, 256, D),
        placed[3].reshape(4, 1, 64, D),
        placed[0].reshape(1, 1, 256, D),
        placed[1].reshape(4, 1, 64, D),
        par_total[0:8],
        par_total[8:11],
        par_total[11:14],
        total[:, 0:768].reshape(32, 3, 256),
        total[:, 768:1024],
        grads[:, 2 * D : 2 * D + 768].reshape(32, 3, 256),
        grads[:, 2 * D + 768 : 3 * D],
        grads[:, 0:D],
        grads[:, D : 2 * D],
    )


def solution(mesh):
    fine = Mesh(mesh.devices.reshape(2, 4, 2, 2, 4), ALL)
    tokens = P("clip", FRAME, None, None)
    columns = P(None, CF)
    square, cube = P(CF, "head"), P(CF, None, "head")
    frames = P("clip", FRAME)
    weights = (cube, square, cube, square, square, square)
    in_specs = (tokens, tokens, frames, frames, tokens, tokens) + (columns,) * 3 + weights
    out_specs = (tokens,) * 4 + (columns,) * 3 + weights
    return jax.shard_map(body, mesh=fine, in_specs=in_specs, out_specs=out_specs, check_vma=False)
```

```python
import functools
import math

import jax
import jax.numpy as jnp
from jax import lax
from jax.experimental import pallas as pl
from jax.experimental.pallas import tpu as pltpu
from jax.sharding import Mesh
from jax.sharding import PartitionSpec as P

BF = jnp.bfloat16
F32 = jnp.float32
EPS = 1e-05
CF = ("clip", "z", "yh", "core")
FRAME = ("z", "yh", "core")
CHIPS = ("clip", "z", "yh")
HF = ("head", "z", "yh", "core")
ALL = ("clip", "z", "yh", "core", "head")
D = 1024
VM = pl.BlockSpec(memory_space=pltpu.VMEM)
SM = pl.BlockSpec(memory_space=pltpu.SMEM)
HB = pl.BlockSpec(memory_space=pltpu.MemorySpace.HBM)
SCALE = 0.125


def mm(a, b):
    return lax.dot_general(a, b, (((1,), (0,)), ((), ())), preferred_element_type=F32)


def mt(a, b):
    return lax.dot_general(a, b, (((1,), (1,)), ((), ())), preferred_element_type=F32)


def tm(a, b):
    return lax.dot_general(a, b, (((0,), (0,)), ((), ())), preferred_element_type=F32)


def call(body, outs, specs, args, scratch=(), flops=0, size=0):
    return pl.pallas_call(
        body,
        out_shape=[jax.ShapeDtypeStruct(s, t) for s, t in outs],
        in_specs=specs,
        out_specs=[VM] * len(outs),
        scratch_shapes=list(scratch),
        compiler_params=pltpu.CompilerParams(vmem_limit_bytes=50 * 2**20),
        cost_estimate=pl.CostEstimate(flops=flops, bytes_accessed=size, transcendentals=0),
    )(*args)


def scaled_of(stream):
    average = jnp.mean(stream, axis=-1, keepdims=True)
    centered = stream - average
    inverse = lax.rsqrt(jnp.mean(centered * centered, axis=-1, keepdims=True) + EPS)
    return centered * inverse, inverse


def norm_back(grad, scaled, inverse, gain):
    grad_scaled = grad * gain
    inner = jnp.mean(grad_scaled, axis=-1, keepdims=True)
    along = jnp.mean(grad_scaled * scaled, axis=-1, keepdims=True)
    return inverse * (grad_scaled - inner - scaled * along)


def lane_half(side):
    lane = lax.broadcasted_iota(jnp.int32, (1, 128), 1)
    return (lane < 64) if side == 0 else (lane >= 64)


def both_heads(block):
    zero = jnp.zeros_like(block)
    return jnp.concatenate([jnp.where(lane_half(0), block, zero), jnp.where(lane_half(1), block, zero)], axis=0)


def own_lanes(double):
    rows = double.shape[0] // 2
    return jnp.where(lane_half(0), double[:rows], double[rows:])


def chances_of(q_both, keys, mask):
    scores = mt(keys, q_both) * SCALE
    if mask is not None:
        scores = jnp.where(mask, scores, -1e30)
    raised = jnp.exp(scores - jnp.max(scores, axis=0, keepdims=True))
    return raised * (1.0 / jnp.sum(raised, axis=0, keepdims=True))


def attend(q2, k2, v2, mask):
    chances = chances_of(both_heads(q2), k2, mask).astype(BF)
    return own_lanes(tm(chances, v2)).astype(BF)


def attend_back(q2, k2, v2, g2, mask):
    q_both, g_both = both_heads(q2), both_heads(g2)
    chances = chances_of(q_both, k2, mask)
    grad_v = mm(chances.astype(BF), g_both)
    grad_chances = mt(v2, g_both)
    weighted = jnp.sum(grad_chances * chances, axis=0, keepdims=True)
    grad_scores = (chances * (grad_chances - weighted)).astype(BF)
    grad_q = own_lanes(tm(grad_scores, k2))
    grad_k = mm(grad_scores, q_both)
    return (grad_q * SCALE).astype(BF), (grad_k * SCALE).astype(BF), grad_v.astype(BF)


def small_mask():
    key = lax.broadcasted_iota(jnp.int32, (256, 512), 0)
    query = lax.broadcasted_iota(jnp.int32, (256, 512), 1) % 256
    return (key // 64) == (query // 64)


def time_mask():
    key = lax.broadcasted_iota(jnp.int32, (128, 256), 0)
    query = lax.broadcasted_iota(jnp.int32, (128, 256), 1) % 128
    return (key <= query) & ((key % 8) == (query % 8))


TURNS = (0, 2, 3, 1)


def load_chips(side, mine, other, dest, sems):
    core = side[0]
    copies = [
        pltpu.make_async_copy(mine, dest.at[:, core], sems.at[0]),
        pltpu.make_async_copy(other, dest.at[:, 1 - core], sems.at[1]),
    ]
    for copy in copies:
        copy.start()
    return copies


def load_turns(big, offset, dest, sems):
    copies = []
    for d in range(4):
        start = 2816 + 512 * d + offset
        copies.append(pltpu.make_async_copy(big.at[:, start : start + 256], dest.at[d], sems.at[d]))
        copies[d].start()
    return copies


def finish(copies):
    for copy in copies:
        copy.wait()


def turned(side, d, sign):
    return lax.rem(side[1] + 4 + sign * d, 4)


def regroup(block):
    width = block.shape[1]
    parts = block.reshape(16, 4, 8, width)
    return [parts[:, g].reshape(128, width) for g in range(4)]


def ungroup(blocks):
    width = blocks[0].shape[1]
    return jnp.stack([block.reshape(16, 8, width) for block in blocks], axis=1).reshape(512, width)


def space_norm(acts, wide, small, par, normed):
    for sub, ref in enumerate((wide, small)):
        for b in range(4):
            action = acts[0] if sub == 0 else acts[1 + b]
            entered = ref[64 * b : 64 * b + 64, :].astype(F32) + par[pl.ds(action, 1), :]
            scaled, _ = scaled_of(entered)
            start = sub * 256 + b * 64
            normed[start : start + 64, :] = (scaled * par[8:9, :] + par[11:12, :]).astype(BF)


def space_kernel(side, acts, wide, small, mine, other, mix, packed, par, normed, weight, sems):
    finish(load_chips(side, mine, other, weight, sems))
    par[...] = weight[:, :, :, 768:896].reshape(D, 128).astype(F32).T[0:16, :]
    space_norm(acts, wide, small, par, normed)
    for sub in range(2):
        rows = normed[sub * 256 : sub * 256 + 256, :]
        for j in range(3):
            columns = weight[:, :, :, j * 256 : j * 256 + 256].reshape(D, 256)
            packed[sub, :, j * 256 : j * 256 + 256] = mm(rows, columns).astype(BF)
        mask = None if sub == 0 else small_mask()
        for p in range(2):
            q2, k2, v2 = (packed[sub, :, j * 256 + p * 128 : j * 256 + p * 128 + 128] for j in range(3))
            mix[sub * 256 : sub * 256 + 256, p * 128 : p * 128 + 128] = attend(q2, k2, v2, mask)


def time_kernel(
    side, s0, s1, s2, s3, mix, par, big,
    after_space, own_after, normed, packed, mixture, own_mix, wso, wtp, sems,
):
    copies = load_turns(big, 0, wso, sems)
    copy = pltpu.make_async_copy(big.at[:, 0:768], wtp, sems.at[4])
    copy.start()
    lane = lax.broadcasted_iota(jnp.int32, (1, 16), 1).astype(F32)
    for d, s in zip(TURNS, (s0, s1, s2, s3)):
        chosen = (s[:, D : D + 1].astype(F32) == lane).astype(BF)
        after_space[turned(side, d, -1)] = s[:, 0:D].astype(F32) + mm(chosen, par[...].astype(BF))
    stepped = 0.0
    for i, d in enumerate(TURNS):
        copies[i].wait()
        stepped = stepped + mt(mix[turned(side, d, -1)], wso[i])
    for g, block in enumerate(regroup(stepped)):
        block = after_space[g] + block
        after_space[g] = block
        scaled, _ = scaled_of(block)
        normed[128 * g : 128 * g + 128, :] = (scaled * par[9:10, :] + par[12:13, :]).astype(BF)
    for g, block in enumerate(regroup(mix[side[1]].astype(F32))):
        own_mix[128 * g : 128 * g + 128, :] = block.astype(BF)
    own_after[...] = after_space[side[1]]
    copy.wait()
    for j in range(3):
        packed[:, j * 256 : j * 256 + 256] = mm(normed[...], wtp[:, j * 256 : j * 256 + 256]).astype(BF)
    mask = time_mask()
    for g in range(4):
        rows = slice(128 * g, 128 * g + 128)
        for p in range(2):
            q2, k2, v2 = (packed[rows, j * 256 + p * 128 : j * 256 + p * 128 + 128] for j in range(3))
            mixture[rows, p * 128 : p * 128 + 128] = attend(q2, k2, v2, mask)


UP = slice(768, 1792)
DOWN = slice(1792, 2816)


def ffn_kernel(
    side, m0, m1, m2, m3, c0, c1, c2, c3, after_space, par, big,
    own_after, normed, cot, hidden, grad_raised, g0, g1, g2, g3, done, grad, wto, we, ws, sems,
):
    copies = load_turns(big, 256, wto, sems)
    more = [
        pltpu.make_async_copy(big.at[:, UP], we, sems.at[4]),
        pltpu.make_async_copy(big.at[:, DOWN], ws, sems.at[5]),
    ]
    for copy in more:
        copy.start()
    for d, c in zip(TURNS, (c0, c1, c2, c3)):
        cot[turned(side, d, -1)] = c[...]
    total = after_space[...].reshape(512, D)
    for i, m in enumerate((m0, m1, m2, m3)):
        copies[i].wait()
        total = total + mt(m[...], wto[i])
    scaled, _ = scaled_of(total)
    done[...] = total.reshape(4, 128, D)
    normed[...] = (scaled * par[10:11, :] + par[13:14, :]).astype(BF)
    own_after[...] = done[side[1]]
    for copy in more:
        copy.wait()
    for c in range(4):
        cols = slice(c * 256, c * 256 + 256)
        raised = mm(normed[...], we[:, cols])
        grad_hidden = mm(cot[...].reshape(512, D), ws[:, cols])
        spread = 0.5 * (1.0 + lax.erf(raised * math.sqrt(0.5)))
        bell = jnp.exp(-0.5 * raised * raised) * (1.0 / math.sqrt(2.0 * math.pi))
        hidden[:, cols] = (raised * spread).astype(BF)
        grad_raised[:, cols] = (grad_hidden * (spread + raised * bell)).astype(BF)
    grad[...] = mt(grad_raised[...], we[...]).astype(BF).reshape(4, 128, D)
    for d, g in zip(TURNS, (g0, g1, g2, g3)):
        g[...] = grad[turned(side, d, 1)]


def ffn_out_kernel(side, hidden, big, o0, o1, o2, o3, out, ws, sems):
    copy = pltpu.make_async_copy(big.at[:, DOWN], ws, sems.at[0])
    copy.start()
    copy.wait()
    out[...] = mt(hidden[...], ws[...]).astype(BF).reshape(4, 128, D)
    for d, o in zip(TURNS, (o0, o1, o2, o3)):
        o[...] = out[turned(side, d, 1)]


def halves(side, block):
    first, second = block[:, 0], block[:, 1]
    low = side[0] == 0
    return jnp.where(low, first, second), jnp.where(low, second, first)


def put_frames(piece, out, start):
    block = piece.astype(BF).reshape(16, 2, 32, piece.shape[1])
    for chip in range(16):
        clip, z, yh = chip // 8, (chip // 2) % 4, chip % 2
        for s in range(2):
            out[z * 2 + s, clip * 2 + yh, :, start : start + piece.shape[1]] = block[chip, s]


def ffn_grad_kernel(normed, cot, hidden, grad_raised, out):
    for c in range(4):
        cols = slice(c * 256, c * 256 + 256)
        put_frames(tm(normed[...], grad_raised[:, cols]), out, c * 256)
        put_frames(tm(cot[...].reshape(512, D), hidden[:, cols]), out, D + c * 256)


def total_of(parts):
    return (parts[0][...].astype(F32) + parts[1][...].astype(F32)) + (parts[2][...].astype(F32) + parts[3][...].astype(F32))


def after_time_kernel(p0, p1, p2, p3, own_after, cot, par, grad_after, branch, sums):
    grad = total_of((p0, p1, p2, p3))
    scaled, inverse = scaled_of(own_after[...])
    sums[...] = jnp.zeros_like(sums)
    sums[10:11, :] = jnp.sum(grad * scaled, axis=0, keepdims=True)
    sums[13:14, :] = jnp.sum(grad, axis=0, keepdims=True)
    total = cot[...].astype(F32) + norm_back(grad, scaled, inverse, par[10:11, :])
    grad_after[...] = total
    branch[...] = total.astype(BF)


def time_back_kernel(
    side, b0, b1, b2, b3, packed, big,
    branches, grad_packed, p0, p1, p2, p3, grad, wto, wtp, sems,
):
    copy_out = pltpu.make_async_copy(big.at[:, 2816 + 256 : 2816 + 512], wto, sems.at[0])
    copy_out.start()
    copy = pltpu.make_async_copy(big.at[:, 0:768], wtp, sems.at[1])
    copy.start()
    copy_out.wait()
    mask = time_mask()
    for d, b in zip(TURNS, (b0, b1, b2, b3)):
        at = turned(side, d, -1)
        branches[at] = b[...]
        grad_mixture = mm(b[...], wto[...]).astype(BF)
        for p in range(2):
            q2, k2, v2 = (packed[at, :, j * 256 + p * 128 : j * 256 + p * 128 + 128] for j in range(3))
            back = attend_back(q2, k2, v2, grad_mixture[:, p * 128 : p * 128 + 128], mask)
            for j in range(3):
                grad_packed[at, :, j * 256 + p * 128 : j * 256 + p * 128 + 128] = back[j]
    copy.wait()
    grad[...] = mt(grad_packed[...].reshape(512, 768), wtp[...]).astype(BF).reshape(4, 128, D)
    for d, p in zip(TURNS, (p0, p1, p2, p3)):
        p[...] = grad[turned(side, d, 1)]


def after_space_kernel(
    side, p0, p1, p2, p3, own_after, grad_time, par, sums_in, big, grad_mix, grad_after, sums, wso, sems,
):
    copies = load_turns(big, 0, wso, sems)
    grad = total_of((p0, p1, p2, p3))
    scaled, inverse = scaled_of(own_after[...])
    sums[...] = sums_in[...]
    sums[9:10, :] = jnp.sum(grad * scaled, axis=0, keepdims=True)
    sums[12:13, :] = jnp.sum(grad, axis=0, keepdims=True)
    branch = (grad_time[...] + norm_back(grad, scaled, inverse, par[9:10, :])).astype(BF)
    grad_after[...] = branch
    for h in range(4):
        grad_mix[h, :, 256:512] = branch[:, h * 256 : h * 256 + 256]
    for i, d in enumerate(TURNS):
        copies[i].wait()
        grad_mix[turned(side, d, -1), :, 0:256] = mm(branch, wso[i]).astype(BF)


def put_halves(side, pieces, kept, sent):
    for i, piece in enumerate(pieces):
        here, there = halves(side, piece.astype(BF).reshape(16, 2, 32, 256))
        kept[:, :, i * 256 : i * 256 + 256] = here
        sent[:, :, i * 256 : i * 256 + 256] = there


def time_grad_kernel(normed, grad_packed, branches, mixture, grads_in, grads, part, sems):
    for j in range(3):
        put_frames(tm(normed[...], grad_packed[:, j * 256 : j * 256 + 256]), part, j * 256)
    put_frames(tm(branches[...], mixture[...]), part, 768)
    copy = pltpu.make_async_copy(part, grads.at[:, :, :, 2 * D : 3 * D], sems.at[0])
    copy.start()
    copy.wait()


def space_back_kernel(
    side, grad_mix, packed_in, mine, other, grad_packed, g0, g1, g2, g3, natural, grad, weight, packed, sems
):
    copy = pltpu.make_async_copy(packed_in, packed, sems.at[2])
    copy.start()
    copies = load_chips(side, mine, other, weight, sems)
    natural[...] = ungroup([grad_mix[g, :, 0:256].astype(F32) for g in range(4)]).astype(BF)
    copy.wait()
    for sub in range(2):
        mask = None if sub == 0 else small_mask()
        for p in range(2):
            q2, k2, v2 = (packed[sub, :, j * 256 + p * 128 : j * 256 + p * 128 + 128] for j in range(3))
            back = attend_back(q2, k2, v2, natural[sub * 256 : sub * 256 + 256, p * 128 : p * 128 + 128], mask)
            for j in range(3):
                grad_packed[sub, :, j * 256 + p * 128 : j * 256 + p * 128 + 128] = back[j]
    finish(copies)
    total = mt(grad_packed[...].reshape(512, 768), weight[:, :, :, 0:768].reshape(D, 768))
    for g, block in enumerate(regroup(total)):
        grad[g] = block.astype(BF)
    for d, ref in zip(TURNS, (g0, g1, g2, g3)):
        at = turned(side, d, 1)
        ref[:, 0:D] = grad[at]
        ref[:, D : D + 256] = grad_mix[at, :, 256:512]


def space_grad_kernel(side, normed, grad_packed, own_mix, s0, s1, s2, s3, kept, sent, spaces):
    for d, s in zip(TURNS, (s0, s1, s2, s3)):
        spaces[turned(side, d, -1)] = s[...]
    pieces = [tm(normed[...], grad_packed[...].reshape(512, 768)[:, j * 256 : j * 256 + 256]) for j in range(3)]
    put_halves(side, pieces + [tm(spaces[...].reshape(512, D), own_mix[...])], kept, sent)


def final_kernel(side, acts, own, p0, p1, p2, p3, result, par, sums_in, grad_out, par_out, sums, after):
    sums[...] = sums_in[...]
    for d, p in zip(TURNS, (p0, p1, p2, p3)):
        after[:, pl.ds(pl.multiple_of(turned(side, d, -1) * 256, 256), 256)] = p[:, D : D + 256]
    spans = [(0, 64, acts[0])] + [(64 + 16 * c, 80 + 16 * c, acts[1 + c]) for c in range(4)]
    for low, high, action in spans:
        rows = slice(low, high)
        entered = own[rows, 0:D].astype(F32) + par[pl.ds(action, 1), :]
        scaled, inverse = scaled_of(entered)
        grad = total_of([p.at[rows, 0:D] for p in (p0, p1, p2, p3)])
        sums[8:9, :] += jnp.sum(grad * scaled, axis=0, keepdims=True)
        sums[11:12, :] += jnp.sum(grad, axis=0, keepdims=True)
        total = after[rows, :].astype(F32) + norm_back(grad, scaled, inverse, par[8:9, :])
        grad_out[rows, 0:D] = total.astype(BF)
        sums[pl.ds(action, 1), :] += jnp.sum(total, axis=0, keepdims=True)
    grad_out[:, D : 2 * D] = result[...]
    turned_sums = jnp.concatenate([sums[...], jnp.zeros((112, D), F32)], axis=0).T.reshape(16, 2, 32, 128)
    both = jnp.concatenate([turned_sums[:, 0, :, 0:16], turned_sums[:, 1, :, 0:16], turned_sums[:, 0, :, 32:128]], axis=2)
    par_out[...] = both.astype(BF)


def place_kernel(side, b0, b1, b2, b3, grad_wide, grad_small, wide, small, grad, result):
    for d, b in zip(TURNS, (b0, b1, b2, b3)):
        at = turned(side, d, -1)
        for start, dest in ((0, grad), (D, result)):
            block = b[:, start : start + D].astype(F32)
            for f in range(16):
                dest[f, at] = block[8 * f : 8 * f + 8]
    grad_wide[...] = grad[0:8].reshape(256, D)
    grad_small[...] = grad[8:16].reshape(256, D)
    wide[...] = result[0:8].reshape(256, D).astype(BF)
    small[...] = result[8:16].reshape(256, D).astype(BF)


def swap(x, axes):
    return lax.all_to_all(x, axes, split_axis=0, concat_axis=0, tiled=True)


def spread(x, axes, n):
    return swap(jnp.broadcast_to(x[None], (n,) + x.shape), axes)


def shift(x, d):
    return lax.ppermute(x, "head", [(i, (i + d) % 4) for i in range(4)])


def core_swap(x):
    return lax.ppermute(x, "core", [(0, 1), (1, 0)])


def after(x, *others):
    return lax.optimization_barrier((x,) + others)[0]


def around(x):
    return [x] + [shift(x, d) for d in TURNS[1:]]


def body(
    frames_wide, frames_small, actions_wide, actions_small, cotangent_wide, cotangent_small,
    action_table, norm_gains, norm_shifts, space_project, space_output, time_project, time_output,
    expand_weight, shrink_weight,
):
    me = lax.axis_index("head")
    core = lax.axis_index("core")
    side = jnp.stack([core, me]).astype(jnp.int32)
    wide, small = frames_wide.reshape(256, D), frames_small.reshape(256, D)
    acts = jnp.concatenate([actions_wide.reshape(1), actions_small.reshape(4), jnp.zeros((3,), jnp.int32)])

    outputs = jnp.concatenate([space_output, time_output], axis=1)
    outputs, *big = lax.optimization_barrier((outputs, time_project, expand_weight, shrink_weight))
    big = [big[0].reshape(32, 768)] + big[1:] + around(outputs)
    big = lax.all_gather(jnp.concatenate(big, axis=1), CF, axis=0, tiled=True)

    def own_rows(x):
        return lax.dynamic_index_in_dim(x.reshape(8, 4, 8, D), me, 1, keepdims=False)

    marks = jnp.concatenate([jnp.broadcast_to(acts[0:1], (8,)), jnp.repeat(acts[1:5], 2)]).astype(BF)
    marks = jnp.broadcast_to(marks[:, None, None], (16, 8, 128))
    own = jnp.concatenate([own_rows(wide), own_rows(small)])
    own_cot = jnp.concatenate([own_rows(cotangent_wide), own_rows(cotangent_small)])
    own = lax.optimization_barrier(jnp.concatenate([own, marks, own_cot], axis=2))

    small_par = jnp.concatenate([action_table, norm_gains, norm_shifts, jnp.zeros((2, 32), BF)], axis=0)
    small_par = lax.optimization_barrier(small_par).T
    first = jnp.concatenate([space_project.reshape(32, 768), jnp.pad(small_par, ((0, 0), (0, 112)))], axis=1)
    mine = spread(first, CHIPS, 16)
    other = core_swap(mine)
    stream = swap(after(own, mine), FRAME).reshape(128, 2176)
    streams = around(stream[:, 0:1152])
    cots = around(after(stream[:, 1152:2176], *streams))

    def chips(size):
        return pltpu.VMEM((16, 2, 32, size), BF)

    def sems(count):
        return pltpu.SemaphoreType.DMA((count,))

    one, four, all_rows = ((128, D), BF), ((4, 128, D), BF), ((512, D), BF)
    mix_f, packed_f, par, normed_s = call(
        space_kernel, [((512, 256), BF), ((2, 256, 768), BF), ((16, D), F32), all_rows], [SM] * 2 + [VM] * 2 + [HB] * 2,
        (side, acts, wide, small, mine, other), [chips(896), sems(2)],
        flops=2 * 10**9, size=5 * 10**6,
    )
    mix = jnp.broadcast_to(mix_f.reshape(1, 16, 32, 256), (4, 16, 32, 256)).reshape(64, 32, 256)
    mix = swap(after(mix, stream), HF).reshape(4, 512, 256)

    turns = pltpu.VMEM((4, D, 256), BF)
    after_space, own_space, normed_t, packed_t, mixture, own_mix = call(
        time_kernel,
        [((4, 128, D), F32), ((128, D), F32), all_rows, ((512, 768), BF), ((512, 256), BF), ((512, 256), BF)],
        [SM] + [VM] * 6 + [HB], (side, *streams, mix, par, big),
        [turns, pltpu.VMEM((D, 768), BF), sems(5)], flops=3 * 10**9, size=9 * 10**6,
    )
    square = pltpu.VMEM((D, D), BF)
    own_time, normed_ffn, cot, hidden, grad_raised, *parts = call(
        ffn_kernel, [((128, D), F32), all_rows, four, all_rows, all_rows] + [one] * 4, [SM] + [VM] * 10 + [HB],
        (side, *around(after(mixture, *cots)), *cots, after_space, par, big),
        [pltpu.VMEM((4, 128, D), F32), pltpu.VMEM((4, 128, D), BF), turns, square, square, sems(6)],
        flops=5 * 10**9, size=14 * 10**6,
    )

    def send(blocks):
        return [blocks[0]] + [shift(block, d) for block, d in zip(blocks[1:], TURNS[1:])]

    parts = send(parts)
    (ffn_grad,) = call(
        ffn_grad_kernel, [((8, 4, 32, 3 * D), BF)], [VM] * 4, (normed_ffn, cot, hidden, grad_raised),
        flops=2 * 10**9, size=8 * 10**6,
    )
    grad_time, branch, sums = call(
        after_time_kernel, [((128, D), F32), one, ((16, D), F32)], [VM] * 7,
        (*parts, own_time, cots[0], after(par, ffn_grad)), flops=10**8, size=4 * 10**6,
    )
    branch_list = around(branch)
    outs = call(
        ffn_out_kernel, [one] * 4, [SM, VM, HB], (side, after(hidden, grad_time), big),
        [pltpu.VMEM((4, 128, D), BF), square, sems(1)], flops=10**9, size=4 * 10**6,
    )
    branches, grad_packed_t, *parts = call(
        time_back_kernel, [four, ((4, 128, 768), BF)] + [one] * 4, [SM] + [VM] * 5 + [HB],
        (side, *branch_list, after(packed_t, outs[0]).reshape(4, 128, 768), big),
        [pltpu.VMEM((4, 128, D), BF), pltpu.VMEM((D, 256), BF), pltpu.VMEM((D, 768), BF), sems(2)], flops=2 * 10**9, size=8 * 10**6,
    )
    grads = pl.pallas_call(
        time_grad_kernel,
        out_shape=jax.ShapeDtypeStruct((8, 4, 32, 3 * D), BF),
        in_specs=[VM] * 4 + [HB],
        out_specs=HB,
        scratch_shapes=[pltpu.VMEM((8, 4, 32, D), BF), sems(1)],
        input_output_aliases={4: 0},
        compiler_params=pltpu.CompilerParams(vmem_limit_bytes=50 * 2**20),
        cost_estimate=pl.CostEstimate(flops=2 * 10**9, bytes_accessed=8 * 10**6, transcendentals=0),
    )(normed_t, grad_packed_t.reshape(512, 768), branches.reshape(512, D), mixture, ffn_grad)
    parts = send(parts)
    early = parts[1:]
    grad_mix, grad_space, sums = call(
        after_space_kernel, [((4, 128, 512), BF), one, ((16, D), F32)], [SM] + [VM] * 8 + [HB],
        (side, *parts, own_space, grad_time, after(par, grads), sums, big),
        [turns, sems(4)],
        flops=3 * 10**8, size=5 * 10**6,
    )
    grad_mix = swap(grad_mix.reshape(64, 8, 512), HF).reshape(4, 128, 512)
    spaces = around(grad_space)
    outs = send([outs[0]] + [after(block, grad_space) for block in outs[1:]])
    result = (total_of(outs) + own_time).astype(BF)
    packed_f = after(packed_f, result)
    result = swap(after(result, grad_mix).reshape(16, 8, D), FRAME).reshape(128, D)
    def pair_sum(kept, sent):
        return (kept.astype(F32) + core_swap(sent).astype(F32)).astype(BF)

    def chip_sum(x):
        return jnp.sum(swap(x, CHIPS).astype(F32), axis=0)

    grad_packed_f, *parts = call(
        space_back_kernel, [((2, 256, 768), BF)] + [((128, 1280), BF)] * 4, [SM, VM] + [HB] * 3,
        (side, grad_mix, packed_f, mine, other),
        [pltpu.VMEM((512, 256), BF), pltpu.VMEM((4, 128, D), BF), chips(896), pltpu.VMEM((2, 256, 768), BF), sems(3)], flops=2 * 10**9, size=4 * 10**6,
    )
    parts = send(parts)
    space_kept, space_sent = call(
        space_grad_kernel, [((16, 32, D), BF)] * 2, [SM] + [VM] * 7, (side, normed_s, grad_packed_f, after(own_mix, result), *spaces),
        [pltpu.VMEM((4, 128, D), BF)], flops=10**9, size=4 * 10**6,
    )
    chunk = ((16, 32, 128), BF)
    grad_own, par_part = call(
        final_kernel, [((128, 2 * D), BF), chunk], [SM] * 2 + [VM] * 8,
        (side, acts, own.reshape(128, 2176), *parts, result, after(par, space_kept), sums),
        [pltpu.VMEM((16, D), F32), pltpu.VMEM((128, D), BF)],
        flops=10**8, size=2 * 10**6,
    )
    shape = (256, D)
    placed = call(
        place_kernel, [(shape, F32), (shape, F32), (shape, BF), (shape, BF)], [SM] + [VM] * 4,
        (side, *around(grad_own)), [pltpu.VMEM((16, 4, 8, D), F32)] * 2, flops=10**6, size=6 * 10**6,
    )

    total = jnp.concatenate([pair_sum(space_kept, after(space_sent, *parts)), par_part], axis=2)
    total = chip_sum(total)
    grads = lax.psum_scatter(after(grads, *early), ("z", "core"), scatter_dimension=0, tiled=True).reshape(4, 32, 3 * D)
    grads = lax.psum_scatter(after(grads, space_kept), ("clip", "yh"), scatter_dimension=0, tiled=True)
    grads = grads.reshape(32, 3 * D).astype(F32)
    par_total = total[:, D : D + 128]
    par_total = (par_total + core_swap(par_total.astype(BF)).astype(F32)).astype(BF)
    par_total = total_of(around(par_total))
    par_total = jnp.where(core == 0, par_total[:, 0:16], par_total[:, 16:32]).T

    return (
        placed[2].reshape(1, 1, 256, D),
        placed[3].reshape(4, 1, 64, D),
        placed[0].reshape(1, 1, 256, D),
        placed[1].reshape(4, 1, 64, D),
        par_total[0:8],
        par_total[8:11],
        par_total[11:14],
        total[:, 0:768].reshape(32, 3, 256),
        total[:, 768:1024],
        grads[:, 2 * D : 2 * D + 768].reshape(32, 3, 256),
        grads[:, 2 * D + 768 : 3 * D],
        grads[:, 0:D],
        grads[:, D : 2 * D],
    )


def solution(mesh):
    fine = Mesh(mesh.devices.reshape(2, 4, 2, 2, 4), ALL)
    tokens = P("clip", FRAME, None, None)
    columns = P(None, CF)
    square, cube = P(CF, "head"), P(CF, None, "head")
    frames = P("clip", FRAME)
    weights = (cube, square, cube, square, square, square)
    in_specs = (tokens, tokens, frames, frames, tokens, tokens) + (columns,) * 3 + weights
    out_specs = (tokens,) * 4 + (columns,) * 3 + weights
    return jax.shard_map(body, mesh=fine, in_specs=in_specs, out_specs=out_specs, check_vma=False)
```
